128 devices in a mesh: row: 8 (over y, z_hi), col: 16 (over x, z_lo, core).
Axes of the slice: x: 4, y: 4, z: 4 (z_hi: 2, z_lo: 2; z = z_hi * 2 + z_lo), core: 2. Of those that a mesh axis runs over, the one named last changes fastest.
Arguments:
- x_seq: bfloat16 [4096, 4096], P(('row', 'col')), may hold values from -6 to 6
- dy_seq: bfloat16 [4096, 4096], P(('row', 'col')), may hold values from -3 to 3
- gate_vals: bfloat16 [224, 32, 4096], P('col', 'row'), may hold values from -0.125 to 0.125
- gate_idx: int32 [224, 32], P('col'), may hold values from 0 to 63, as said below
- up_vals: bfloat16 [224, 32, 4096], P('col', 'row'), may hold values from -0.125 to 0.125
- up_idx: int32 [224, 32], P('col'), may hold values from 0 to 63, as said below
- down_vals: bfloat16 [224, 32, 4096], P('col', 'row'), may hold values from -0.0625 to 0.0625
- down_idx: int32 [224, 32], P('col'), may hold values from 0 to 63, as said below
Outputs:
- y_seq: bfloat16 [4096, 4096], P(('row', 'col'))
- dx_seq: bfloat16 [4096, 4096], P(('row', 'col'))
- d_gate_vals: bfloat16 [224, 32, 4096], P('col', 'row')
- d_up_vals: bfloat16 [224, 32, 4096], P('col', 'row')
- d_down_vals: bfloat16 [224, 32, 4096], P('col', 'row')
The draws below stay inside these ranges and needn't reach their ends.
Inputs may be any that keep to these rules, and one draw needn't show every extreme that they name: `gate_idx`: each row lists 32 distinct block numbers. `up_idx`: each row lists 32 distinct block numbers. `down_idx`: each row lists 32 distinct block numbers.
All inputs are finite; a program needn't handle non-finite values.
Results may differ from the reference program's by a relative error of at most 0.023.
Values may be sent and summed in bfloat16 or wider, within the bound.
No kernel may reach another device: no remote copies, remote signals or barrier semaphores. Data moves between devices by JAX's collectives and lax.ppermute only.
A program may use at most 192 MiB of HBM per device.

```python
import jax
import jax.numpy as jnp
from jax import lax

D = 4096
FF = 14336
BLK = 64
GRID_ROWS = 512
TOKENS = 4096
FBLK = 224
KEEP = 32
N_ROW = 8
N_COL = 16


def pick_blocks(key, panels, blocks, kept_count):
    key_favour, key_jitter = jax.random.split(key)
    favour = jax.random.randint(key_favour, (blocks,), 0, 4)
    jitter = jax.random.randint(key_jitter, (panels, blocks), 0, 65536)
    column_ids = lax.broadcasted_iota(jnp.int32, (panels, blocks), 1)
    panel_ids = lax.broadcasted_iota(jnp.int32, (panels, blocks), 0)
    scores = (favour[None, :] * 65536 + jitter) * blocks + column_ids
    at_edges = (column_ids == 0) | (column_ids == blocks - 1)
    scores = jnp.where((panel_ids == 0) & at_edges, 268435456 + column_ids, scores)
    chosen = lax.top_k(scores, kept_count)[1]
    return chosen.astype(jnp.int32)


def draw_gate_idx(key, part):
    return pick_blocks(jax.random.fold_in(key, 11), FF // BLK, D // BLK, D // BLK // 2)


def draw_up_idx(key, part):
    return pick_blocks(jax.random.fold_in(key, 12), FF // BLK, D // BLK, D // BLK // 2)


def draw_down_idx(key, part):
    return pick_blocks(jax.random.fold_in(key, 13), FF // BLK, D // BLK, D // BLK // 2)


def shard_levels(rng, dims, cuts, smallest, largest):
    loudness = 1.0
    for position, parts in cuts:
        heights = jax.random.uniform(jax.random.fold_in(jax.random.fold_in(rng, 6), position), (parts,), jnp.float32, smallest / len(cuts), largest / len(cuts))
        loudness = loudness * jnp.repeat(jnp.exp(heights), dims[position] // parts).reshape((-1,) + (1,) * (len(dims) - 1 - position))
    return loudness


def noise(own_key, shape, width, bound, pieces=(), kind=jnp.bfloat16):
    result = width * jax.random.normal(own_key, shape, jnp.float32)
    if pieces:
        result = result * shard_levels(own_key, shape, pieces, -0.22, 0.18)
    return jnp.clip(result, -bound, bound).astype(kind)


def setup_inputs(seed: int = 0) -> dict:
    keys = jax.random.split(jax.random.key(seed), 9)
    x_seq = noise(keys[0], (TOKENS, D), 1.0, 6.0, ((0, 128),))
    dy_seq = noise(keys[1], (TOKENS, D), 0.5, 3.0, ((0, 128),))
    gate_vals = noise(keys[2], (FBLK, KEEP, BLK * BLK), (D // 2) ** -0.5, 0.125, ((0, 16), (1, 8)))
    gate_idx = draw_gate_idx(jax.random.fold_in(keys[8], 71), 0)
    up_vals = noise(keys[4], (FBLK, KEEP, BLK * BLK), (D // 2) ** -0.5, 0.125, ((0, 16), (1, 8)))
    up_idx = draw_up_idx(jax.random.fold_in(keys[8], 71), 0)
    down_vals = noise(keys[6], (FBLK, KEEP, BLK * BLK), (FF // 2) ** -0.5, 0.0625, ((0, 16), (1, 8)))
    down_idx = draw_down_idx(jax.random.fold_in(keys[8], 71), 0)
    return dict(x_seq=x_seq, dy_seq=dy_seq, gate_vals=gate_vals, gate_idx=gate_idx, up_vals=up_vals, up_idx=up_idx, down_vals=down_vals, down_idx=down_idx)


def panel_lines(block_ids):
    return jnp.broadcast_to(jnp.arange(block_ids.shape[0], dtype=jnp.int32)[:, None], block_ids.shape)


def dense_in(values, block_ids):
    panels, kept = block_ids.shape
    blocks = values.reshape(panels, kept, BLK, BLK)
    grid = jnp.zeros((D // BLK, BLK, panels, BLK), values.dtype)
    grid = grid.at[block_ids, :, panel_lines(block_ids), :].set(blocks)
    return grid.reshape(D, FF)


def dense_out(values, block_ids):
    panels, kept = block_ids.shape
    blocks = values.reshape(panels, kept, BLK, BLK)
    grid = jnp.zeros((panels, BLK, D // BLK, BLK), values.dtype)
    grid = grid.at[panel_lines(block_ids), :, block_ids, :].set(blocks)
    return grid.reshape(FF, D)


def pack_in(dense, block_ids):
    panels, kept = block_ids.shape
    grid = dense.reshape(D // BLK, BLK, panels, BLK)
    return grid[block_ids, :, panel_lines(block_ids), :].reshape(panels, kept, BLK * BLK)


def pack_out(dense, block_ids):
    panels, kept = block_ids.shape
    grid = dense.reshape(panels, BLK, D // BLK, BLK)
    return grid[panel_lines(block_ids), :, block_ids, :].reshape(panels, kept, BLK * BLK)


def owner_sum(lefts, rights):
    units = FF // N_COL
    rows = lefts[0].shape[0]
    cols = rights[0].shape[1]

    def step(total, index):
        term = jnp.zeros((rows, cols), jnp.float32)
        for left, right in zip(lefts, rights):
            left_part = lax.dynamic_slice_in_dim(left, index * units, units, 1)
            right_part = lax.dynamic_slice_in_dim(right, index * units, units, 0)
            term = term + jnp.dot(left_part, right_part, preferred_element_type=jnp.float32)
        rounded = lax.optimization_barrier(term.astype(jnp.bfloat16))
        return total + rounded.astype(jnp.float32), None

    start = jnp.zeros((rows, cols), jnp.float32)
    total, _ = lax.scan(step, start, jnp.arange(N_COL, dtype=jnp.int32))
    return total.astype(jnp.bfloat16)


def grouped_blocks(left, right, block_ids, outward):
    rows = GRID_ROWS
    panels, kept = block_ids.shape

    def step(total, index):
        first = lax.dynamic_slice_in_dim(left, index * rows, rows, 0)
        second = lax.dynamic_slice_in_dim(right, index * rows, rows, 0)
        part = lax.dot_general(first, second, (((0,), (0,)), ((), ())), preferred_element_type=jnp.float32)
        packed = pack_out(part, block_ids) if outward else pack_in(part, block_ids)
        rounded = lax.optimization_barrier(packed.astype(jnp.bfloat16))
        return total + rounded.astype(jnp.float32), None

    start = jnp.zeros((panels, kept, BLK * BLK), jnp.float32)
    total, _ = lax.scan(step, start, jnp.arange(N_ROW, dtype=jnp.int32))
    return total.astype(jnp.bfloat16)


def reference(x_seq, dy_seq, gate_vals, gate_idx, up_vals, up_idx, down_vals, down_idx):
    w_gate = dense_in(gate_vals, gate_idx)
    w_up = dense_in(up_vals, up_idx)
    w_down = dense_out(down_vals, down_idx)
    gate = jnp.dot(x_seq, w_gate, preferred_element_type=jnp.float32)
    up = jnp.dot(x_seq, w_up, preferred_element_type=jnp.float32)
    sigma = jax.nn.sigmoid(gate)
    hidden = (gate * sigma * up).astype(jnp.bfloat16)
    y_seq = owner_sum((hidden,), (w_down,))
    d_hidden = jnp.dot(dy_seq, w_down.T, preferred_element_type=jnp.float32)
    d_gate = (d_hidden * up * sigma * (1.0 + gate * (1.0 - sigma))).astype(jnp.bfloat16)
    d_up = (d_hidden * gate * sigma).astype(jnp.bfloat16)
    dx_seq = owner_sum((d_gate, d_up), (w_gate.T, w_up.T))
    d_gate_vals = grouped_blocks(x_seq, d_gate, gate_idx, False)
    d_up_vals = grouped_blocks(x_seq, d_up, up_idx, False)
    d_down_vals = grouped_blocks(hidden, dy_seq, down_idx, True)
    return (y_seq, dx_seq, d_gate_vals, d_up_vals, d_down_vals)
```

```python
import jax
import jax.numpy as jnp
from jax import lax
from jax.experimental import pallas as pl
from jax.experimental.pallas import tpu as pltpu
from jax.sharding import Mesh, PartitionSpec as P

BLK = 64
AXES = ("y", "zh", "x", "zl", "c")
Z = ("zh", "zl")
RING = 4
BF = jnp.bfloat16
F32 = jnp.float32
MIB = 1024 * 1024


def shift(value, axis, step):
    return lax.ppermute(value, axis, [(i, (i + step) % RING) for i in range(RING)])


def swap(value, axis):
    return lax.ppermute(value, axis, [(0, 1), (1, 0)])


def gather_direct(own, axis):
    below = shift(own, axis, 1)
    above = shift(own, axis, -1)
    across = shift(own, axis, 2)
    return [own, above, across, below]


def gather_ring(own, axis):
    half = own.shape[0] // 2
    below = shift(own, axis, 1)
    above = shift(own, axis, -1)
    across_a = shift(below[:half], axis, 1)
    across_b = shift(above[half:], axis, -1)
    return [own, above, across_a, across_b, below]


def scatter_direct(chunks, axis):
    from_below = shift(chunks[1], axis, 1)
    from_above = shift(chunks[3], axis, -1)
    from_across = shift(chunks[2], axis, 2)
    total = chunks[0].astype(F32) + from_below.astype(F32)
    total = total + from_above.astype(F32) + from_across.astype(F32)
    return total.astype(BF)


def left_half(shape):
    return lax.broadcasted_iota(jnp.int32, shape, len(shape) - 1) % (2 * BLK) < BLK


def flip(value):
    groups = value.shape[1] // 128
    parts = []
    for g in range(groups):
        parts.append(pltpu.roll(value[:, g * 128 : (g + 1) * 128], BLK, 1))
    return jnp.concatenate(parts, axis=1) if groups > 1 else parts[0]


def kernel_params(limit):
    return pltpu.CompilerParams(
        dimension_semantics=("arbitrary",), vmem_limit_bytes=limit * MIB
    )


def forward_kernel(half_panels, kept_here, place, gate_idx, up_idx, x_ref, tiles, w_ref, m_ref, h_ref):
    rows = x_ref.shape[0]
    zh = place[0]

    @pl.when(pl.program_id(0) == 0)
    def _():
        w_ref[...] = jnp.zeros_like(w_ref)
        mask = left_half((BLK, 2 * BLK))

        def put(step, carry):
            group = step // kept_here
            k = step % kept_here
            j = (group // 2) * (2 * kept_here) + (zh ^ (group % 2)) * kept_here + k
            for p in range(half_panels):
                tile = tiles[(group * half_panels + p) * kept_here + k]
                gate_row = pl.multiple_of(gate_idx[zh * half_panels + p, j] * BLK, BLK)
                up_row = pl.multiple_of(up_idx[zh * half_panels + p, j] * BLK, BLK)
                lanes = pl.ds(p * 2 * BLK, 2 * BLK)
                old = w_ref[pl.ds(gate_row, BLK), lanes]
                w_ref[pl.ds(gate_row, BLK), lanes] = jnp.where(mask, tile, old)
                old = w_ref[pl.ds(up_row, BLK), lanes]
                w_ref[pl.ds(up_row, BLK), lanes] = jnp.where(mask, old, tile)
            return carry

        lax.fori_loop(0, 2 * RING * kept_here, put, 0)

    both = jnp.dot(x_ref[...], w_ref[...], preferred_element_type=F32)
    mask = left_half((rows, 2 * BLK))
    previous = None
    for p in range(half_panels):
        lanes = slice(p * 2 * BLK, (p + 1) * 2 * BLK)
        here = both[:, lanes]
        turned = pltpu.roll(here, BLK, 1)
        gate = jnp.where(mask, here, turned)
        up = jnp.where(mask, turned, here)
        sigma = jax.nn.sigmoid(gate)
        silu = gate * sigma
        m_ref[:, lanes] = jnp.where(mask, up * sigma * (1.0 + gate * (1.0 - sigma)), silu)
        hidden = silu * up
        if p % 2 == 0:
            previous = hidden
        if p % 2 == 1:
            merged = jnp.where(mask, previous, hidden)
            h_ref[:, (p // 2) * 128 : (p // 2 + 1) * 128] = merged.astype(BF)
        elif p == half_panels - 1:
            merged = jnp.where(mask, hidden, 0.0)
            h_ref[:, (p // 2) * 128 : (p // 2 + 1) * 128] = merged.astype(BF)


def output_kernel(half_panels, kept_here, place, down_idx, h_ref, tiles, w_ref, y_ref):
    zh = place[0]
    pairs = kept_here // 2

    @pl.when(pl.program_id(0) == 0)
    def _():
        w_ref[...] = jnp.zeros_like(w_ref)
        mask = left_half((BLK, 2 * BLK))

        def put(step, carry):
            group = step // pairs
            m = step % pairs
            j = (group // 2) * (2 * kept_here) + (zh ^ (group % 2)) * kept_here + 2 * m
            for p in range(half_panels):
                tile = tiles[(group * half_panels + p) * pairs + m]
                turned = flip(tile)
                lanes = pl.ds((p // 2) * 128, 128)
                for h in range(2):
                    row = pl.multiple_of(down_idx[zh * half_panels + p, j + h] * BLK, BLK)
                    source = tile if h == p % 2 else turned
                    old = w_ref[pl.ds(row, BLK), lanes]
                    if p % 2 == 0:
                        w_ref[pl.ds(row, BLK), lanes] = jnp.where(mask, source, old)
                    else:
                        w_ref[pl.ds(row, BLK), lanes] = jnp.where(mask, old, source)
            return carry

        lax.fori_loop(0, 2 * RING * pairs, put, 0)

    width = w_ref.shape[0]
    step = min(width, 1024)
    for start in range(0, width, step):
        part = lax.dot_general(
            h_ref[...], w_ref[start : start + step, :], (((1,), (1,)), ((), ())),
            preferred_element_type=F32,
        )
        y_ref[:, start : start + step] = part.astype(BF)


def backward_kernel(half_panels, dy_ref, wd_ref, m_ref, w_ref, g_ref, dx_ref):
    rows = dy_ref.shape[0]
    d_hidden = jnp.dot(dy_ref[...], wd_ref[...], preferred_element_type=F32)
    mask = left_half((rows, 2 * BLK))
    for p in range(half_panels):
        if p % 2 == 0:
            here = d_hidden[:, (p // 2) * 128 : (p // 2 + 1) * 128]
            turned = pltpu.roll(here, BLK, 1)
            spread = jnp.where(mask, here, turned)
        else:
            spread = jnp.where(mask, turned, here)
        lanes = slice(p * 2 * BLK, (p + 1) * 2 * BLK)
        g_ref[:, lanes] = (spread * m_ref[:, lanes]).astype(BF)
    width = w_ref.shape[0]
    step = min(width, 1024)
    back = g_ref[...]
    blocks = dx_ref.shape
    for start in range(0, width, step):
        part = lax.dot_general(
            back, w_ref[start : start + step, :], (((1,), (1,)), ((), ())),
            preferred_element_type=F32,
        ).astype(BF)
        per = blocks[3]
        for rz in range(blocks[2]):
            for rx in range(blocks[1]):
                at = (rz * blocks[1] + rx) * per
                dx_ref[0, rx, rz, :, start : start + step] = part[at : at + per]


def down_grad_kernel(half_panels, kept_here, place, down_idx, dy_ref, h_ref, out_ref, acc):
    zh = place[0]
    pairs = kept_here // 2
    i = pl.program_id(0)
    cols = dy_ref.shape[1]
    part = lax.dot_general(
        dy_ref[...], h_ref[...], (((0,), (0,)), ((), ())), preferred_element_type=F32
    )
    acc[pl.ds(pl.multiple_of(i * cols, cols), cols), :] = part.astype(BF)

    @pl.when(i == pl.num_programs(0) - 1)
    def _():
        mask = left_half((BLK, 2 * BLK))

        def take(step, carry):
            group = step // pairs
            m = step % pairs
            j = (group // 2) * (2 * kept_here) + (zh ^ (group % 2)) * kept_here + 2 * m
            for p in range(half_panels):
                lanes = pl.ds((p // 2) * 128, 128)
                row0 = pl.multiple_of(down_idx[zh * half_panels + p, j] * BLK, BLK)
                row1 = pl.multiple_of(down_idx[zh * half_panels + p, j + 1] * BLK, BLK)
                first = acc[pl.ds(row0, BLK), lanes]
                second = acc[pl.ds(row1, BLK), lanes]
                if p % 2 == 0:
                    second = flip(second)
                else:
                    first = flip(first)
                out_ref[(group * half_panels + p) * pairs + m] = jnp.where(mask, first, second)
            return carry

        lax.fori_loop(0, 2 * RING * pairs, take, 0)


def input_grad_kernel(half_panels, kept_here, place, gate_idx, up_idx, x_ref, g_ref, out_ref, acc):
    zh = place[0]
    i = pl.program_id(0)
    cols = x_ref.shape[1]
    part = lax.dot_general(
        x_ref[...], g_ref[...], (((0,), (0,)), ((), ())), preferred_element_type=F32
    )
    acc[pl.ds(pl.multiple_of(i * cols, cols), cols), :] = part.astype(BF)

    @pl.when(i == pl.num_programs(0) - 1)
    def _():
        mask = left_half((BLK, 2 * BLK))

        def take(step, carry):
            group = step // kept_here
            k = step % kept_here
            j = (group // 2) * (2 * kept_here) + (zh ^ (group % 2)) * kept_here + k
            for p in range(half_panels):
                lanes = pl.ds(p * 2 * BLK, 2 * BLK)
                gate_row = pl.multiple_of(gate_idx[zh * half_panels + p, j] * BLK, BLK)
                up_row = pl.multiple_of(up_idx[zh * half_panels + p, j] * BLK, BLK)
                first = acc[pl.ds(gate_row, BLK), lanes]
                second = acc[pl.ds(up_row, BLK), lanes]
                out_ref[(group * half_panels + p) * kept_here + k] = jnp.where(mask, first, second)
            return carry

        lax.fori_loop(0, 2 * RING * kept_here, take, 0)


def cost(flops, nbytes):
    return pl.CostEstimate(flops=flops, bytes_accessed=nbytes, transcendentals=0)


def per_device(x_seq, dy_seq, gate_vals, gate_idx, up_vals, up_idx, down_vals, down_idx):
    panels, kept_here, square = gate_vals.shape
    per, width = x_seq.shape
    edge = BLK
    half = panels // 2
    zh = lax.axis_index("zh")
    place = jnp.reshape(zh, (1,)).astype(jnp.int32)
    shape = jax.ShapeDtypeStruct

    gate_blk = gate_vals.reshape(panels, kept_here, edge, edge)
    up_blk = up_vals.reshape(panels, kept_here, edge, edge)
    pair_gu = jnp.concatenate([gate_blk, up_blk], axis=3)
    down_blk = down_vals.reshape(panels, kept_here // 2, 2, edge, edge)
    pair_d = jnp.transpose(down_blk, (0, 1, 4, 2, 3)).reshape(
        panels, kept_here // 2, edge, 2 * edge
    )

    def spread(tiles):
        own = lax.dynamic_slice_in_dim(tiles, zh * half, half, 0)
        other = swap(lax.dynamic_slice_in_dim(tiles, (1 - zh) * half, half, 0), "zh")
        both = jnp.stack([own, other]).reshape(-1, edge, 2 * edge)
        return lax.all_gather(both, "y", axis=0, tiled=True)

    gu_tiles = spread(pair_gu)
    d_tiles = spread(pair_d)

    x_row = jnp.concatenate(gather_direct(x_seq, "x"), axis=0)
    x_own = gather_ring(x_row, Z)
    x_all = jnp.concatenate(x_own + [swap(v, "c") for v in x_own], axis=0)
    dy_row = jnp.concatenate(gather_direct(dy_seq, Z), axis=0)
    dy_own = gather_ring(dy_row, "x")
    dy_list = dy_own + [swap(v, "c") for v in dy_own]
    blocks = []
    for v in dy_list:
        for at in range(0, v.shape[0], per):
            blocks.append(v[at : at + per])
    dy_all = jnp.concatenate(
        [blocks[(c * RING + rx) * RING + rz] for c in range(2) for rz in range(RING) for rx in range(RING)],
        axis=0,
    )

    tokens = 2 * RING * RING * per
    rows = tokens // 4
    hid = -(-half * edge // 128) * 128
    two = half * 2 * edge
    full = lambda *dims: pl.BlockSpec(dims, lambda i: (0,) * len(dims))
    smem = pl.BlockSpec(memory_space=pltpu.SMEM)
    gu_flops = 2 * tokens * width * two
    d_flops = 2 * tokens * width * hid

    def part(fn, *extra):
        def body(*refs):
            fn(*extra, *refs)

        return body

    w_gu, mult, hidden = pl.pallas_call(
        part(forward_kernel, half, kept_here),
        grid=(4,),
        in_specs=[
            smem, smem, smem,
            pl.BlockSpec((rows, width), lambda i: (i, 0)),
            full(*gu_tiles.shape),
        ],
        out_specs=[
            full(width, two),
            pl.BlockSpec((rows, two), lambda i: (i, 0)),
            pl.BlockSpec((rows, hid), lambda i: (i, 0)),
        ],
        out_shape=[shape((width, two), BF), shape((tokens, two), F32), shape((tokens, hid), BF)],
        compiler_params=kernel_params(56),
        cost_estimate=cost(gu_flops, 24 * MIB),
        name="forward",
    )(place, gate_idx, up_idx, x_all, gu_tiles)

    w_d, y_part = pl.pallas_call(
        part(output_kernel, half, kept_here),
        grid=(4,),
        in_specs=[
            smem, smem,
            pl.BlockSpec((rows, hid), lambda i: (i, 0)),
            full(*d_tiles.shape),
        ],
        out_specs=[full(width, hid), pl.BlockSpec((rows, width), lambda i: (i, 0))],
        out_shape=[shape((width, hid), BF), shape((tokens, width), BF)],
        compiler_params=kernel_params(48),
        cost_estimate=cost(d_flops, 16 * MIB),
        name="outputs",
    )(place, down_idx, hidden, d_tiles)

    y_half = tokens // 2
    y_chip = (y_part[:y_half].astype(F32) + swap(y_part[y_half:], "c").astype(F32)).astype(BF)
    y_row = RING * per
    y_z = scatter_direct([y_chip[r * y_row : (r + 1) * y_row] for r in range(RING)], Z)
    y_seq = scatter_direct([y_z[r * per : (r + 1) * per] for r in range(RING)], "x")

    back, dx_part = pl.pallas_call(
        part(backward_kernel, half),
        grid=(4,),
        in_specs=[
            pl.BlockSpec((rows, width), lambda i: (i, 0)),
            full(width, hid),
            pl.BlockSpec((rows, two), lambda i: (i, 0)),
            full(width, two),
        ],
        out_specs=[
            pl.BlockSpec((rows, two), lambda i: (i, 0)),
            pl.BlockSpec((1, RING, RING // 2, per, width), lambda i: (i // 2, 0, i % 2, 0, 0)),
        ],
        out_shape=[shape((tokens, two), BF), shape((2, RING, RING, per, width), BF)],
        compiler_params=kernel_params(60),
        cost_estimate=cost(gu_flops + d_flops, 32 * MIB),
        name="backward",
    )(dy_all, w_d, mult, w_gu)

    dx_chip = (dx_part[0].astype(F32) + swap(dx_part[1], "c").astype(F32)).astype(BF)
    dx_x = scatter_direct([dx_chip[r] for r in range(RING)], "x")
    dx_seq = scatter_direct([dx_x[r] for r in range(RING)], Z)

    cols = 512
    gu_terms = pl.pallas_call(
        part(input_grad_kernel, half, kept_here),
        grid=(width // cols,),
        in_specs=[
            smem, smem, smem,
            pl.BlockSpec((tokens, cols), lambda i: (0, i)),
            full(tokens, two),
        ],
        out_specs=full(*gu_tiles.shape),
        out_shape=shape(gu_tiles.shape, BF),
        scratch_shapes=[pltpu.VMEM((width, two), BF)],
        compiler_params=kernel_params(48),
        cost_estimate=cost(gu_flops, 16 * MIB),
        name="input_grads",
    )(place, gate_idx, up_idx, x_all, back)

    d_terms = pl.pallas_call(
        part(down_grad_kernel, half, kept_here),
        grid=(width // cols,),
        in_specs=[
            smem, smem,
            pl.BlockSpec((tokens, cols), lambda i: (0, i)),
            full(tokens, hid),
        ],
        out_specs=full(*d_tiles.shape),
        out_shape=shape(d_tiles.shape, BF),
        scratch_shapes=[pltpu.VMEM((width, hid), BF)],
        compiler_params=kernel_params(48),
        cost_estimate=cost(d_flops, 12 * MIB),
        name="down_grads",
    )(place, down_idx, dy_all, hidden)

    def collect(terms, per_panel):
        summed = lax.psum_scatter(terms, "y", scatter_dimension=0, tiled=True)
        summed = summed.reshape(2, half, per_panel, edge, 2 * edge)
        other = swap(summed[1], "zh")
        low = jnp.where(zh == 0, summed[0], other)
        high = jnp.where(zh == 0, other, summed[0])
        return jnp.concatenate([low, high], axis=0)

    gu_grads = collect(gu_terms, kept_here)
    d_grads = collect(d_terms, kept_here // 2)
    d_gate_vals = gu_grads[..., :edge].reshape(panels, kept_here, square)
    d_up_vals = gu_grads[..., edge:].reshape(panels, kept_here, square)
    d_grads = d_grads.reshape(panels, kept_here // 2, edge, 2, edge)
    d_down_vals = jnp.transpose(d_grads, (0, 1, 3, 4, 2)).reshape(panels, kept_here, square)
    return (y_seq, dx_seq, d_gate_vals, d_up_vals, d_down_vals)


def solution(mesh):
    grid = Mesh(mesh.devices.reshape(4, 2, 4, 2, 2), AXES)
    row, col = ("y", "zh"), ("x", "zl", "c")
    tokens = P(row + col, None)
    vals = P(col, row, None)
    idx = P(col, None)
    return jax.shard_map(
        per_device,
        mesh=grid,
        in_specs=(tokens, tokens, vals, idx, vals, idx, vals, idx),
        out_specs=(tokens, tokens, vals, vals, vals),
        check_vma=False,
    )
```

```python
import jax
import jax.numpy as jnp
from jax import lax
from jax.experimental import pallas as pl
from jax.experimental.pallas import tpu as pltpu
from jax.sharding import Mesh, PartitionSpec as P

BLK = 64
AXES = ("y", "zh", "x", "zl", "c")
Z = ("zh", "zl")
RING = 4
BF = jnp.bfloat16
F32 = jnp.float32
MIB = 1024 * 1024


def shift(value, axis, step):
    return lax.ppermute(value, axis, [(i, (i + step) % RING) for i in range(RING)])


def swap(value, axis):
    return lax.ppermute(value, axis, [(0, 1), (1, 0)])


def gather_direct(own, axis):
    below = shift(own, axis, 1)
    above = shift(own, axis, -1)
    across = shift(own, axis, 2)
    return [own, above, across, below]


def gather_near(own, axis):
    return shift(own, axis, 1), shift(own, axis, -1)


def gather_far(own, near, axis):
    half = own.shape[0] // 2
    below, above = near
    across_a = shift(below[:half], axis, 1)
    across_b = shift(above[half:], axis, -1)
    return [own, above, across_a, across_b, below]


def scatter_direct(chunks, axis):
    from_below = shift(chunks[1], axis, 1)
    from_above = shift(chunks[3], axis, -1)
    from_across = shift(chunks[2], axis, 2)
    total = chunks[0].astype(F32) + from_below.astype(F32)
    total = total + from_above.astype(F32) + from_across.astype(F32)
    return total.astype(BF)


def scatter_halves(chunks, axis):
    half = chunks[2].shape[0] // 2
    low = shift(chunks[2][:half], axis, 1)
    high = shift(chunks[2][half:], axis, -1)
    return low, high


def add(first, second):
    return (first.astype(F32) + second.astype(F32)).astype(BF)


def scatter_rest(chunks, low, high, axis):
    half = chunks[2].shape[0] // 2
    up = jnp.concatenate([add(chunks[1][:half], low), chunks[1][half:]], axis=0)
    down = jnp.concatenate([chunks[3][:half], add(chunks[3][half:], high)], axis=0)
    return shift(up, axis, 1), shift(down, axis, -1)


def left_half(shape):
    return lax.broadcasted_iota(jnp.int32, shape, len(shape) - 1) % (2 * BLK) < BLK


def flip(value):
    groups = value.shape[1] // 128
    parts = []
    for g in range(groups):
        parts.append(pltpu.roll(value[:, g * 128 : (g + 1) * 128], BLK, 1))
    return jnp.concatenate(parts, axis=1) if groups > 1 else parts[0]


def kernel_params(limit):
    return pltpu.CompilerParams(
        dimension_semantics=("arbitrary",), vmem_limit_bytes=limit * MIB
    )


def piece_places(per):
    rows = RING * per
    return [(0, rows), (rows, rows), (2 * rows, rows // 2), (2 * rows + rows // 2, rows // 2), (3 * rows, rows)]


def piece_copies(pieces, buf, sems, columns):
    per_core = len(pieces) // 2
    per = buf.shape[0] // (2 * RING * RING)
    width = buf.shape[1] // columns
    copies = []
    for t in range(columns):
        at = pl.ds(t * width, width)
        group = []
        for n, piece in enumerate(pieces):
            start, rows = piece_places(per)[n % per_core]
            start += (n // per_core) * RING * RING * per
            source = piece if columns == 1 else piece.at[:, at]
            group.append(
                pltpu.make_async_copy(source, buf.at[pl.ds(start, rows), at], sems.at[t, n])
            )
        copies.append(group)
    return copies


def row_tile_waits(copies, i):
    per_core = len(copies) // 2
    for core in range(2):
        for part, names in enumerate(((0, 1), range(2, per_core))):

            @pl.when(i == 2 * core + part)
            def _(core=core, names=names):
                for n in names:
                    copies[core * per_core + n].wait()


def kept_number(group, kept_here, zh):
    return (group // 2) * (2 * kept_here) + (zh ^ (group % 2)) * kept_here


def forward_kernel(half_panels, kept_here, place, gate_idx, up_idx, *refs):
    pieces, (tiles, w_ref, m_ref, h_ref, h2_ref, buf, sems) = refs[:10], refs[10:]
    i = pl.program_id(0)
    zh = place[0]
    rows = buf.shape[0] // 4
    copies = piece_copies(pieces, buf, sems, 1)[0]

    @pl.when(i == 0)
    def _():
        for copy in copies:
            copy.start()
        w_ref[...] = jnp.zeros_like(w_ref)
        mask = left_half((BLK, 2 * BLK))

        def put(step, carry):
            group = step // kept_here
            k = step % kept_here
            j = kept_number(group, kept_here, zh) + k
            for p in range(half_panels):
                tile = tiles[(group * half_panels + p) * kept_here + k]
                gate_row = pl.multiple_of(gate_idx[zh * half_panels + p, j] * BLK, BLK)
                up_row = pl.multiple_of(up_idx[zh * half_panels + p, j] * BLK, BLK)
                lanes = pl.ds(p * 2 * BLK, 2 * BLK)
                old = w_ref[pl.ds(gate_row, BLK), lanes]
                w_ref[pl.ds(gate_row, BLK), lanes] = jnp.where(mask, tile, old)
                old = w_ref[pl.ds(up_row, BLK), lanes]
                w_ref[pl.ds(up_row, BLK), lanes] = jnp.where(mask, old, tile)
            return carry

        lax.fori_loop(0, 2 * RING * kept_here, put, 0)

    row_tile_waits(copies, i)
    x_tile = buf[pl.ds(pl.multiple_of(i * rows, rows), rows), :]
    both = jnp.dot(x_tile, w_ref[...], preferred_element_type=F32)
    mask = left_half((rows, 2 * BLK))
    per = m_ref.shape[3]
    spans = [(a, b, (a * RING + b) * per) for a in range(RING // 2) for b in range(RING)]
    previous = None
    for p in range(half_panels):
        lanes = slice(p * 2 * BLK, (p + 1) * 2 * BLK)
        here = both[:, lanes]
        turned = pltpu.roll(here, BLK, 1)
        gate = jnp.where(mask, here, turned)
        up = jnp.where(mask, turned, here)
        sigma = jax.nn.sigmoid(gate)
        silu = gate * sigma
        mult = jnp.where(mask, up * sigma * (1.0 + gate * (1.0 - sigma)), silu)
        for a, b, at in spans:
            m_ref[0, a, b, :, lanes] = mult[at : at + per]
        hidden = silu * up
        if p % 2 == 0:
            previous = hidden
        if p % 2 == 1 or p == half_panels - 1:
            merged = jnp.where(mask, previous, hidden if p % 2 == 1 else 0.0).astype(BF)
            out = slice((p // 2) * 128, (p // 2 + 1) * 128)
            h_ref[:, out] = merged
            for a, b, at in spans:
                h2_ref[0, b, a, :, out] = merged[at : at + per]


def hidden_grad_kernel(half_panels, *refs):
    pieces, (w_ref, m_ref, g_ref, buf, sems) = refs[:10], refs[10:]
    i = pl.program_id(0)
    rows = buf.shape[0] // 4
    copies = piece_copies(pieces, buf, sems, 1)[0]

    @pl.when(i == 0)
    def _():
        for copy in copies:
            copy.start()

    row_tile_waits(copies, i)
    dy_tile = buf[pl.ds(pl.multiple_of(i * rows, rows), rows), :]
    d_hidden = jnp.dot(dy_tile, w_ref[...], preferred_element_type=F32)
    mask = left_half((rows, 2 * BLK))
    per = m_ref.shape[3]
    for p in range(half_panels):
        if p % 2 == 0:
            here = d_hidden[:, (p // 2) * 128 : (p // 2 + 1) * 128]
            turned = pltpu.roll(here, BLK, 1)
            spread = jnp.where(mask, here, turned)
        else:
            spread = jnp.where(mask, turned, here)
        lanes = slice(p * 2 * BLK, (p + 1) * 2 * BLK)
        for rx in range(RING // 2):
            for rz in range(RING):
                at = (rx * RING + rz) * per
                g_ref[0, rz, rx, :, lanes] = (
                    spread[at : at + per] * m_ref[0, rz, rx, :, lanes]
                ).astype(BF)


def rows_kernel(left_ref, w_ref, out_ref):
    width = w_ref.shape[0]
    step = min(width, 1024)
    left = left_ref[...]
    for start in range(0, width, step):
        out_ref[:, start : start + step] = lax.dot_general(
            left, w_ref[start : start + step, :], (((1,), (1,)), ((), ())),
            preferred_element_type=F32,
        ).astype(BF)


def output_kernel(half_panels, kept_here, place, down_idx, h_ref, tiles, w_ref, y_ref):
    zh = place[0]
    pairs = kept_here // 2

    @pl.when(pl.program_id(0) == 0)
    def _():
        w_ref[...] = jnp.zeros_like(w_ref)
        mask = left_half((BLK, 2 * BLK))

        def put(step, carry):
            group = step // pairs
            m = step % pairs
            j = kept_number(group, kept_here, zh) + 2 * m
            for p in range(half_panels):
                tile = tiles[(group * half_panels + p) * pairs + m]
                turned = flip(tile)
                lanes = pl.ds((p // 2) * 128, 128)
                for h in range(2):
                    row = pl.multiple_of(down_idx[zh * half_panels + p, j + h] * BLK, BLK)
                    source = tile if h == p % 2 else turned
                    old = w_ref[pl.ds(row, BLK), lanes]
                    if p % 2 == 0:
                        w_ref[pl.ds(row, BLK), lanes] = jnp.where(mask, source, old)
                    else:
                        w_ref[pl.ds(row, BLK), lanes] = jnp.where(mask, old, source)
            return carry

        lax.fori_loop(0, 2 * RING * pairs, put, 0)

    rows_kernel(h_ref, w_ref, y_ref)


def back_kernel(left_ref, w_ref, first_ref, second_ref):
    width = w_ref.shape[0]
    half = width // 2
    step = min(half, 1024)
    per = first_ref.shape[2]
    left = left_ref[...]
    for start in range(0, width, step):
        part = lax.dot_general(
            left, w_ref[start : start + step, :], (((1,), (1,)), ((), ())),
            preferred_element_type=F32,
        ).astype(BF)
        for a in range(RING // 2):
            for b in range(RING):
                at = (a * RING + b) * per
                if start < half:
                    first_ref[b, a, :, start : start + step] = part[at : at + per]
                else:
                    second_ref[a, b, :, start - half : start - half + step] = part[at : at + per]


def grad_matmul(pieces, right_ref, acc, buf, sems):
    i = pl.program_id(0)
    count = sems.shape[0]
    copies = piece_copies(pieces, buf, sems, count)
    cols = buf.shape[1] // count

    @pl.when(i == 0)
    def _():
        for group in copies:
            for copy in group:
                copy.start()

    for t in range(count):

        @pl.when(i == t)
        def _(t=t):
            for copy in copies[t]:
                copy.wait()
            at = slice(t * cols, (t + 1) * cols)
            part = lax.dot_general(
                buf[:, at], right_ref[...], (((0,), (0,)), ((), ())), preferred_element_type=F32
            )
            acc[at, :] = part.astype(BF)


def down_grad_kernel(half_panels, kept_here, place, down_idx, *refs):
    pieces, (h_ref, out_ref, acc, buf, sems) = refs[:10], refs[10:]
    zh = place[0]
    pairs = kept_here // 2
    grad_matmul(pieces, h_ref, acc, buf, sems)

    @pl.when(pl.program_id(0) == pl.num_programs(0) - 1)
    def _():
        mask = left_half((BLK, 2 * BLK))

        def take(step, carry):
            group = step // pairs
            m = step % pairs
            j = kept_number(group, kept_here, zh) + 2 * m
            for p in range(half_panels):
                lanes = pl.ds((p // 2) * 128, 128)
                row0 = pl.multiple_of(down_idx[zh * half_panels + p, j] * BLK, BLK)
                row1 = pl.multiple_of(down_idx[zh * half_panels + p, j + 1] * BLK, BLK)
                first = acc[pl.ds(row0, BLK), lanes]
                second = acc[pl.ds(row1, BLK), lanes]
                if p % 2 == 0:
                    second = flip(second)
                else:
                    first = flip(first)
                out_ref[(group * half_panels + p) * pairs + m] = jnp.where(mask, first, second)
            return carry

        lax.fori_loop(0, 2 * RING * pairs, take, 0)


def input_grad_kernel(half_panels, kept_here, place, gate_idx, up_idx, *refs):
    pieces, (g_ref, out_ref, acc, buf, sems) = refs[:10], refs[10:]
    zh = place[0]
    grad_matmul(pieces, g_ref, acc, buf, sems)

    @pl.when(pl.program_id(0) == pl.num_programs(0) - 1)
    def _():
        mask = left_half((BLK, 2 * BLK))

        def take(step, carry):
            group = step // kept_here
            k = step % kept_here
            j = kept_number(group, kept_here, zh) + k
            for p in range(half_panels):
                lanes = pl.ds(p * 2 * BLK, 2 * BLK)
                gate_row = pl.multiple_of(gate_idx[zh * half_panels + p, j] * BLK, BLK)
                up_row = pl.multiple_of(up_idx[zh * half_panels + p, j] * BLK, BLK)
                first = acc[pl.ds(gate_row, BLK), lanes]
                second = acc[pl.ds(up_row, BLK), lanes]
                out_ref[(group * half_panels + p) * kept_here + k] = jnp.where(mask, first, second)
            return carry

        lax.fori_loop(0, 2 * RING * kept_here, take, 0)


def cost(flops, nbytes):
    return pl.CostEstimate(flops=flops // 8, bytes_accessed=nbytes // 8, transcendentals=0)


def per_device(x_seq, dy_seq, gate_vals, gate_idx, up_vals, up_idx, down_vals, down_idx):
    panels, kept_here, square = gate_vals.shape
    per, width = x_seq.shape
    edge = BLK
    half = panels // 2
    zh = lax.axis_index("zh")
    place = jnp.reshape(zh, (1,)).astype(jnp.int32)
    shape = jax.ShapeDtypeStruct

    gate_blk = gate_vals.reshape(panels, kept_here, edge, edge)
    up_blk = up_vals.reshape(panels, kept_here, edge, edge)
    pair_gu = jnp.concatenate([gate_blk, up_blk], axis=3)
    down_blk = down_vals.reshape(panels, kept_here // 2, 2, edge, edge)
    pair_d = jnp.transpose(down_blk, (0, 1, 4, 2, 3)).reshape(
        panels, kept_here // 2, edge, 2 * edge
    )

    def shares(tiles):
        own = lax.dynamic_slice_in_dim(tiles, zh * half, half, 0)
        other = lax.dynamic_slice_in_dim(tiles, (1 - zh) * half, half, 0)
        return own, other

    def spread(own, received):
        both = jnp.stack([own, received]).reshape(-1, edge, 2 * edge)
        return lax.all_gather(both, "y", axis=0, tiled=True)

    dy_abs = lax.all_gather(dy_seq, Z, axis=0, tiled=True)
    gu_own, gu_other = shares(pair_gu)
    gu_recv = swap(gu_other, "zh")
    d_own, d_other = shares(pair_d)
    d_recv = swap(d_other, "zh")
    x_row = jnp.concatenate(gather_direct(x_seq, "x"), axis=0)
    gu_recv, dy_abs, x_row = lax.optimization_barrier((gu_recv, dy_abs, x_row))
    gu_tiles = spread(gu_own, gu_recv)
    z_place = lax.axis_index(Z)
    dy_row = jnp.roll(dy_abs, -z_place * per, axis=0)
    x_near, dy_near = gather_near(x_row, Z), gather_near(dy_row, "x")
    x_near, dy_near, d_recv = lax.optimization_barrier((x_near, dy_near, d_recv))
    x_own = gather_far(x_row, x_near, Z)
    x_pieces = x_own + [swap(v, "c") for v in x_own]
    dy_own = gather_far(dy_row, dy_near, "x")
    dy_pieces = dy_own + [swap(v, "c") for v in dy_own]
    d_tiles = spread(d_own, d_recv)

    tokens = 2 * RING * RING * per
    rows = tokens // 4
    hid = -(-half * edge // 128) * 128
    two = half * 2 * edge
    pair = RING // 2
    full = lambda *dims: pl.BlockSpec(dims, lambda i: (0,) * len(dims))
    smem = pl.BlockSpec(memory_space=pltpu.SMEM)
    hbm = [pl.BlockSpec(memory_space=pl.ANY)] * 10
    z_major = lambda last: pl.BlockSpec((1, pair, RING, per, last), lambda i: (i // 2, i % 2, 0, 0, 0))
    x_major = lambda last: pl.BlockSpec((1, RING, pair, per, last), lambda i: (i // 2, 0, i % 2, 0, 0))
    ordered = lambda last: (2, RING, RING, per, last)
    gu_flops = 2 * tokens * width * two
    d_flops = 2 * tokens * width * hid
    token_buf = pltpu.VMEM((tokens, width), BF)

    def part(fn, *extra):
        def body(*refs):
            fn(*extra, *refs)

        return body

    w_gu, mult, hidden, hidden_x = pl.pallas_call(
        part(forward_kernel, half, kept_here),
        grid=(4,),
        in_specs=[smem, smem, smem, *hbm, full(*gu_tiles.shape)],
        out_specs=[
            full(width, two),
            z_major(two),
            pl.BlockSpec((rows, hid), lambda i: (i, 0)),
            x_major(hid),
        ],
        out_shape=[
            shape((width, two), BF),
            shape(ordered(two), F32),
            shape((tokens, hid), BF),
            shape(ordered(hid), BF),
        ],
        scratch_shapes=[token_buf, pltpu.SemaphoreType.DMA((1, 10))],
        compiler_params=kernel_params(56),
        cost_estimate=cost(gu_flops, 24 * MIB),
        name="forward",
    )(place, gate_idx, up_idx, *x_pieces, gu_tiles)

    cols = 8
    d_terms = pl.pallas_call(
        part(down_grad_kernel, half, kept_here),
        grid=(cols,),
        in_specs=[smem, smem, *hbm, full(tokens, hid)],
        out_specs=full(*d_tiles.shape),
        out_shape=shape(d_tiles.shape, BF),
        scratch_shapes=[pltpu.VMEM((width, hid), BF), token_buf, pltpu.SemaphoreType.DMA((cols, 10))],
        compiler_params=kernel_params(48),
        cost_estimate=cost(d_flops, 12 * MIB),
        name="down_grads",
    )(place, down_idx, *dy_pieces, hidden_x.reshape(tokens, hid))

    def project(left, weights, core, name):
        depth = weights.shape[1]
        return pl.pallas_call(
            back_kernel,
            grid=(2,),
            in_specs=[
                pl.BlockSpec((rows, depth), lambda i: (2 * core + i, 0)),
                full(width, depth),
            ],
            out_specs=[
                pl.BlockSpec((RING, pair, per, width // 2), lambda i: (0, i, 0, 0)),
                pl.BlockSpec((pair, RING, per, width // 2), lambda i: (i, 0, 0, 0)),
            ],
            out_shape=[shape((RING, RING, per, width // 2), BF)] * 2,
            compiler_params=kernel_params(48),
            cost_estimate=cost(gu_flops // 2, 10 * MIB),
            name=name,
        )(left, weights)

    hidden, d_terms = lax.optimization_barrier((hidden, d_terms))
    w_d, y_away = pl.pallas_call(
        part(output_kernel, half, kept_here),
        grid=(2,),
        in_specs=[
            smem, smem,
            pl.BlockSpec((rows, hid), lambda i: (2 + i, 0)),
            full(*d_tiles.shape),
        ],
        out_specs=[full(width, hid), pl.BlockSpec((rows, width), lambda i: (i, 0))],
        out_shape=[shape((width, hid), BF), shape((tokens // 2, width), BF)],
        compiler_params=kernel_params(48),
        cost_estimate=cost(d_flops // 2, 10 * MIB),
        name="outputs_away",
    )(place, down_idx, hidden, d_tiles)
    y_recv = swap(y_away, "c")
    y_kept = pl.pallas_call(
        rows_kernel,
        grid=(2,),
        in_specs=[pl.BlockSpec((rows, hid), lambda i: (i, 0)), full(width, hid)],
        out_specs=pl.BlockSpec((rows, width), lambda i: (i, 0)),
        out_shape=shape((tokens // 2, width), BF),
        compiler_params=kernel_params(48),
        cost_estimate=cost(d_flops // 2, 10 * MIB),
        name="outputs_kept",
    )(hidden, w_d)

    mult, y_kept = lax.optimization_barrier((mult, y_kept))
    back = pl.pallas_call(
        part(hidden_grad_kernel, half),
        grid=(4,),
        in_specs=[*hbm, full(width, hid), x_major(two)],
        out_specs=x_major(two),
        out_shape=shape(ordered(two), BF),
        scratch_shapes=[token_buf, pltpu.SemaphoreType.DMA((1, 10))],
        compiler_params=kernel_params(56),
        cost_estimate=cost(d_flops, 20 * MIB),
        name="hidden_grads",
    )(*dy_pieces, w_d, mult)
    back = back.reshape(tokens, two)

    z_rows = RING * per
    y_sum = [
        add(y_kept[r * z_rows : (r + 1) * z_rows], y_recv[r * z_rows : (r + 1) * z_rows])
        for r in range(RING)
    ]
    back, y_sum = lax.optimization_barrier((back, y_sum))
    y_low, y_high = scatter_halves(y_sum, Z)

    gu_terms = pl.pallas_call(
        part(input_grad_kernel, half, kept_here),
        grid=(cols,),
        in_specs=[smem, smem, smem, *hbm, full(tokens, two)],
        out_specs=full(*gu_tiles.shape),
        out_shape=shape(gu_tiles.shape, BF),
        scratch_shapes=[pltpu.VMEM((width, two), BF), token_buf, pltpu.SemaphoreType.DMA((cols, 10))],
        compiler_params=kernel_params(56),
        cost_estimate=cost(gu_flops, 16 * MIB),
        name="input_grads",
    )(place, gate_idx, up_idx, *x_pieces, back)

    back, gu_terms, y_low, y_high = lax.optimization_barrier((back, gu_terms, y_low, y_high))
    y_below, y_above = scatter_rest(y_sum, y_low, y_high, Z)
    dx_away = project(back, w_gu, 1, "backward_away")
    dx_recv = [swap(v, "c") for v in dx_away]
    back, dx_away = lax.optimization_barrier((back, dx_away))
    dx_kept = project(back, w_gu, 0, "backward_kept")
    first, second = [[add(dx_kept[n][r], dx_recv[n][r]) for r in range(RING)] for n in range(2)]
    y_below, y_above, first, second = lax.optimization_barrier((y_below, y_above, first, second))
    y_z = add(y_sum[0].astype(F32) + y_below.astype(F32), y_above)
    first = scatter_direct(first, "x")
    second = scatter_direct(second, Z)
    y_seq = scatter_direct([y_z[r * per : (r + 1) * per] for r in range(RING)], "x")
    first = scatter_direct([first[r] for r in range(RING)], Z)
    second = scatter_direct([second[r] for r in range(RING)], "x")
    dx_seq = jnp.concatenate([first, second], axis=1)

    def collect(terms, per_panel):
        summed = lax.psum_scatter(terms, "y", scatter_dimension=0, tiled=True)
        summed = summed.reshape(2, half, per_panel, edge, 2 * edge)
        other = swap(summed[1], "zh")
        low = jnp.where(zh == 0, summed[0], other)
        high = jnp.where(zh == 0, other, summed[0])
        return jnp.concatenate([low, high], axis=0)

    gu_grads = collect(gu_terms, kept_here)
    d_grads = collect(d_terms, kept_here // 2)
    d_gate_vals = gu_grads[..., :edge].reshape(panels, kept_here, square)
    d_up_vals = gu_grads[..., edge:].reshape(panels, kept_here, square)
    d_grads = d_grads.reshape(panels, kept_here // 2, edge, 2, edge)
    d_down_vals = jnp.transpose(d_grads, (0, 1, 3, 4, 2)).reshape(panels, kept_here, square)
    return (y_seq, dx_seq, d_gate_vals, d_up_vals, d_down_vals)


def solution(mesh):
    grid = Mesh(mesh.devices.reshape(4, 2, 4, 2, 2), AXES)
    row, col = ("y", "zh"), ("x", "zl", "c")
    tokens = P(row + col, None)
    vals = P(col, row, None)
    idx = P(col, None)
    return jax.shard_map(
        per_device,
        mesh=grid,
        in_specs=(tokens, tokens, vals, idx, vals, idx, vals, idx),
        out_specs=(tokens, tokens, vals, vals, vals),
        check_vma=False,
    )
```

```python
import jax
import jax.numpy as jnp
from jax import lax
from jax.experimental import pallas as pl
from jax.experimental.pallas import tpu as pltpu
from jax.sharding import Mesh, PartitionSpec as P

BLK = 64
AXES = ("y", "zh", "x", "zl", "c")
Z = ("zh", "zl")
RING = 4
BF = jnp.bfloat16
F32 = jnp.float32
MIB = 1024 * 1024


def shift(value, axis, step):
    return lax.ppermute(value, axis, [(i, (i + step) % RING) for i in range(RING)])


def swap(value, axis):
    return lax.ppermute(value, axis, [(0, 1), (1, 0)])


def gather_direct(own, axis):
    below = shift(own, axis, 1)
    above = shift(own, axis, -1)
    across = shift(own, axis, 2)
    return [own, above, across, below]


def gather_near(own, axis):
    return shift(own, axis, 1), shift(own, axis, -1)


def gather_far(own, near, axis):
    half = own.shape[0] // 2
    below, above = near
    across_a = shift(below[:half], axis, 1)
    across_b = shift(above[half:], axis, -1)
    return [own, above, across_a, across_b, below]


def scatter_direct(chunks, axis):
    from_below = shift(chunks[1], axis, 1)
    from_above = shift(chunks[3], axis, -1)
    from_across = shift(chunks[2], axis, 2)
    total = chunks[0].astype(F32) + from_below.astype(F32)
    total = total + from_above.astype(F32) + from_across.astype(F32)
    return total.astype(BF)


def scatter_halves(chunks, axis):
    half = chunks[2].shape[0] // 2
    low = shift(chunks[2][:half], axis, 1)
    high = shift(chunks[2][half:], axis, -1)
    return low, high


def add(first, second):
    return (first.astype(F32) + second.astype(F32)).astype(BF)


def scatter_rest(chunks, low, high, axis):
    half = chunks[2].shape[0] // 2
    up = jnp.concatenate([add(chunks[1][:half], low), chunks[1][half:]], axis=0)
    down = jnp.concatenate([chunks[3][:half], add(chunks[3][half:], high)], axis=0)
    return shift(up, axis, 1), shift(down, axis, -1)


def left_half(shape):
    return lax.broadcasted_iota(jnp.int32, shape, len(shape) - 1) % (2 * BLK) < BLK


def flip(value):
    groups = value.shape[1] // 128
    parts = []
    for g in range(groups):
        parts.append(pltpu.roll(value[:, g * 128 : (g + 1) * 128], BLK, 1))
    return jnp.concatenate(parts, axis=1) if groups > 1 else parts[0]


def kernel_params(limit):
    return pltpu.CompilerParams(
        dimension_semantics=("arbitrary",), vmem_limit_bytes=limit * MIB
    )


def piece_places(per):
    rows = RING * per
    return [(0, rows), (rows, rows), (2 * rows, rows // 2), (2 * rows + rows // 2, rows // 2), (3 * rows, rows)]


def piece_copies(pieces, buf, sems, columns):
    per_core = len(pieces) // 2
    per = buf.shape[0] // (2 * RING * RING)
    width = buf.shape[1] // columns
    copies = []
    for t in range(columns):
        at = pl.ds(t * width, width)
        group = []
        for n, piece in enumerate(pieces):
            start, rows = piece_places(per)[n % per_core]
            start += (n // per_core) * RING * RING * per
            source = piece if columns == 1 else piece.at[:, at]
            group.append(
                pltpu.make_async_copy(source, buf.at[pl.ds(start, rows), at], sems.at[t, n])
            )
        copies.append(group)
    return copies


def row_tile_waits(copies, i):
    per_core = len(copies) // 2
    for core in range(2):
        for part, names in enumerate(((0, 1), range(2, per_core))):

            @pl.when(i == 2 * core + part)
            def _(core=core, names=names):
                for n in names:
                    copies[core * per_core + n].wait()


def kept_number(group, kept_here, zh):
    return (group // 2) * (2 * kept_here) + (zh ^ (group % 2)) * kept_here


def forward_kernel(half_panels, kept_here, place, gate_idx, up_idx, *refs):
    pieces, (tiles, w_out, m_ref, h_ref, h2_ref, w_ref, buf, sems, w_sem) = refs[:10], refs[10:]
    w_copy = pltpu.make_async_copy(w_ref, w_out, w_sem)
    i = pl.program_id(0)
    zh = place[0]
    rows = buf.shape[0] // 4
    copies = piece_copies(pieces, buf, sems, 1)[0]

    @pl.when(i == 0)
    def _():
        for copy in copies:
            copy.start()
        w_ref[...] = jnp.zeros_like(w_ref)
        mask = left_half((BLK, 2 * BLK))

        def put(step, carry):
            group = step // kept_here
            k = step % kept_here
            j = kept_number(group, kept_here, zh) + k
            for p in range(half_panels):
                tile = tiles[(group * half_panels + p) * kept_here + k]
                gate_row = pl.multiple_of(gate_idx[zh * half_panels + p, j] * BLK, BLK)
                up_row = pl.multiple_of(up_idx[zh * half_panels + p, j] * BLK, BLK)
                lanes = pl.ds(p * 2 * BLK, 2 * BLK)
                old = w_ref[pl.ds(gate_row, BLK), lanes]
                w_ref[pl.ds(gate_row, BLK), lanes] = jnp.where(mask, tile, old)
                old = w_ref[pl.ds(up_row, BLK), lanes]
                w_ref[pl.ds(up_row, BLK), lanes] = jnp.where(mask, old, tile)
            return carry

        lax.fori_loop(0, 2 * RING * kept_here, put, 0)
        w_copy.start()

    row_tile_waits(copies, i)
    x_tile = buf[pl.ds(pl.multiple_of(i * rows, rows), rows), :]
    both = jnp.dot(x_tile, w_ref[...], preferred_element_type=F32)
    mask = left_half((rows, 2 * BLK))
    per = m_ref.shape[3]
    spans = [(a, b, (a * RING + b) * per) for a in range(RING // 2) for b in range(RING)]
    previous = None
    for p in range(half_panels):
        lanes = slice(p * 2 * BLK, (p + 1) * 2 * BLK)
        here = both[:, lanes]
        turned = pltpu.roll(here, BLK, 1)
        gate = jnp.where(mask, here, turned)
        up = jnp.where(mask, turned, here)
        sigma = jax.nn.sigmoid(gate)
        silu = gate * sigma
        mult = jnp.where(mask, up * sigma * (1.0 + gate * (1.0 - sigma)), silu)
        for a, b, at in spans:
            m_ref[0, a, b, :, lanes] = mult[at : at + per]
        hidden = silu * up
        if p % 2 == 0:
            previous = hidden
        if p % 2 == 1 or p == half_panels - 1:
            merged = jnp.where(mask, previous, hidden if p % 2 == 1 else 0.0).astype(BF)
            out = slice((p // 2) * 128, (p // 2 + 1) * 128)
            h_ref[:, out] = merged
            for a, b, at in spans:
                h2_ref[0, b, a, :, out] = merged[at : at + per]

    @pl.when(i == pl.num_programs(0) - 1)
    def _():
        w_copy.wait()


def hidden_grad_kernel(half_panels, *refs):
    pieces, (w_ref, m_ref, g_ref, buf, sems) = refs[:10], refs[10:]
    i = pl.program_id(0)
    rows = buf.shape[0] // 4
    copies = piece_copies(pieces, buf, sems, 1)[0]

    @pl.when(i == 0)
    def _():
        for copy in copies:
            copy.start()

    row_tile_waits(copies, i)
    dy_tile = buf[pl.ds(pl.multiple_of(i * rows, rows), rows), :]
    d_hidden = jnp.dot(dy_tile, w_ref[...], preferred_element_type=F32)
    mask = left_half((rows, 2 * BLK))
    per = m_ref.shape[3]
    for p in range(half_panels):
        if p % 2 == 0:
            here = d_hidden[:, (p // 2) * 128 : (p // 2 + 1) * 128]
            turned = pltpu.roll(here, BLK, 1)
            spread = jnp.where(mask, here, turned)
        else:
            spread = jnp.where(mask, turned, here)
        lanes = slice(p * 2 * BLK, (p + 1) * 2 * BLK)
        for rx in range(RING // 2):
            for rz in range(RING):
                at = (rx * RING + rz) * per
                g_ref[0, rz, rx, :, lanes] = (
                    spread[at : at + per] * m_ref[0, rz, rx, :, lanes]
                ).astype(BF)


def rows_kernel(left_ref, w_ref, out_ref):
    width = w_ref.shape[0]
    step = min(width, 1024)
    left = left_ref[...]
    for start in range(0, width, step):
        out_ref[:, start : start + step] = lax.dot_general(
            left, w_ref[start : start + step, :], (((1,), (1,)), ((), ())),
            preferred_element_type=F32,
        ).astype(BF)


def output_kernel(half_panels, kept_here, place, down_idx, h_ref, tiles, w_ref, y_ref):
    zh = place[0]
    pairs = kept_here // 2

    @pl.when(pl.program_id(0) == 0)
    def _():
        w_ref[...] = jnp.zeros_like(w_ref)
        mask = left_half((BLK, 2 * BLK))

        def put(step, carry):
            group = step // pairs
            m = step % pairs
            j = kept_number(group, kept_here, zh) + 2 * m
            for p in range(half_panels):
                tile = tiles[(group * half_panels + p) * pairs + m]
                turned = flip(tile)
                lanes = pl.ds((p // 2) * 128, 128)
                for h in range(2):
                    row = pl.multiple_of(down_idx[zh * half_panels + p, j + h] * BLK, BLK)
                    source = tile if h == p % 2 else turned
                    old = w_ref[pl.ds(row, BLK), lanes]
                    if p % 2 == 0:
                        w_ref[pl.ds(row, BLK), lanes] = jnp.where(mask, source, old)
                    else:
                        w_ref[pl.ds(row, BLK), lanes] = jnp.where(mask, old, source)
            return carry

        lax.fori_loop(0, 2 * RING * pairs, put, 0)

    rows_kernel(h_ref, w_ref, y_ref)


def back_kernel(place, left_ref, w_ref, out_ref):
    i = pl.program_id(0)
    width = w_ref.shape[0]
    step = min(width, 1024)
    per = out_ref.shape[1]
    left = left_ref[...]
    for start in range(0, width, step):
        part = lax.dot_general(
            left, w_ref[start : start + step, :], (((1,), (1,)), ((), ())),
            preferred_element_type=F32,
        ).astype(BF)
        for a in range(RING // 2):
            for b in range(RING):
                at = (a * RING + b) * per
                z = (place[1] + i * (RING // 2) + a) % RING
                x = (place[2] + b) % RING
                out_ref[z * RING + x, :, start : start + step] = part[at : at + per]


def grad_matmul(pieces, right_ref, acc, buf, sems):
    i = pl.program_id(0)
    count = sems.shape[0]
    copies = piece_copies(pieces, buf, sems, count)
    cols = buf.shape[1] // count

    @pl.when(i == 0)
    def _():
        for group in copies:
            for copy in group:
                copy.start()

    for t in range(count):

        @pl.when(i == t)
        def _(t=t):
            for copy in copies[t]:
                copy.wait()
            at = slice(t * cols, (t + 1) * cols)
            part = lax.dot_general(
                buf[:, at], right_ref[...], (((0,), (0,)), ((), ())), preferred_element_type=F32
            )
            acc[at, :] = part.astype(BF)


def down_grad_kernel(half_panels, kept_here, place, down_idx, *refs):
    pieces, (h_ref, out_ref, acc, buf, sems) = refs[:10], refs[10:]
    zh = place[0]
    pairs = kept_here // 2
    grad_matmul(pieces, h_ref, acc, buf, sems)

    @pl.when(pl.program_id(0) == pl.num_programs(0) - 1)
    def _():
        mask = left_half((BLK, 2 * BLK))

        def take(step, carry):
            group = step // pairs
            m = step % pairs
            j = kept_number(group, kept_here, zh) + 2 * m
            for p in range(half_panels):
                lanes = pl.ds((p // 2) * 128, 128)
                row0 = pl.multiple_of(down_idx[zh * half_panels + p, j] * BLK, BLK)
                row1 = pl.multiple_of(down_idx[zh * half_panels + p, j + 1] * BLK, BLK)
                first = acc[pl.ds(row0, BLK), lanes]
                second = acc[pl.ds(row1, BLK), lanes]
                if p % 2 == 0:
                    second = flip(second)
                else:
                    first = flip(first)
                out_ref[(group * half_panels + p) * pairs + m] = jnp.where(mask, first, second)
            return carry

        lax.fori_loop(0, 2 * RING * pairs, take, 0)


def input_grad_kernel(half_panels, kept_here, place, gate_idx, up_idx, *refs):
    pieces, (g_ref, out_ref, acc, buf, sems) = refs[:10], refs[10:]
    zh = place[0]
    grad_matmul(pieces, g_ref, acc, buf, sems)

    @pl.when(pl.program_id(0) == pl.num_programs(0) - 1)
    def _():
        mask = left_half((BLK, 2 * BLK))

        def take(step, carry):
            group = step // kept_here
            k = step % kept_here
            j = kept_number(group, kept_here, zh) + k
            for p in range(half_panels):
                lanes = pl.ds(p * 2 * BLK, 2 * BLK)
                gate_row = pl.multiple_of(gate_idx[zh * half_panels + p, j] * BLK, BLK)
                up_row = pl.multiple_of(up_idx[zh * half_panels + p, j] * BLK, BLK)
                first = acc[pl.ds(gate_row, BLK), lanes]
                second = acc[pl.ds(up_row, BLK), lanes]
                out_ref[(group * half_panels + p) * kept_here + k] = jnp.where(mask, first, second)
            return carry

        lax.fori_loop(0, 2 * RING * kept_here, take, 0)


def cost(flops, nbytes):
    return pl.CostEstimate(flops=flops // 8, bytes_accessed=nbytes // 8, transcendentals=0)


def per_device(x_seq, dy_seq, gate_vals, gate_idx, up_vals, up_idx, down_vals, down_idx):
    panels, kept_here, square = gate_vals.shape
    per, width = x_seq.shape
    edge = BLK
    half = panels // 2
    zh = lax.axis_index("zh")
    place = jnp.stack([zh, lax.axis_index(Z), lax.axis_index("x")]).astype(jnp.int32)
    shape = jax.ShapeDtypeStruct

    gate_blk = gate_vals.reshape(panels, kept_here, edge, edge)
    up_blk = up_vals.reshape(panels, kept_here, edge, edge)
    pair_gu = jnp.concatenate([gate_blk, up_blk], axis=3)
    down_blk = down_vals.reshape(panels, kept_here // 2, 2, edge, edge)
    pair_d = jnp.transpose(down_blk, (0, 1, 4, 2, 3)).reshape(
        panels, kept_here // 2, edge, 2 * edge
    )

    def shares(tiles):
        own = lax.dynamic_slice_in_dim(tiles, zh * half, half, 0)
        other = lax.dynamic_slice_in_dim(tiles, (1 - zh) * half, half, 0)
        return own, other

    def spread(own, received):
        both = jnp.stack([own, received]).reshape(-1, edge, 2 * edge)
        return lax.all_gather(both, "y", axis=0, tiled=True)

    dy_abs = lax.all_gather(dy_seq, Z, axis=0, tiled=True)
    gu_own, gu_other = shares(pair_gu)
    gu_recv = swap(gu_other, "zh")
    d_own, d_other = shares(pair_d)
    x_row = jnp.concatenate(gather_direct(x_seq, "x"), axis=0)
    gu_recv, dy_abs, x_row = lax.optimization_barrier((gu_recv, dy_abs, x_row))
    gu_tiles = spread(gu_own, gu_recv)
    z_place = lax.axis_index(Z)
    dy_row = jnp.roll(dy_abs, -z_place * per, axis=0)
    x_near, dy_near = gather_near(x_row, Z), gather_near(dy_row, "x")
    x_core = swap(x_row, "c")
    x_near, dy_near, x_core = lax.optimization_barrier((x_near, dy_near, x_core))
    x_own = gather_far(x_row, x_near, Z)
    dy_own = gather_far(dy_row, dy_near, "x")
    x_near_core = [swap(x_own[1], "c"), swap(x_own[4], "c")]
    x_own, dy_own, x_near_core, d_other = lax.optimization_barrier((x_own, dy_own, x_near_core, d_other))
    x_far_core = [swap(x_own[2], "c"), swap(x_own[3], "c")]
    x_pieces = x_own + [x_core, x_near_core[0], *x_far_core, x_near_core[1]]
    dy_pieces = dy_own + [swap(v, "c") for v in dy_own]
    d_recv = swap(d_other, "zh")
    d_tiles = spread(d_own, d_recv)

    tokens = 2 * RING * RING * per
    rows = tokens // 4
    hid = -(-half * edge // 128) * 128
    two = half * 2 * edge
    pair = RING // 2
    full = lambda *dims: pl.BlockSpec(dims, lambda i: (0,) * len(dims))
    smem = pl.BlockSpec(memory_space=pltpu.SMEM)
    hbm = [pl.BlockSpec(memory_space=pl.ANY)] * 10
    z_major = lambda last: pl.BlockSpec((1, pair, RING, per, last), lambda i: (i // 2, i % 2, 0, 0, 0))
    x_major = lambda last: pl.BlockSpec((1, RING, pair, per, last), lambda i: (i // 2, 0, i % 2, 0, 0))
    ordered = lambda last: (2, RING, RING, per, last)
    gu_flops = 2 * tokens * width * two
    d_flops = 2 * tokens * width * hid
    token_buf = pltpu.VMEM((tokens, width), BF)

    def part(fn, *extra):
        def body(*refs):
            fn(*extra, *refs)

        return body

    w_gu, mult, hidden, hidden_x = pl.pallas_call(
        part(forward_kernel, half, kept_here),
        grid=(4,),
        in_specs=[smem, smem, smem, *hbm, full(*gu_tiles.shape)],
        out_specs=[
            pl.BlockSpec(memory_space=pl.ANY),
            z_major(two),
            pl.BlockSpec((rows, hid), lambda i: (i, 0)),
            x_major(hid),
        ],
        out_shape=[
            shape((width, two), BF),
            shape(ordered(two), F32),
            shape((tokens, hid), BF),
            shape(ordered(hid), BF),
        ],
        scratch_shapes=[
            pltpu.VMEM((width, two), BF),
            token_buf,
            pltpu.SemaphoreType.DMA((1, 10)),
            pltpu.SemaphoreType.DMA,
        ],
        compiler_params=kernel_params(56),
        cost_estimate=cost(gu_flops, 24 * MIB),
        name="forward",
    )(place, gate_idx, up_idx, *x_pieces, gu_tiles)

    cols = 8
    d_terms = pl.pallas_call(
        part(down_grad_kernel, half, kept_here),
        grid=(cols,),
        in_specs=[smem, smem, *hbm, full(tokens, hid)],
        out_specs=full(*d_tiles.shape),
        out_shape=shape(d_tiles.shape, BF),
        scratch_shapes=[pltpu.VMEM((width, hid), BF), token_buf, pltpu.SemaphoreType.DMA((cols, 10))],
        compiler_params=kernel_params(48),
        cost_estimate=cost(d_flops, 12 * MIB),
        name="down_grads",
    )(place, down_idx, *dy_pieces, hidden_x.reshape(tokens, hid))

    def project(left, weights, core, name):
        depth = weights.shape[1]
        return pl.pallas_call(
            back_kernel,
            grid=(2,),
            in_specs=[
                smem,
                pl.BlockSpec((rows, depth), lambda i: (2 * core + i, 0)),
                full(width, depth),
            ],
            out_specs=full(RING * RING, per, width),
            out_shape=shape((RING * RING, per, width), BF),
            compiler_params=kernel_params(48),
            cost_estimate=cost(gu_flops // 2, 10 * MIB),
            name=name,
        )(place, left, weights)

    hidden, d_terms = lax.optimization_barrier((hidden, d_terms))
    w_d, y_away = pl.pallas_call(
        part(output_kernel, half, kept_here),
        grid=(2,),
        in_specs=[
            smem, smem,
            pl.BlockSpec((rows, hid), lambda i: (2 + i, 0)),
            full(*d_tiles.shape),
        ],
        out_specs=[full(width, hid), pl.BlockSpec((rows, width), lambda i: (i, 0))],
        out_shape=[shape((width, hid), BF), shape((tokens // 2, width), BF)],
        compiler_params=kernel_params(48),
        cost_estimate=cost(d_flops // 2, 10 * MIB),
        name="outputs_away",
    )(place, down_idx, hidden, d_tiles)
    y_recv = swap(y_away, "c")
    y_kept = pl.pallas_call(
        rows_kernel,
        grid=(2,),
        in_specs=[pl.BlockSpec((rows, hid), lambda i: (i, 0)), full(width, hid)],
        out_specs=pl.BlockSpec((rows, width), lambda i: (i, 0)),
        out_shape=shape((tokens // 2, width), BF),
        compiler_params=kernel_params(48),
        cost_estimate=cost(d_flops // 2, 10 * MIB),
        name="outputs_kept",
    )(hidden, w_d)

    mult, y_kept = lax.optimization_barrier((mult, y_kept))
    back = pl.pallas_call(
        part(hidden_grad_kernel, half),
        grid=(4,),
        in_specs=[*hbm, full(width, hid), x_major(two)],
        out_specs=x_major(two),
        out_shape=shape(ordered(two), BF),
        scratch_shapes=[token_buf, pltpu.SemaphoreType.DMA((1, 10))],
        compiler_params=kernel_params(56),
        cost_estimate=cost(d_flops, 20 * MIB),
        name="hidden_grads",
    )(*dy_pieces, w_d, mult)
    back = back.reshape(tokens, two)

    z_rows = RING * per
    y_sum = [
        add(y_kept[r * z_rows : (r + 1) * z_rows], y_recv[r * z_rows : (r + 1) * z_rows])
        for r in range(RING)
    ]
    back, y_sum = lax.optimization_barrier((back, y_sum))
    y_low, y_high = scatter_halves(y_sum, Z)

    gu_terms = pl.pallas_call(
        part(input_grad_kernel, half, kept_here),
        grid=(cols,),
        in_specs=[smem, smem, smem, *hbm, full(tokens, two)],
        out_specs=full(*gu_tiles.shape),
        out_shape=shape(gu_tiles.shape, BF),
        scratch_shapes=[pltpu.VMEM((width, two), BF), token_buf, pltpu.SemaphoreType.DMA((cols, 10))],
        compiler_params=kernel_params(56),
        cost_estimate=cost(gu_flops, 16 * MIB),
        name="input_grads",
    )(place, gate_idx, up_idx, *x_pieces, back)

    back, gu_terms, y_low, y_high = lax.optimization_barrier((back, gu_terms, y_low, y_high))
    y_below, y_above = scatter_rest(y_sum, y_low, y_high, Z)
    dx_away = project(back, w_gu, 1, "backward_away")
    dx_recv = swap(dx_away, "c")
    back, dx_away = lax.optimization_barrier((back, dx_away))
    dx_kept = project(back, w_gu, 0, "backward_kept")
    dx_chip = add(dx_kept, dx_recv)
    dx_parts = lax.all_to_all(dx_chip, (*Z, "x"), 0, 0, tiled=True)
    y_z = add(y_sum[0].astype(F32) + y_below.astype(F32), y_above)
    y_seq = scatter_direct([y_z[r * per : (r + 1) * per] for r in range(RING)], "x")
    dx_seq = jnp.sum(dx_parts.astype(F32), axis=0).astype(BF)

    def collect(terms, per_panel):
        summed = lax.psum_scatter(terms, "y", scatter_dimension=0, tiled=True)
        summed = summed.reshape(2, half, per_panel, edge, 2 * edge)
        other = swap(summed[1], "zh")
        low = jnp.where(zh == 0, summed[0], other)
        high = jnp.where(zh == 0, other, summed[0])
        return jnp.concatenate([low, high], axis=0)

    gu_grads = collect(gu_terms, kept_here)
    d_grads = collect(d_terms, kept_here // 2)
    d_gate_vals = gu_grads[..., :edge].reshape(panels, kept_here, square)
    d_up_vals = gu_grads[..., edge:].reshape(panels, kept_here, square)
    d_grads = d_grads.reshape(panels, kept_here // 2, edge, 2, edge)
    d_down_vals = jnp.transpose(d_grads, (0, 1, 3, 4, 2)).reshape(panels, kept_here, square)
    return (y_seq, dx_seq, d_gate_vals, d_up_vals, d_down_vals)


def solution(mesh):
    grid = Mesh(mesh.devices.reshape(4, 2, 4, 2, 2), AXES)
    row, col = ("y", "zh"), ("x", "zl", "c")
    tokens = P(row + col, None)
    vals = P(col, row, None)
    idx = P(col, None)
    return jax.shard_map(
        per_device,
        mesh=grid,
        in_specs=(tokens, tokens, vals, idx, vals, idx, vals, idx),
        out_specs=(tokens, tokens, vals, vals, vals),
        check_vma=False,
    )
```

```python
import jax
import jax.numpy as jnp
from jax import lax
from jax.experimental import pallas as pl
from jax.experimental.pallas import tpu as pltpu
from jax.sharding import Mesh, PartitionSpec as P

BLK = 64
AXES = ("y", "zh", "x", "zl", "c")
Z = ("zh", "zl")
ZX = ("zh", "zl", "x")
RING = 4
BF = jnp.bfloat16
F32 = jnp.float32
MIB = 1024 * 1024


def shift(value, axis, step):
    return lax.ppermute(value, axis, [(i, (i + step) % RING) for i in range(RING)])


def swap(value, axis):
    return lax.ppermute(value, axis, [(0, 1), (1, 0)])


def gather_direct(own, axis):
    below = shift(own, axis, 1)
    above = shift(own, axis, -1)
    across = shift(own, axis, 2)
    return [own, above, across, below]


def add(first, second):
    return (first.astype(F32) + second.astype(F32)).astype(BF)


def left_half(shape):
    return lax.broadcasted_iota(jnp.int32, shape, len(shape) - 1) % (2 * BLK) < BLK


def flip(value):
    return pltpu.roll(value, BLK, 1)


def kernel_params(limit):
    return pltpu.CompilerParams(
        dimension_semantics=("arbitrary",), vmem_limit_bytes=limit * MIB
    )


def row_copies(pieces, buf, sems):
    rows = pieces[0].shape[0]
    return [
        pltpu.make_async_copy(piece, buf.at[pl.ds(n * rows, rows)], sems.at[n])
        for n, piece in enumerate(pieces)
    ]


def owner_row(place, core, z, x):
    return core * RING * RING + (place[1] + z) % RING * RING + (place[2] + x) % RING


def chunk_copies(pieces, buf, sems, place):
    per = pieces[0].shape[0] // RING
    copies = []
    for n, piece in enumerate(pieces):
        for x in range(RING):
            at = owner_row(place, n // RING, n % RING, x) * per
            copies.append(
                pltpu.make_async_copy(
                    piece.at[pl.ds(x * per, per)],
                    buf.at[pl.ds(pl.multiple_of(at, per), per)],
                    sems.at[n * RING + x],
                )
            )
    return copies


def tile_wait(copies, i):
    for t in range(len(copies) // 2):

        @pl.when(i == t)
        def _(t=t):
            copies[2 * t].wait()
            copies[2 * t + 1].wait()


class Tiles:
    def __init__(self, half_panels, kept_here, zh):
        self.half_panels, self.kept_here, self.zh = half_panels, kept_here, zh
        self.pairs = kept_here // 2
        self.per_panel = kept_here + self.pairs

    def at(self, group, p, k):
        return (group * self.half_panels + p) * self.per_panel + k

    def kept(self, group, k):
        return (group // 2) * (2 * self.kept_here) + (self.zh ^ (group % 2)) * self.kept_here + k

    def row(self, idx_ref, p, j):
        return pl.multiple_of(idx_ref[self.zh * self.half_panels + p, j] * BLK, BLK)


def build_input_weights(where, gate_idx, up_idx, tiles, w_ref):
    w_ref[...] = jnp.zeros_like(w_ref)
    mask = left_half((BLK, 2 * BLK))

    def put(step, carry):
        group, k = step // where.kept_here, step % where.kept_here
        j = where.kept(group, k)
        for p in range(where.half_panels):
            tile = tiles[where.at(group, p, k)]
            lanes = pl.ds(p * 2 * BLK, 2 * BLK)
            for idx_ref, left in ((gate_idx, True), (up_idx, False)):
                rows = pl.ds(where.row(idx_ref, p, j), BLK)
                old = w_ref[rows, lanes]
                w_ref[rows, lanes] = jnp.where(mask, tile, old) if left else jnp.where(mask, old, tile)
        return carry

    lax.fori_loop(0, 2 * RING * where.kept_here, put, 0)


def build_down_weights(where, down_idx, tiles, w_ref):
    w_ref[...] = jnp.zeros_like(w_ref)
    mask = left_half((BLK, 2 * BLK))

    def put(step, carry):
        group, m = step // where.pairs, step % where.pairs
        j = where.kept(group, 2 * m)
        for p in range(where.half_panels):
            tile = tiles[where.at(group, p, where.kept_here + m)]
            turned = flip(tile)
            lanes = pl.ds((p // 2) * 128, 128)
            for h in range(2):
                rows = pl.ds(where.row(down_idx, p, j + h), BLK)
                source = tile if h == p % 2 else turned
                old = w_ref[rows, lanes]
                if p % 2 == 0:
                    w_ref[rows, lanes] = jnp.where(mask, source, old)
                else:
                    w_ref[rows, lanes] = jnp.where(mask, old, source)
        return carry

    lax.fori_loop(0, 2 * RING * where.pairs, put, 0)


def back_rows(left, w_ref, out_ref, place, i):
    width = w_ref.shape[0]
    step = min(width, 1024)
    per = out_ref.shape[1]
    for start in range(0, width, step):
        part = lax.dot_general(
            left, w_ref[start : start + step, :], (((1,), (1,)), ((), ())),
            preferred_element_type=F32,
        ).astype(BF)
        for a in range(RING // 2):
            for b in range(RING):
                at = (a * RING + b) * per
                z = (place[1] + i * (RING // 2) + a) % RING
                x = (place[2] + b) % RING
                out_ref[z * RING + x, :, start : start + step] = part[at : at + per]


def forward_tile(half_panels, x_tile, w_ref, m_ref, h_ref, h2_ref):
    rows = x_tile.shape[0]
    both = jnp.dot(x_tile, w_ref[...], preferred_element_type=F32)
    mask = left_half((rows, 2 * BLK))
    per = m_ref.shape[3]
    spans = [(a, b, (a * RING + b) * per) for a in range(RING // 2) for b in range(RING)]
    previous = None
    for p in range(half_panels):
        lanes = slice(p * 2 * BLK, (p + 1) * 2 * BLK)
        here = both[:, lanes]
        turned = flip(here)
        gate = jnp.where(mask, here, turned)
        up = jnp.where(mask, turned, here)
        sigma = jax.nn.sigmoid(gate)
        silu = gate * sigma
        mult = jnp.where(mask, up * sigma * (1.0 + gate * (1.0 - sigma)), silu)
        for a, b, at in spans:
            m_ref[0, a, b, :, lanes] = mult[at : at + per]
        hidden = silu * up
        if p % 2 == 0:
            previous = hidden
        if p % 2 == 1 or p == half_panels - 1:
            merged = jnp.where(mask, previous, hidden if p % 2 == 1 else 0.0).astype(BF)
            out = slice((p // 2) * 128, (p // 2 + 1) * 128)
            h_ref[:, out] = merged
            for a, b, at in spans:
                h2_ref[0, b, a, :, out] = merged[at : at + per]


def forward_kernel(half_panels, kept_here, first, place, *refs):
    if first:
        gate_idx, up_idx, down_idx, tiles = refs[:4]
        pieces, refs = refs[4:8], refs[8:]
        m_ref, h2_ref, y_ref, w_other, wd_other = refs[:5]
    else:
        w_other, wd_other = refs[:2]
        pieces, refs = refs[2:6], refs[8:]
        m_ref, h2_ref, y_ref = refs[:3]
    w_ref, wd_ref, h_ref, buf, sems, w_sems = refs[-6:]
    i = pl.program_id(0)
    rows = buf.shape[0] // 2
    copies = row_copies(pieces, buf, sems)
    pairs = ((w_ref, w_other), (wd_ref, wd_other))
    if not first:
        pairs = [(b, a) for a, b in pairs]
    w_copies = [pltpu.make_async_copy(a, b, w_sems.at[n]) for n, (a, b) in enumerate(pairs)]

    @pl.when(i == 0)
    def _():
        if not first:
            for copy in w_copies:
                copy.start()
        for copy in copies:
            copy.start()
        if first:
            where = Tiles(half_panels, kept_here, place[0])
            build_input_weights(where, gate_idx, up_idx, tiles, w_ref)
            w_copies[0].start()
            build_down_weights(where, down_idx, tiles, wd_ref)
            w_copies[1].start()
        else:
            w_copies[0].wait()

    tile_wait(copies, i)
    x_tile = buf[pl.ds(pl.multiple_of(i * rows, rows), rows), :]
    forward_tile(half_panels, x_tile, w_ref, m_ref, h_ref, h2_ref)
    if not first:

        @pl.when(i == 0)
        def _():
            w_copies[1].wait()

    back_rows(h_ref[...], wd_ref, y_ref, place, i)
    if first:

        @pl.when(i == pl.num_programs(0) - 1)
        def _():
            for copy in w_copies:
                copy.wait()


def gradient_kernel(half_panels, kept_here, place, gate_idx, up_idx, down_idx, *refs):
    dy_pieces, x_pieces = refs[:8], refs[8:16]
    wd_ref, m_ref, h_ref, back_kept, back_away, out_ref, dy_buf, x_buf, g_ref, acc, dy_sems, x_sems, g_sems = refs[16:]
    i = pl.program_id(0)
    where = Tiles(half_panels, kept_here, place[0])
    rows = dy_buf.shape[0] // 4
    dy_copies = row_copies(dy_pieces, dy_buf, dy_sems)
    x_copies = chunk_copies(x_pieces, x_buf, x_sems, place)
    half_rows = back_kept.shape[0]
    g_copies = [
        pltpu.make_async_copy(g_ref.at[pl.ds(n * half_rows, half_rows)], out, g_sems.at[n])
        for n, out in enumerate((back_kept, back_away))
    ]
    hid = h_ref.shape[1]
    cols = dy_buf.shape[1] // 4
    mask = left_half((rows, 2 * BLK))
    small = left_half((BLK, 2 * BLK))

    @pl.when(i == 0)
    def _():
        for copy in dy_copies:
            copy.start()
        for copy in x_copies:
            copy.start()

    tile_wait(dy_copies, i)

    @pl.when(i < 4)
    def _():
        dy_tile = dy_buf[pl.ds(pl.multiple_of(i * rows, rows), rows), :]
        d_hidden = jnp.dot(dy_tile, wd_ref[...], preferred_element_type=F32)
        per = m_ref.shape[3]
        for p in range(half_panels):
            if p % 2 == 0:
                here = d_hidden[:, (p // 2) * 128 : (p // 2 + 1) * 128]
                turned = flip(here)
                spread = jnp.where(mask, here, turned)
            else:
                spread = jnp.where(mask, turned, here)
            lanes = slice(p * 2 * BLK, (p + 1) * 2 * BLK)
            for a in range(RING // 2):
                for b in range(RING):
                    at = (a * RING + b) * per
                    chunk = owner_row(place, i // 2, b, (i % 2) * (RING // 2) + a)
                    rows_at = pl.ds(pl.multiple_of(chunk * per, per), per)
                    g_ref[rows_at, lanes] = (
                        spread[at : at + per] * m_ref[0, b, a, :, lanes]
                    ).astype(BF)

    @pl.when((i >= 4) & (i < 8))
    def _():
        at = pl.multiple_of((i - 4) * cols, cols)
        part = lax.dot_general(
            dy_buf[:, pl.ds(at, cols)], h_ref[...], (((0,), (0,)), ((), ())),
            preferred_element_type=F32,
        )
        acc[pl.ds(at, cols), :hid] = part.astype(BF)

    @pl.when(i == 4)
    def _():
        for copy in g_copies:
            copy.start()

    @pl.when(i == 7)
    def _():
        for copy in x_copies:
            copy.wait()

        def take(step, carry):
            group, m = step // where.pairs, step % where.pairs
            j = where.kept(group, 2 * m)
            for p in range(half_panels):
                lanes = pl.ds((p // 2) * 128, 128)
                first = acc[pl.ds(where.row(down_idx, p, j), BLK), lanes]
                second = acc[pl.ds(where.row(down_idx, p, j + 1), BLK), lanes]
                if p % 2 == 0:
                    second = flip(second)
                else:
                    first = flip(first)
                out_ref[where.at(group, p, kept_here + m)] = jnp.where(small, first, second)
            return carry

        lax.fori_loop(0, 2 * RING * where.pairs, take, 0)

    @pl.when(i >= 8)
    def _():
        at = pl.multiple_of((i - 8) * cols, cols)
        part = lax.dot_general(
            x_buf[:, pl.ds(at, cols)], g_ref[...], (((0,), (0,)), ((), ())),
            preferred_element_type=F32,
        )
        acc[pl.ds(at, cols), :] = part.astype(BF)

    @pl.when(i == pl.num_programs(0) - 1)
    def _():
        def take(step, carry):
            group, k = step // kept_here, step % kept_here
            j = where.kept(group, k)
            for p in range(half_panels):
                lanes = pl.ds(p * 2 * BLK, 2 * BLK)
                first = acc[pl.ds(where.row(gate_idx, p, j), BLK), lanes]
                second = acc[pl.ds(where.row(up_idx, p, j), BLK), lanes]
                out_ref[where.at(group, p, k)] = jnp.where(small, first, second)
            return carry

        lax.fori_loop(0, 2 * RING * kept_here, take, 0)
        for copy in g_copies:
            copy.wait()


def cost(flops, nbytes):
    return pl.CostEstimate(flops=flops // 8, bytes_accessed=nbytes // 8, transcendentals=0)


def per_device(x_seq, dy_seq, gate_vals, gate_idx, up_vals, up_idx, down_vals, down_idx):
    panels, kept_here, square = gate_vals.shape
    per, width = x_seq.shape
    edge = BLK
    half = panels // 2
    pairs = kept_here // 2
    per_panel = kept_here + pairs
    zh, z_place = lax.axis_index("zh"), lax.axis_index(Z)
    place = jnp.stack([zh, z_place, lax.axis_index("x")]).astype(jnp.int32)
    shape = jax.ShapeDtypeStruct

    gate_blk = gate_vals.reshape(panels, kept_here, edge, edge)
    up_blk = up_vals.reshape(panels, kept_here, edge, edge)
    pair_gu = jnp.concatenate([gate_blk, up_blk], axis=3)
    down_blk = down_vals.reshape(panels, pairs, 2, edge, edge)
    pair_d = jnp.transpose(down_blk, (0, 1, 4, 2, 3)).reshape(panels, pairs, edge, 2 * edge)
    all_pairs = jnp.concatenate([pair_gu, pair_d], axis=1)
    own = lax.dynamic_slice_in_dim(all_pairs, zh * half, half, 0)
    other = swap(lax.dynamic_slice_in_dim(all_pairs, (1 - zh) * half, half, 0), "zh")

    dy_abs = lax.all_gather(dy_seq, Z, axis=0, tiled=True)
    x_row = jnp.concatenate(gather_direct(x_seq, "x"), axis=0)
    other, dy_abs, x_row = lax.optimization_barrier((other, dy_abs, x_row))
    both = jnp.stack([own, other]).reshape(-1, edge, 2 * edge)
    tiles = lax.all_gather(both, "y", axis=0, tiled=True)
    dy_row = jnp.roll(dy_abs, -z_place * per, axis=0)
    x_own = gather_direct(x_row, Z)
    dy_below, dy_above = shift(dy_row, "x", 1), shift(dy_row, "x", -1)
    dy_own = [dy_row, dy_above, shift(dy_row, "x", 2), dy_below]
    x_own, dy_own = lax.optimization_barrier((x_own, dy_own))
    x_core = [swap(v, "c") for v in x_own]

    tokens = 2 * RING * RING * per
    rows = tokens // 4
    hid = -(-half * edge // 128) * 128
    two = half * 2 * edge
    pair = RING // 2
    once = pl.Buffered(1)
    full = lambda *dims: pl.BlockSpec(dims, lambda i: (0,) * len(dims), pipeline_mode=once)
    out_full = lambda *dims: pl.BlockSpec(dims, lambda i: (0,) * len(dims))
    smem = pl.BlockSpec(memory_space=pltpu.SMEM)
    hbm = pl.BlockSpec(memory_space=pl.ANY)
    ordered = lambda last: (2, RING, RING, per, last)
    gu_flops = 2 * tokens * width * two
    d_flops = 2 * tokens * width * hid
    chunks = (RING * RING, per, width)

    def part(fn, *extra):
        def body(*refs):
            fn(*extra, *refs)

        return body

    def forward(core, first, inputs, name):
        specs = [smem] * 4 + [full(*tiles.shape)] + [hbm] * 4 if first else [smem] + [hbm] * 8
        extra_out = [shape((width, two), BF), shape((width, hid), BF)] if first else []
        return pl.pallas_call(
            part(forward_kernel, half, kept_here, first),
            grid=(2,),
            in_specs=specs,
            out_specs=[
                pl.BlockSpec((1, pair, RING, per, two), lambda i: (core, i, 0, 0, 0)),
                pl.BlockSpec((1, RING, pair, per, hid), lambda i: (core, 0, i, 0, 0)),
                out_full(*chunks),
            ] + [hbm] * len(extra_out),
            out_shape=[shape(ordered(two), F32), shape(ordered(hid), BF), shape(chunks, BF)] + extra_out,
            scratch_shapes=[
                pltpu.VMEM((width, two), BF),
                pltpu.VMEM((width, hid), BF),
                pltpu.VMEM((rows, hid), BF),
                pltpu.VMEM((tokens // 2, width), BF),
                pltpu.SemaphoreType.DMA((4,)),
                pltpu.SemaphoreType.DMA((2,)),
            ],
            input_output_aliases={} if first else {7: 0, 8: 1},
            compiler_params=kernel_params(56),
            cost_estimate=cost((gu_flops + d_flops) // 2, 24 * MIB),
            name=name,
        )(place, *inputs)

    mult, hidden, y_away, w_gu, w_d = forward(
        1, True, (gate_idx, up_idx, down_idx, tiles, *x_core), "forward_away"
    )
    dy_core = [swap(v, "c") for v in dy_own]
    y_recv = swap(y_away, "c")
    mult, hidden, y_kept = forward(0, False, (w_gu, w_d, *x_own, mult, hidden), "forward_kept")
    y_chip = add(y_kept, y_recv)
    mult, y_chip = lax.optimization_barrier((mult, y_chip))
    y_parts = lax.all_to_all(y_chip, ZX, 0, 0, tiled=True)

    steps = 12
    x_tile = lambda i: jnp.minimum(i, 3)
    back_kept, back_away, terms = pl.pallas_call(
        part(gradient_kernel, half, kept_here),
        grid=(steps,),
        in_specs=[smem] * 4
        + [hbm] * 16
        + [
            full(width, hid),
            pl.BlockSpec(
                (1, RING, pair, per, two), lambda i: (x_tile(i) // 2, 0, x_tile(i) % 2, 0, 0)
            ),
            full(tokens, hid),
        ],
        out_specs=[hbm, hbm, out_full(*tiles.shape)],
        out_shape=[shape((tokens // 2, two), BF)] * 2 + [shape(tiles.shape, BF)],
        scratch_shapes=[
            pltpu.VMEM((tokens, width), BF),
            pltpu.VMEM((tokens, width), BF),
            pltpu.VMEM((tokens, two), BF),
            pltpu.VMEM((width, two), BF),
            pltpu.SemaphoreType.DMA((8,)),
            pltpu.SemaphoreType.DMA((32,)),
            pltpu.SemaphoreType.DMA((2,)),
        ],
        compiler_params=kernel_params(60),
        cost_estimate=cost(gu_flops + 2 * d_flops, 40 * MIB),
        name="gradients",
    )(
        place, gate_idx, up_idx, down_idx, *dy_own, *dy_core, *x_own, *x_core,
        w_d, mult, hidden.reshape(tokens, hid),
    )

    def project(left):
        return lax.dot_general(left, w_gu, (((1,), (1,)), ((), ())), preferred_element_type=F32)

    back_away, y_parts = lax.optimization_barrier((back_away, y_parts))
    dx_away = project(back_away).astype(BF)
    dx_recv = swap(dx_away, "c")
    back_kept, dx_away = lax.optimization_barrier((back_kept, dx_away))
    dx_kept, dx_recv = lax.optimization_barrier((project(back_kept).astype(BF), dx_recv))
    dx_chip = add(dx_kept, dx_recv).reshape(chunks)
    dx_parts = lax.all_to_all(dx_chip, ZX, 0, 0, tiled=True)
    y_seq = jnp.sum(y_parts.astype(F32), axis=0).astype(BF)
    dx_seq = jnp.sum(dx_parts.astype(F32), axis=0).astype(BF)

    summed = lax.psum_scatter(terms, "y", scatter_dimension=0, tiled=True)
    summed = summed.reshape(2, half, per_panel, edge, 2 * edge)
    other = swap(summed[1], "zh")
    low = jnp.where(zh == 0, summed[0], other)
    high = jnp.where(zh == 0, other, summed[0])
    grads = jnp.concatenate([low, high], axis=0)
    gu_grads = grads[:, :kept_here]
    d_gate_vals = gu_grads[..., :edge].reshape(panels, kept_here, square)
    d_up_vals = gu_grads[..., edge:].reshape(panels, kept_here, square)
    d_grads = grads[:, kept_here:].reshape(panels, pairs, edge, 2, edge)
    d_down_vals = jnp.transpose(d_grads, (0, 1, 3, 4, 2)).reshape(panels, kept_here, square)
    return (y_seq, dx_seq, d_gate_vals, d_up_vals, d_down_vals)


def solution(mesh):
    grid = Mesh(mesh.devices.reshape(4, 2, 4, 2, 2), AXES)
    row, col = ("y", "zh"), ("x", "zl", "c")
    tokens = P(row + col, None)
    vals = P(col, row, None)
    idx = P(col, None)
    return jax.shard_map(
        per_device,
        mesh=grid,
        in_specs=(tokens, tokens, vals, idx, vals, idx, vals, idx),
        out_specs=(tokens, tokens, vals, vals, vals),
        check_vma=False,
    )
```

```python
import jax
import jax.numpy as jnp
from jax import lax
from jax.experimental import pallas as pl
from jax.experimental.pallas import tpu as pltpu
from jax.sharding import Mesh, PartitionSpec as P

BLK = 64
AXES = ("y", "zh", "x", "zl", "c")
Z = ("zh", "zl")
ZX = ("zh", "zl", "x")
RING = 4
BF = jnp.bfloat16
F32 = jnp.float32
MIB = 1024 * 1024


def shift(value, axis, step):
    return lax.ppermute(value, axis, [(i, (i + step) % RING) for i in range(RING)])


def swap(value, axis):
    return lax.ppermute(value, axis, [(0, 1), (1, 0)])


def gather_direct(own, axis):
    below = shift(own, axis, 1)
    above = shift(own, axis, -1)
    across = shift(own, axis, 2)
    return [own, above, across, below]


def scatter_direct(chunks, axis):
    from_below = shift(chunks[1], axis, 1)
    from_above = shift(chunks[3], axis, -1)
    from_across = shift(chunks[2], axis, 2)
    total = chunks[0].astype(F32) + from_below.astype(F32)
    total = total + from_above.astype(F32) + from_across.astype(F32)
    return total.astype(BF)


def add(first, second):
    return (first.astype(F32) + second.astype(F32)).astype(BF)


def left_half(shape):
    return lax.broadcasted_iota(jnp.int32, shape, len(shape) - 1) % (2 * BLK) < BLK


def flip(value):
    return pltpu.roll(value, BLK, 1)


def kernel_params(limit):
    return pltpu.CompilerParams(
        dimension_semantics=("arbitrary",), vmem_limit_bytes=limit * MIB
    )


def row_copies(pieces, buf, sems):
    rows = pieces[0].shape[0]
    return [
        pltpu.make_async_copy(piece, buf.at[pl.ds(n * rows, rows)], sems.at[n])
        for n, piece in enumerate(pieces)
    ]


def owner_row(place, core, z, x):
    return core * RING * RING + (place[1] + z) % RING * RING + (place[2] + x) % RING


def chunk_copies(pieces, buf, sems, place):
    per = pieces[0].shape[0] // RING
    copies = []
    for n, piece in enumerate(pieces):
        for x in range(RING):
            at = owner_row(place, n // RING, n % RING, x) * per
            copies.append(
                pltpu.make_async_copy(
                    piece.at[pl.ds(x * per, per)],
                    buf.at[pl.ds(pl.multiple_of(at, per), per)],
                    sems.at[n * RING + x],
                )
            )
    return copies


def ring_copies(pieces, buf, sems, place):
    per = pieces[0].shape[2]
    copies = []
    for n in range(2 * RING * RING):
        core, x, z = n // (RING * RING), n // RING % RING, n % RING
        source = pieces[core].at[(place[2] + x) % RING, (place[1] + z) % RING]
        copies.append(pltpu.make_async_copy(source, buf.at[pl.ds(n * per, per)], sems.at[n]))
    return copies


def tile_wait(copies, i):
    for t in range(len(copies) // 2):

        @pl.when(i == t)
        def _(t=t):
            copies[2 * t].wait()
            copies[2 * t + 1].wait()


class Tiles:
    def __init__(self, half_panels, kept_here, zh):
        self.half_panels, self.kept_here, self.zh = half_panels, kept_here, zh
        self.pairs = kept_here // 2
        self.per_panel = kept_here + self.pairs

    def at(self, group, p, k):
        return (group * self.half_panels + p) * self.per_panel + k

    def kept(self, group, k):
        return (group // 2) * (2 * self.kept_here) + (self.zh ^ (group % 2)) * self.kept_here + k

    def row(self, idx_ref, p, j):
        return pl.multiple_of(idx_ref[self.zh * self.half_panels + p, j] * BLK, BLK)


def put_blocks(w_ref, places):
    mask = left_half((BLK, 2 * BLK))
    old = [w_ref[rows, lanes] for rows, lanes, _, _ in places]
    for before, (rows, lanes, tile, left) in zip(old, places):
        w_ref[rows, lanes] = jnp.where(mask, tile, before) if left else jnp.where(mask, before, tile)


def build_input_weights(where, gate_idx, up_idx, tiles, w_ref):
    w_ref[...] = jnp.zeros_like(w_ref)

    def put(step, carry):
        group, k = step // where.kept_here, step % where.kept_here
        j = where.kept(group, k)
        block = [tiles[where.at(group, p, k)] for p in range(where.half_panels)]
        for idx_ref, left in ((gate_idx, True), (up_idx, False)):
            put_blocks(w_ref, [
                (pl.ds(where.row(idx_ref, p, j), BLK), pl.ds(p * 2 * BLK, 2 * BLK), block[p], left)
                for p in range(where.half_panels)
            ])
        return carry

    lax.fori_loop(0, 2 * RING * where.kept_here, put, 0)


def build_down_weights(where, down_idx, tiles, w_ref):
    w_ref[...] = jnp.zeros_like(w_ref)

    def put(step, carry):
        group, m = step // where.pairs, step % where.pairs
        j = where.kept(group, 2 * m)
        for parity in range(2):
            places = []
            for p in range(parity, where.half_panels, 2):
                tile = tiles[where.at(group, p, where.kept_here + m)]
                for h in range(2):
                    rows = pl.ds(where.row(down_idx, p, j + h), BLK)
                    source = tile if h == parity else flip(tile)
                    places.append((rows, pl.ds((p // 2) * 128, 128), source, parity == 0))
            put_blocks(w_ref, places)
        return carry

    lax.fori_loop(0, 2 * RING * where.pairs, put, 0)


def back_rows(left, w_ref, out_ref, i):
    width = w_ref.shape[0]
    step = min(width, 1024)
    per = out_ref.shape[1]
    for start in range(0, width, step):
        part = lax.dot_general(
            left, w_ref[start : start + step, :], (((1,), (1,)), ((), ())),
            preferred_element_type=F32,
        ).astype(BF)
        for a in range(RING // 2):
            for b in range(RING):
                at = (a * RING + b) * per
                chunk = (i * (RING // 2) + a) * RING + b
                out_ref[chunk, :, start : start + step] = part[at : at + per]


def forward_tile(half_panels, x_tile, w_ref, m_ref, h_ref, h2_ref):
    rows = x_tile.shape[0]
    both = jnp.dot(x_tile, w_ref[...], preferred_element_type=F32)
    mask = left_half((rows, 2 * BLK))
    per = m_ref.shape[3]
    spans = [(a, b, (a * RING + b) * per) for a in range(RING // 2) for b in range(RING)]
    previous = None
    for p in range(half_panels):
        lanes = slice(p * 2 * BLK, (p + 1) * 2 * BLK)
        here = both[:, lanes]
        turned = flip(here)
        gate = jnp.where(mask, here, turned)
        up = jnp.where(mask, turned, here)
        sigma = jax.nn.sigmoid(gate)
        silu = gate * sigma
        mult = jnp.where(mask, up * sigma * (1.0 + gate * (1.0 - sigma)), silu)
        for a, b, at in spans:
            m_ref[0, a, b, :, lanes] = mult[at : at + per]
        hidden = silu * up
        if p % 2 == 0:
            previous = hidden
        if p % 2 == 1 or p == half_panels - 1:
            merged = jnp.where(mask, previous, hidden if p % 2 == 1 else 0.0).astype(BF)
            out = slice((p // 2) * 128, (p // 2 + 1) * 128)
            h_ref[:, out] = merged
            for a, b, at in spans:
                h2_ref[0, b, a, :, out] = merged[at : at + per]


def forward_kernel(half_panels, kept_here, first, place, *refs):
    if first:
        gate_idx, up_idx, down_idx, tiles = refs[:4]
        pieces, refs = refs[4:8], refs[8:]
        m_ref, h2_ref, y_ref, w_other, wd_other = refs[:5]
    else:
        w_other, wd_other = refs[:2]
        pieces, refs = refs[2:6], refs[8:]
        m_ref, h2_ref, y_ref = refs[:3]
    w_ref, wd_ref, h_ref, buf, sems, w_sems = refs[-6:]
    i = pl.program_id(0)
    rows = buf.shape[0] // 2
    copies = row_copies(pieces, buf, sems)
    pairs = ((w_ref, w_other), (wd_ref, wd_other))
    if not first:
        pairs = [(b, a) for a, b in pairs]
    w_copies = [pltpu.make_async_copy(a, b, w_sems.at[n]) for n, (a, b) in enumerate(pairs)]

    @pl.when(i == 0)
    def _():
        if not first:
            for copy in w_copies:
                copy.start()
        for copy in copies:
            copy.start()
        if first:
            where = Tiles(half_panels, kept_here, place[0])
            build_input_weights(where, gate_idx, up_idx, tiles, w_ref)
            w_copies[0].start()
            build_down_weights(where, down_idx, tiles, wd_ref)
            w_copies[1].start()
        else:
            w_copies[0].wait()

    tile_wait(copies, i)
    x_tile = buf[pl.ds(pl.multiple_of(i * rows, rows), rows), :]
    forward_tile(half_panels, x_tile, w_ref, m_ref, h_ref, h2_ref)
    if not first:

        @pl.when(i == 0)
        def _():
            w_copies[1].wait()

    back_rows(h_ref[...], wd_ref, y_ref, i)
    if first:

        @pl.when(i == pl.num_programs(0) - 1)
        def _():
            for copy in w_copies:
                copy.wait()


def gradient_kernel(half_panels, kept_here, place, gate_idx, up_idx, down_idx, *refs):
    dy_pieces, x_pieces = refs[:2], refs[2:10]
    wd_ref, m_ref, h_ref, back_kept, back_away, out_ref, dy_buf, x_buf, g_ref, acc, dy_sems, x_sems, g_sems = refs[10:]
    i = pl.program_id(0)
    where = Tiles(half_panels, kept_here, place[0])
    rows = dy_buf.shape[0] // 4
    dy_copies = ring_copies(dy_pieces, dy_buf, dy_sems, place)
    x_copies = chunk_copies(x_pieces, x_buf, x_sems, place)
    half_rows = back_kept.shape[0]
    g_copies = [
        pltpu.make_async_copy(g_ref.at[pl.ds(n * half_rows, half_rows)], out, g_sems.at[n])
        for n, out in enumerate((back_kept, back_away))
    ]
    hid = h_ref.shape[1]
    cols = dy_buf.shape[1] // 4
    mask = left_half((rows, 2 * BLK))
    small = left_half((BLK, 2 * BLK))

    @pl.when(i == 0)
    def _():
        for copy in dy_copies:
            copy.start()
        for copy in x_copies:
            copy.start()

    for t in range(4):

        @pl.when(i == t)
        def _(t=t):
            for copy in dy_copies[8 * t : 8 * t + 8]:
                copy.wait()

    @pl.when(i < 4)
    def _():
        dy_tile = dy_buf[pl.ds(pl.multiple_of(i * rows, rows), rows), :]
        d_hidden = jnp.dot(dy_tile, wd_ref[...], preferred_element_type=F32)
        per = m_ref.shape[3]
        for p in range(half_panels):
            if p % 2 == 0:
                here = d_hidden[:, (p // 2) * 128 : (p // 2 + 1) * 128]
                turned = flip(here)
                spread = jnp.where(mask, here, turned)
            else:
                spread = jnp.where(mask, turned, here)
            lanes = slice(p * 2 * BLK, (p + 1) * 2 * BLK)
            for a in range(RING // 2):
                for b in range(RING):
                    at = (a * RING + b) * per
                    chunk = owner_row(place, i // 2, b, (i % 2) * (RING // 2) + a)
                    rows_at = pl.ds(pl.multiple_of(chunk * per, per), per)
                    g_ref[rows_at, lanes] = (
                        spread[at : at + per] * m_ref[0, b, a, :, lanes]
                    ).astype(BF)

    @pl.when((i >= 4) & (i < 8))
    def _():
        at = pl.multiple_of((i - 4) * cols, cols)
        part = lax.dot_general(
            dy_buf[:, pl.ds(at, cols)], h_ref[...], (((0,), (0,)), ((), ())),
            preferred_element_type=F32,
        )
        acc[pl.ds(at, cols), :hid] = part.astype(BF)

    @pl.when(i == 4)
    def _():
        for copy in g_copies:
            copy.start()

    @pl.when(i == 7)
    def _():
        for copy in x_copies:
            copy.wait()

        def take(step, carry):
            group, m = step // where.pairs, step % where.pairs
            j = where.kept(group, 2 * m)
            for p in range(half_panels):
                lanes = pl.ds((p // 2) * 128, 128)
                first = acc[pl.ds(where.row(down_idx, p, j), BLK), lanes]
                second = acc[pl.ds(where.row(down_idx, p, j + 1), BLK), lanes]
                if p % 2 == 0:
                    second = flip(second)
                else:
                    first = flip(first)
                out_ref[where.at(group, p, kept_here + m)] = jnp.where(small, first, second)
            return carry

        lax.fori_loop(0, 2 * RING * where.pairs, take, 0)

    @pl.when(i >= 8)
    def _():
        at = pl.multiple_of((i - 8) * cols, cols)
        part = lax.dot_general(
            x_buf[:, pl.ds(at, cols)], g_ref[...], (((0,), (0,)), ((), ())),
            preferred_element_type=F32,
        )
        acc[pl.ds(at, cols), :] = part.astype(BF)

    @pl.when(i == pl.num_programs(0) - 1)
    def _():
        def take(step, carry):
            group, k = step // kept_here, step % kept_here
            j = where.kept(group, k)
            for p in range(half_panels):
                lanes = pl.ds(p * 2 * BLK, 2 * BLK)
                first = acc[pl.ds(where.row(gate_idx, p, j), BLK), lanes]
                second = acc[pl.ds(where.row(up_idx, p, j), BLK), lanes]
                out_ref[where.at(group, p, k)] = jnp.where(small, first, second)
            return carry

        lax.fori_loop(0, 2 * RING * kept_here, take, 0)
        for copy in g_copies:
            copy.wait()


def cost(flops, nbytes):
    return pl.CostEstimate(flops=flops // 8, bytes_accessed=nbytes // 8, transcendentals=0)


def per_device(x_seq, dy_seq, gate_vals, gate_idx, up_vals, up_idx, down_vals, down_idx):
    panels, kept_here, square = gate_vals.shape
    per, width = x_seq.shape
    edge = BLK
    half = panels // 2
    pairs = kept_here // 2
    per_panel = kept_here + pairs
    zh, z_place = lax.axis_index("zh"), lax.axis_index(Z)
    place = jnp.stack([zh, z_place, lax.axis_index("x")]).astype(jnp.int32)
    shape = jax.ShapeDtypeStruct

    gate_blk = gate_vals.reshape(panels, kept_here, edge, edge)
    up_blk = up_vals.reshape(panels, kept_here, edge, edge)
    pair_gu = jnp.concatenate([gate_blk, up_blk], axis=3)
    down_blk = down_vals.reshape(panels, pairs, 2, edge, edge)
    pair_d = jnp.transpose(down_blk, (0, 1, 4, 2, 3)).reshape(panels, pairs, edge, 2 * edge)
    all_pairs = jnp.concatenate([pair_gu, pair_d], axis=1)
    own = lax.dynamic_slice_in_dim(all_pairs, zh * half, half, 0)
    other = swap(lax.dynamic_slice_in_dim(all_pairs, (1 - zh) * half, half, 0), "zh")

    def gather_all(value, axis):
        wide = jnp.broadcast_to(value[None], (RING, *value.shape))
        return lax.all_to_all(wide, axis, 0, 0, tiled=True)

    dy_row = gather_all(dy_seq, Z)
    x_row = jnp.concatenate(gather_direct(x_seq, "x"), axis=0)
    other, x_row, dy_row = lax.optimization_barrier((other, x_row, dy_row))
    both = jnp.stack([own, other]).reshape(-1, edge, 2 * edge)
    tiles = lax.all_gather(both, "y", axis=0, tiled=True)
    dy_own = gather_all(dy_row, "x")
    x_own = gather_direct(x_row, Z)
    x_core = [swap(v, "c") for v in x_own]
    x_core, dy_own = lax.optimization_barrier((x_core, dy_own))
    dy_core = swap(dy_own, "c")

    tokens = 2 * RING * RING * per
    rows = tokens // 4
    hid = -(-half * edge // 128) * 128
    two = half * 2 * edge
    pair = RING // 2
    once = pl.Buffered(1)
    full = lambda *dims: pl.BlockSpec(dims, lambda i: (0,) * len(dims), pipeline_mode=once)
    out_full = lambda *dims: pl.BlockSpec(dims, lambda i: (0,) * len(dims))
    smem = pl.BlockSpec(memory_space=pltpu.SMEM)
    hbm = pl.BlockSpec(memory_space=pl.ANY)
    ordered = lambda last: (2, RING, RING, per, last)
    gu_flops = 2 * tokens * width * two
    d_flops = 2 * tokens * width * hid
    chunks = (RING * RING, per, width)

    def part(fn, *extra):
        def body(*refs):
            fn(*extra, *refs)

        return body

    def forward(core, first, inputs, name):
        specs = [smem] * 4 + [full(*tiles.shape)] + [hbm] * 4 if first else [smem] + [hbm] * 8
        extra_out = [shape((width, two), BF), shape((width, hid), BF)] if first else []
        return pl.pallas_call(
            part(forward_kernel, half, kept_here, first),
            grid=(2,),
            in_specs=specs,
            out_specs=[
                pl.BlockSpec((1, pair, RING, per, two), lambda i: (core, i, 0, 0, 0)),
                pl.BlockSpec((1, RING, pair, per, hid), lambda i: (core, 0, i, 0, 0)),
                out_full(*chunks),
            ] + [hbm] * len(extra_out),
            out_shape=[shape(ordered(two), F32), shape(ordered(hid), BF), shape(chunks, BF)] + extra_out,
            scratch_shapes=[
                pltpu.VMEM((width, two), BF),
                pltpu.VMEM((width, hid), BF),
                pltpu.VMEM((rows, hid), BF),
                pltpu.VMEM((tokens // 2, width), BF),
                pltpu.SemaphoreType.DMA((4,)),
                pltpu.SemaphoreType.DMA((2,)),
            ],
            input_output_aliases={} if first else {7: 0, 8: 1},
            compiler_params=kernel_params(56),
            cost_estimate=cost((gu_flops + d_flops) // 2, 24 * MIB),
            name=name,
        )(place, *inputs)

    mult, hidden, y_away, w_gu, w_d = forward(
        1, True, (gate_idx, up_idx, down_idx, tiles, *x_core), "forward_away"
    )
    y_recv = swap(y_away, "c")
    mult, hidden, y_kept = forward(0, False, (w_gu, w_d, *x_own, mult, hidden), "forward_kept")
    y_kept, dy_core = lax.optimization_barrier((y_kept, dy_core))
    dy_pieces = [v.reshape(RING, RING, per, width) for v in (dy_own, dy_core)]
    y_sum = [add(y_kept[n * RING : n * RING + RING], y_recv[n * RING : n * RING + RING]) for n in range(RING)]
    mult, y_sum = lax.optimization_barrier((mult, y_sum))
    y_z = scatter_direct(y_sum, Z)

    steps = 12
    x_tile = lambda i: jnp.minimum(i, 3)
    back_kept, back_away, terms = pl.pallas_call(
        part(gradient_kernel, half, kept_here),
        grid=(steps,),
        in_specs=[smem] * 4
        + [hbm] * 10
        + [
            full(width, hid),
            pl.BlockSpec(
                (1, RING, pair, per, two), lambda i: (x_tile(i) // 2, 0, x_tile(i) % 2, 0, 0)
            ),
            full(tokens, hid),
        ],
        out_specs=[hbm, hbm, out_full(*tiles.shape)],
        out_shape=[shape((tokens // 2, two), BF)] * 2 + [shape(tiles.shape, BF)],
        scratch_shapes=[
            pltpu.VMEM((tokens, width), BF),
            pltpu.VMEM((tokens, width), BF),
            pltpu.VMEM((tokens, two), BF),
            pltpu.VMEM((width, two), BF),
            pltpu.SemaphoreType.DMA((32,)),
            pltpu.SemaphoreType.DMA((32,)),
            pltpu.SemaphoreType.DMA((2,)),
        ],
        compiler_params=kernel_params(60),
        cost_estimate=cost(gu_flops + 2 * d_flops, 40 * MIB),
        name="gradients",
    )(
        place, gate_idx, up_idx, down_idx, *dy_pieces, *x_own, *x_core,
        w_d, mult, hidden.reshape(tokens, hid),
    )

    def project(left):
        return lax.dot_general(left, w_gu, (((1,), (1,)), ((), ())), preferred_element_type=F32)

    back_away, y_z = lax.optimization_barrier((back_away, y_z))
    y_seq = scatter_direct([y_z[n] for n in range(RING)], "x")
    dx_away = project(back_away).astype(BF)
    dx_recv = swap(dx_away, "c")
    back_kept, dx_away = lax.optimization_barrier((back_kept, dx_away))
    dx_kept, dx_recv = lax.optimization_barrier((project(back_kept).astype(BF), dx_recv))
    dx_chip = add(dx_kept, dx_recv).reshape(chunks)
    dx_chip, y_seq = lax.optimization_barrier((dx_chip, y_seq))
    dx_parts = lax.all_to_all(dx_chip, ZX, 0, 0, tiled=True)
    dx_seq = jnp.sum(dx_parts.astype(F32), axis=0).astype(BF)

    summed = lax.psum_scatter(terms, "y", scatter_dimension=0, tiled=True)
    summed = summed.reshape(2, half, per_panel, edge, 2 * edge)
    other = swap(summed[1], "zh")
    low = jnp.where(zh == 0, summed[0], other)
    high = jnp.where(zh == 0, other, summed[0])
    grads = jnp.concatenate([low, high], axis=0)
    gu_grads = grads[:, :kept_here]
    d_gate_vals = gu_grads[..., :edge].reshape(panels, kept_here, square)
    d_up_vals = gu_grads[..., edge:].reshape(panels, kept_here, square)
    d_grads = grads[:, kept_here:].reshape(panels, pairs, edge, 2, edge)
    d_down_vals = jnp.transpose(d_grads, (0, 1, 3, 4, 2)).reshape(panels, kept_here, square)
    return (y_seq, dx_seq, d_gate_vals, d_up_vals, d_down_vals)


def solution(mesh):
    grid = Mesh(mesh.devices.reshape(4, 2, 4, 2, 2), AXES)
    row, col = ("y", "zh"), ("x", "zl", "c")
    tokens = P(row + col, None)
    vals = P(col, row, None)
    idx = P(col, None)
    return jax.shard_map(
        per_device,
        mesh=grid,
        in_specs=(tokens, tokens, vals, idx, vals, idx, vals, idx),
        out_specs=(tokens, tokens, vals, vals, vals),
        check_vma=False,
    )
```

```python
import jax
import jax.numpy as jnp
from jax import lax
from jax.experimental import pallas as pl
from jax.experimental.pallas import tpu as pltpu
from jax.sharding import Mesh, PartitionSpec as P

BLK = 64
AXES = ("y", "zh", "x", "zl", "c")
Z = ("zh", "zl")
ZX = ("zh", "zl", "x")
RING = 4
BF = jnp.bfloat16
F32 = jnp.float32
MIB = 1024 * 1024


def shift(value, axis, step):
    return lax.ppermute(value, axis, [(i, (i + step) % RING) for i in range(RING)])


def swap(value, axis):
    return lax.ppermute(value, axis, [(0, 1), (1, 0)])


def gather_direct(own, axis):
    below = shift(own, axis, 1)
    above = shift(own, axis, -1)
    across = shift(own, axis, 2)
    return [own, above, across, below]


def scatter_direct(chunks, axis):
    from_below = shift(chunks[1], axis, 1)
    from_above = shift(chunks[3], axis, -1)
    from_across = shift(chunks[2], axis, 2)
    total = chunks[0].astype(F32) + from_below.astype(F32)
    total = total + from_above.astype(F32) + from_across.astype(F32)
    return total.astype(BF)


def add(first, second):
    return (first.astype(F32) + second.astype(F32)).astype(BF)


def left_half(shape):
    return lax.broadcasted_iota(jnp.int32, shape, len(shape) - 1) % (2 * BLK) < BLK


def flip(value):
    return pltpu.roll(value, BLK, 1)


def kernel_params(limit):
    return pltpu.CompilerParams(
        dimension_semantics=("arbitrary",), vmem_limit_bytes=limit * MIB
    )


def row_copies(pieces, buf, sems):
    rows = pieces[0].shape[0]
    return [
        pltpu.make_async_copy(piece, buf.at[pl.ds(n * rows, rows)], sems.at[n])
        for n, piece in enumerate(pieces)
    ]


def z_copies(piece, buf, sems, place):
    rows = piece.shape[1]
    return [
        pltpu.make_async_copy(
            piece.at[(place[1] + n) % RING], buf.at[pl.ds(n * rows, rows)], sems.at[n]
        )
        for n in range(RING)
    ]


def owner_row(core, z, x):
    return core * RING * RING + z % RING * RING + x % RING


def chunk_copies(pieces, buf, sems, place):
    per = pieces[0].shape[1] // RING
    copies = []
    for core, piece in enumerate(pieces):
        for z in range(RING):
            for x in range(RING):
                at = owner_row(core, z, place[2] + x) * per
                copies.append(
                    pltpu.make_async_copy(
                        piece.at[z, pl.ds(x * per, per)],
                        buf.at[pl.ds(pl.multiple_of(at, per), per)],
                        sems.at[len(copies)],
                    )
                )
    return copies


def tile_wait(copies, i):
    for t in range(len(copies) // 2):

        @pl.when(i == t)
        def _(t=t):
            copies[2 * t].wait()
            copies[2 * t + 1].wait()


class Tiles:
    def __init__(self, half_panels, kept_here, zh):
        self.half_panels, self.kept_here, self.zh = half_panels, kept_here, zh
        self.pairs = kept_here // 2
        self.per_panel = kept_here + self.pairs

    def at(self, group, p, k):
        return (group * self.half_panels + p) * self.per_panel + k

    def kept(self, group, k):
        return (group // 2) * (2 * self.kept_here) + (self.zh ^ (group % 2)) * self.kept_here + k

    def row(self, idx_ref, p, j):
        return pl.multiple_of(idx_ref[self.zh * self.half_panels + p, j] * BLK, BLK)


def put_blocks(w_ref, places):
    mask = left_half((BLK, 2 * BLK))
    old = [w_ref[rows, lanes] for rows, lanes, _, _ in places]
    for before, (rows, lanes, tile, left) in zip(old, places):
        w_ref[rows, lanes] = jnp.where(mask, tile, before) if left else jnp.where(mask, before, tile)


def build_input_weights(where, gate_idx, up_idx, tiles, w_ref):
    w_ref[...] = jnp.zeros_like(w_ref)

    def put(step, carry):
        group, k = step // where.kept_here, step % where.kept_here
        j = where.kept(group, k)
        block = [tiles[where.at(group, p, k)] for p in range(where.half_panels)]
        for idx_ref, left in ((gate_idx, True), (up_idx, False)):
            put_blocks(w_ref, [
                (pl.ds(where.row(idx_ref, p, j), BLK), pl.ds(p * 2 * BLK, 2 * BLK), block[p], left)
                for p in range(where.half_panels)
            ])
        return carry

    lax.fori_loop(0, 2 * RING * where.kept_here, put, 0)


def build_down_weights(where, down_idx, tiles, w_ref):
    w_ref[...] = jnp.zeros_like(w_ref)

    def put(step, carry):
        group, m = step // where.pairs, step % where.pairs
        j = where.kept(group, 2 * m)
        for parity in range(2):
            places = []
            for p in range(parity, where.half_panels, 2):
                tile = tiles[where.at(group, p, where.kept_here + m)]
                for h in range(2):
                    rows = pl.ds(where.row(down_idx, p, j + h), BLK)
                    source = tile if h == parity else flip(tile)
                    places.append((rows, pl.ds((p // 2) * 128, 128), source, parity == 0))
            put_blocks(w_ref, places)
        return carry

    lax.fori_loop(0, 2 * RING * where.pairs, put, 0)


def back_rows(left, w_ref, out_ref, i):
    width = w_ref.shape[0]
    step = min(width, 1024)
    per = out_ref.shape[1]
    for start in range(0, width, step):
        part = lax.dot_general(
            left, w_ref[start : start + step, :], (((1,), (1,)), ((), ())),
            preferred_element_type=F32,
        ).astype(BF)
        for a in range(RING // 2):
            for b in range(RING):
                at = (a * RING + b) * per
                chunk = (i * (RING // 2) + a) * RING + b
                out_ref[chunk, :, start : start + step] = part[at : at + per]


def forward_tile(half_panels, x_tile, w_ref, m_ref, h_ref, h2_ref):
    rows = x_tile.shape[0]
    both = jnp.dot(x_tile, w_ref[...], preferred_element_type=F32)
    mask = left_half((rows, 2 * BLK))
    per = m_ref.shape[3]
    spans = [(a, b, (a * RING + b) * per) for a in range(RING // 2) for b in range(RING)]
    previous = None
    for p in range(half_panels):
        lanes = slice(p * 2 * BLK, (p + 1) * 2 * BLK)
        here = both[:, lanes]
        turned = flip(here)
        gate = jnp.where(mask, here, turned)
        up = jnp.where(mask, turned, here)
        sigma = jax.nn.sigmoid(gate)
        silu = gate * sigma
        mult = jnp.where(mask, up * sigma * (1.0 + gate * (1.0 - sigma)), silu)
        for a, b, at in spans:
            m_ref[0, a, b, :, lanes] = mult[at : at + per]
        hidden = silu * up
        if p % 2 == 0:
            previous = hidden
        if p % 2 == 1 or p == half_panels - 1:
            merged = jnp.where(mask, previous, hidden if p % 2 == 1 else 0.0).astype(BF)
            out = slice((p // 2) * 128, (p // 2 + 1) * 128)
            h_ref[:, out] = merged
            for a, b, at in spans:
                h2_ref[0, b, a, :, out] = merged[at : at + per]


def forward_kernel(half_panels, kept_here, first, place, *refs):
    if first:
        gate_idx, up_idx, down_idx, tiles = refs[:4]
        piece, refs = refs[4], refs[5:]
        m_ref, h2_ref, y_ref, w_other, wd_other = refs[:5]
    else:
        w_other, wd_other = refs[:2]
        piece, refs = refs[2], refs[5:]
        m_ref, h2_ref, y_ref = refs[:3]
    w_ref, wd_ref, h_ref, buf, sems, w_sems = refs[-6:]
    i = pl.program_id(0)
    rows = buf.shape[0] // 2
    copies = z_copies(piece, buf, sems, place)
    pairs = ((w_ref, w_other), (wd_ref, wd_other))
    if not first:
        pairs = [(b, a) for a, b in pairs]
    w_copies = [pltpu.make_async_copy(a, b, w_sems.at[n]) for n, (a, b) in enumerate(pairs)]

    @pl.when(i == 0)
    def _():
        if not first:
            for copy in w_copies:
                copy.start()
        for copy in copies:
            copy.start()
        if first:
            where = Tiles(half_panels, kept_here, place[0])
            build_input_weights(where, gate_idx, up_idx, tiles, w_ref)
            w_copies[0].start()
            build_down_weights(where, down_idx, tiles, wd_ref)
            w_copies[1].start()
        else:
            w_copies[0].wait()

    tile_wait(copies, i)
    x_tile = buf[pl.ds(pl.multiple_of(i * rows, rows), rows), :]
    forward_tile(half_panels, x_tile, w_ref, m_ref, h_ref, h2_ref)
    if not first:

        @pl.when(i == 0)
        def _():
            w_copies[1].wait()

    back_rows(h_ref[...], wd_ref, y_ref, i)
    if first:

        @pl.when(i == pl.num_programs(0) - 1)
        def _():
            for copy in w_copies:
                copy.wait()


def gradient_kernel(half_panels, kept_here, place, gate_idx, up_idx, down_idx, *refs):
    dy_pieces, x_pieces, refs = refs[:8], refs[8:10], refs[10:]
    wd_ref, m_ref, h_ref, w_gu, back_kept, dx_away, out_ref = refs[:7]
    dy_buf, x_buf, g_ref, acc, w_ref, dy_sems, x_sems, g_sems = refs[7:]
    i = pl.program_id(0)
    where = Tiles(half_panels, kept_here, place[0])
    rows = dy_buf.shape[0] // 4
    dy_copies = row_copies(dy_pieces, dy_buf, dy_sems)
    w_copy = pltpu.make_async_copy(w_gu, w_ref, g_sems.at[2])
    x_copies = chunk_copies(x_pieces, x_buf, x_sems, place)
    half_rows = back_kept.shape[0]
    g_copy = pltpu.make_async_copy(g_ref.at[pl.ds(0, half_rows)], back_kept, g_sems.at[0])
    dx_copy = pltpu.make_async_copy(dy_buf.at[pl.ds(0, half_rows)], dx_away, g_sems.at[1])
    hid = h_ref.shape[1]
    cols = dy_buf.shape[1] // 4
    mask = left_half((rows, 2 * BLK))
    small = left_half((BLK, 2 * BLK))

    @pl.when(i == 0)
    def _():
        for copy in dy_copies:
            copy.start()
        for copy in x_copies:
            copy.start()
        w_copy.start()

    tile_wait(dy_copies, i)

    @pl.when(i < 4)
    def _():
        dy_tile = dy_buf[pl.ds(pl.multiple_of(i * rows, rows), rows), :]
        d_hidden = jnp.dot(dy_tile, wd_ref[...], preferred_element_type=F32)
        per = m_ref.shape[3]
        for p in range(half_panels):
            if p % 2 == 0:
                here = d_hidden[:, (p // 2) * 128 : (p // 2 + 1) * 128]
                turned = flip(here)
                spread = jnp.where(mask, here, turned)
            else:
                spread = jnp.where(mask, turned, here)
            lanes = slice(p * 2 * BLK, (p + 1) * 2 * BLK)
            for a in range(RING // 2):
                for b in range(RING):
                    at = (a * RING + b) * per
                    chunk = owner_row(i // 2, place[1] + b, place[2] + (i % 2) * (RING // 2) + a)
                    rows_at = pl.ds(pl.multiple_of(chunk * per, per), per)
                    g_ref[rows_at, lanes] = (
                        spread[at : at + per] * m_ref[0, b, a, :, lanes]
                    ).astype(BF)

    @pl.when((i >= 4) & (i < 8))
    def _():
        at = pl.multiple_of((i - 4) * cols, cols)
        part = lax.dot_general(
            dy_buf[:, pl.ds(at, cols)], h_ref[...], (((0,), (0,)), ((), ())),
            preferred_element_type=F32,
        )
        acc[pl.ds(at, cols), :hid] = part.astype(BF)

    @pl.when(i == 4)
    def _():
        g_copy.start()

    @pl.when(i == 7)
    def _():
        def take(step, carry):
            group, m = step // where.pairs, step % where.pairs
            j = where.kept(group, 2 * m)
            for p in range(half_panels):
                lanes = pl.ds((p // 2) * 128, 128)
                first = acc[pl.ds(where.row(down_idx, p, j), BLK), lanes]
                second = acc[pl.ds(where.row(down_idx, p, j + 1), BLK), lanes]
                if p % 2 == 0:
                    second = flip(second)
                else:
                    first = flip(first)
                out_ref[where.at(group, p, kept_here + m)] = jnp.where(small, first, second)
            return carry

        lax.fori_loop(0, 2 * RING * where.pairs, take, 0)

    @pl.when(i == 8)
    def _():
        w_copy.wait()

    @pl.when((i >= 8) & (i < 12))
    def _():
        at = pl.multiple_of((i - 8) * cols, cols)
        part = lax.dot_general(
            g_ref[half_rows:, :], w_ref[pl.ds(at, cols), :], (((1,), (1,)), ((), ())),
            preferred_element_type=F32,
        )
        dy_buf[:half_rows, pl.ds(at, cols)] = part.astype(BF)

    @pl.when(i == 12)
    def _():
        dx_copy.start()
        for copy in x_copies:
            copy.wait()

    @pl.when(i >= 12)
    def _():
        at = pl.multiple_of((i - 12) * cols, cols)
        part = lax.dot_general(
            x_buf[:, pl.ds(at, cols)], g_ref[...], (((0,), (0,)), ((), ())),
            preferred_element_type=F32,
        )
        acc[pl.ds(at, cols), :] = part.astype(BF)

    @pl.when(i == pl.num_programs(0) - 1)
    def _():
        def take(step, carry):
            group, k = step // kept_here, step % kept_here
            j = where.kept(group, k)
            for p in range(half_panels):
                lanes = pl.ds(p * 2 * BLK, 2 * BLK)
                first = acc[pl.ds(where.row(gate_idx, p, j), BLK), lanes]
                second = acc[pl.ds(where.row(up_idx, p, j), BLK), lanes]
                out_ref[where.at(group, p, k)] = jnp.where(small, first, second)
            return carry

        lax.fori_loop(0, 2 * RING * kept_here, take, 0)
        g_copy.wait()
        dx_copy.wait()


def cost(flops, nbytes):
    return pl.CostEstimate(flops=flops // 8, bytes_accessed=nbytes // 8, transcendentals=0)


def per_device(x_seq, dy_seq, gate_vals, gate_idx, up_vals, up_idx, down_vals, down_idx):
    panels, kept_here, square = gate_vals.shape
    per, width = x_seq.shape
    edge = BLK
    half = panels // 2
    pairs = kept_here // 2
    per_panel = kept_here + pairs
    zh, z_place = lax.axis_index("zh"), lax.axis_index(Z)
    place = jnp.stack([zh, z_place, lax.axis_index("x")]).astype(jnp.int32)
    shape = jax.ShapeDtypeStruct

    def block_pairs(values):
        gate, up, down = (
            values[:, n * kept_here : (n + 1) * kept_here].reshape(half, kept_here, edge, edge)
            for n in range(3)
        )
        down = down.reshape(half, pairs, 2, edge, edge)
        down = jnp.transpose(down, (0, 1, 4, 2, 3)).reshape(half, pairs, edge, 2 * edge)
        return jnp.concatenate([jnp.concatenate([gate, up], axis=3), down], axis=1)

    def panel_half(which):
        return jnp.concatenate(
            [lax.dynamic_slice_in_dim(v, which * half, half, 0) for v in (gate_vals, up_vals, down_vals)],
            axis=1,
        )

    other = swap(panel_half(1 - zh), "zh")
    own = block_pairs(panel_half(zh))

    x_row = jnp.concatenate(gather_direct(x_seq, "x"), axis=0)
    other, x_row, own = lax.optimization_barrier((other, x_row, own))
    both = jnp.stack([own, block_pairs(other)]).reshape(-1, edge, 2 * edge)
    tiles = lax.all_gather(both, "y", axis=0, tiled=True)
    dy_seq, other = lax.optimization_barrier((dy_seq, other))
    wide = jnp.broadcast_to(x_row[None], (RING, *x_row.shape))
    x_own = lax.all_to_all(wide, Z, 0, 0, tiled=True)
    dy_row = jnp.concatenate(gather_direct(dy_seq, Z), axis=0)
    dy_own = gather_direct(dy_row, "x")
    x_own, dy_own = lax.optimization_barrier((x_own, dy_own))
    x_core = swap(x_own, "c")

    tokens = 2 * RING * RING * per
    rows = tokens // 4
    hid = -(-half * edge // 128) * 128
    two = half * 2 * edge
    pair = RING // 2
    once = pl.Buffered(1)
    full = lambda *dims: pl.BlockSpec(dims, lambda i: (0,) * len(dims), pipeline_mode=once)
    out_full = lambda *dims: pl.BlockSpec(dims, lambda i: (0,) * len(dims))
    smem = pl.BlockSpec(memory_space=pltpu.SMEM)
    hbm = pl.BlockSpec(memory_space=pl.ANY)
    ordered = lambda last: (2, RING, RING, per, last)
    gu_flops = 2 * tokens * width * two
    d_flops = 2 * tokens * width * hid
    chunks = (RING * RING, per, width)

    def part(fn, *extra):
        def body(*refs):
            fn(*extra, *refs)

        return body

    def forward(core, first, inputs, name):
        specs = [smem] * 4 + [full(*tiles.shape), hbm] if first else [smem] + [hbm] * 5
        extra_out = [shape((width, two), BF), shape((width, hid), BF)] if first else []
        return pl.pallas_call(
            part(forward_kernel, half, kept_here, first),
            grid=(2,),
            in_specs=specs,
            out_specs=[
                pl.BlockSpec((1, pair, RING, per, two), lambda i: (core, i, 0, 0, 0)),
                pl.BlockSpec((1, RING, pair, per, hid), lambda i: (core, 0, i, 0, 0)),
                out_full(*chunks),
            ] + [hbm] * len(extra_out),
            out_shape=[shape(ordered(two), F32), shape(ordered(hid), BF), shape(chunks, BF)] + extra_out,
            scratch_shapes=[
                pltpu.VMEM((width, two), BF),
                pltpu.VMEM((width, hid), BF),
                pltpu.VMEM((rows, hid), BF),
                pltpu.VMEM((tokens // 2, width), BF),
                pltpu.SemaphoreType.DMA((4,)),
                pltpu.SemaphoreType.DMA((2,)),
            ],
            input_output_aliases={} if first else {4: 0, 5: 1},
            compiler_params=kernel_params(56),
            cost_estimate=cost((gu_flops + d_flops) // 2, 24 * MIB),
            name=name,
        )(place, *inputs)

    mult, hidden, y_away, w_gu, w_d = forward(
        1, True, (gate_idx, up_idx, down_idx, tiles, x_core), "forward_away"
    )
    dy_core = [swap(v, "c") for v in dy_own]
    y_recv = swap(y_away, "c")
    mult, hidden, y_kept = forward(0, False, (w_gu, w_d, x_own, mult, hidden), "forward_kept")
    y_kept, dy_core = lax.optimization_barrier((y_kept, dy_core))
    y_sum = [add(y_kept[n * RING : n * RING + RING], y_recv[n * RING : n * RING + RING]) for n in range(RING)]
    mult, y_sum = lax.optimization_barrier((mult, y_sum))
    y_z = scatter_direct(y_sum, Z)

    steps = 16
    x_tile = lambda i: jnp.minimum(i, 3)
    back_kept, dx_away, terms = pl.pallas_call(
        part(gradient_kernel, half, kept_here),
        grid=(steps,),
        in_specs=[smem] * 4
        + [hbm] * 10
        + [
            full(width, hid),
            pl.BlockSpec(
                (1, RING, pair, per, two), lambda i: (x_tile(i) // 2, 0, x_tile(i) % 2, 0, 0)
            ),
            full(tokens, hid),
            hbm,
        ],
        out_specs=[hbm, hbm, out_full(*tiles.shape)],
        out_shape=[
            shape((tokens // 2, two), BF),
            shape((tokens // 2, width), BF),
            shape(tiles.shape, BF),
        ],
        scratch_shapes=[
            pltpu.VMEM((tokens, width), BF),
            pltpu.VMEM((tokens, width), BF),
            pltpu.VMEM((tokens, two), BF),
            pltpu.VMEM((width, two), BF),
            pltpu.VMEM((width, two), BF),
            pltpu.SemaphoreType.DMA((8,)),
            pltpu.SemaphoreType.DMA((32,)),
            pltpu.SemaphoreType.DMA((3,)),
        ],
        compiler_params=kernel_params(60),
        cost_estimate=cost(gu_flops + 2 * d_flops, 40 * MIB),
        name="gradients",
    )(
        place, gate_idx, up_idx, down_idx, *dy_own, *dy_core, x_own, x_core,
        w_d, mult, hidden.reshape(tokens, hid), w_gu,
    )

    def project(left):
        return lax.dot_general(left, w_gu, (((1,), (1,)), ((), ())), preferred_element_type=F32)

    back_kept, dx_away, terms, y_z = lax.optimization_barrier((back_kept, dx_away, terms, y_z))
    dx_recv = swap(dx_away, "c")
    dx_kept, dx_recv = lax.optimization_barrier((project(back_kept).astype(BF), dx_recv))
    dx_chip = add(dx_kept, dx_recv).reshape(chunks)
    y_z, dx_chip = lax.optimization_barrier((y_z, dx_chip))
    dx_parts = lax.all_to_all(dx_chip, ZX, 0, 0, tiled=True)
    y_seq = scatter_direct([y_z[n] for n in range(RING)], "x")
    summed = lax.psum_scatter(terms, "y", scatter_dimension=0, tiled=True)
    summed = summed.reshape(2, half, per_panel, edge, 2 * edge)
    other = swap(summed[1], "zh")
    low = jnp.where(zh == 0, summed[0], other)
    high = jnp.where(zh == 0, other, summed[0])
    grads = jnp.concatenate([low, high], axis=0)
    gu_grads = grads[:, :kept_here]
    d_gate_vals = gu_grads[..., :edge].reshape(panels, kept_here, square)
    d_up_vals = gu_grads[..., edge:].reshape(panels, kept_here, square)
    d_grads = grads[:, kept_here:].reshape(panels, pairs, edge, 2, edge)
    d_down_vals = jnp.transpose(d_grads, (0, 1, 3, 4, 2)).reshape(panels, kept_here, square)
    dx_parts, d_gate_vals, d_up_vals, d_down_vals, y_seq = lax.optimization_barrier(
        (dx_parts, d_gate_vals, d_up_vals, d_down_vals, y_seq)
    )
    dx_seq = jnp.sum(dx_parts.astype(F32), axis=0).astype(BF)
    return (y_seq, dx_seq, d_gate_vals, d_up_vals, d_down_vals)


def solution(mesh):
    grid = Mesh(mesh.devices.reshape(4, 2, 4, 2, 2), AXES)
    row, col = ("y", "zh"), ("x", "zl", "c")
    tokens = P(row + col, None)
    vals = P(col, row, None)
    idx = P(col, None)
    return jax.shard_map(
        per_device,
        mesh=grid,
        in_specs=(tokens, tokens, vals, idx, vals, idx, vals, idx),
        out_specs=(tokens, tokens, vals, vals, vals),
        check_vma=False,
    )
```

```python
import jax
import jax.numpy as jnp
from jax import lax
from jax.experimental import pallas as pl
from jax.experimental.pallas import tpu as pltpu
from jax.sharding import Mesh, PartitionSpec as P

BLK = 64
AXES = ("y", "zh", "x", "zl", "c")
Z = ("zh", "zl")
ZX = ("zh", "zl", "x")
RING = 4
BF = jnp.bfloat16
F32 = jnp.float32
MIB = 1024 * 1024


def shift(value, axis, step):
    return lax.ppermute(value, axis, [(i, (i + step) % RING) for i in range(RING)])


def swap(value, axis):
    return lax.ppermute(value, axis, [(0, 1), (1, 0)])


def gather_direct(own, axis):
    below = shift(own, axis, 1)
    above = shift(own, axis, -1)
    across = shift(own, axis, 2)
    return [own, above, across, below]


def scatter_direct(chunks, axis):
    from_below = shift(chunks[1], axis, 1)
    from_above = shift(chunks[3], axis, -1)
    from_across = shift(chunks[2], axis, 2)
    total = chunks[0].astype(F32) + from_below.astype(F32)
    total = total + from_above.astype(F32) + from_across.astype(F32)
    return total.astype(BF)


def add(first, second):
    return (first.astype(F32) + second.astype(F32)).astype(BF)


def left_half(shape):
    return lax.broadcasted_iota(jnp.int32, shape, len(shape) - 1) % (2 * BLK) < BLK


def flip(value):
    return pltpu.roll(value, BLK, 1)


def kernel_params(limit):
    return pltpu.CompilerParams(
        dimension_semantics=("arbitrary",), vmem_limit_bytes=limit * MIB
    )


def row_copies(pieces, buf, sems):
    rows = pieces[0].shape[0]
    return [
        pltpu.make_async_copy(piece, buf.at[pl.ds(n * rows, rows)], sems.at[n])
        for n, piece in enumerate(pieces)
    ]


def owner_row(core, z, x):
    return core * RING * RING + z * RING + x % RING


def chunk_copies(pieces, buf, sems, place):
    per = pieces[0].shape[0] // RING
    copies = []
    for n, piece in enumerate(pieces):
        for x in range(RING):
            at = owner_row(n // RING, n % RING, place[2] + x) * per
            copies.append(
                pltpu.make_async_copy(
                    piece.at[pl.ds(x * per, per)],
                    buf.at[pl.ds(pl.multiple_of(at, per), per)],
                    sems.at[n * RING + x],
                )
            )
    return copies


def ring_copies(pieces, buf, sems, place):
    per = pieces[0].shape[2]
    copies = []
    for n in range(2 * RING * RING):
        core, x, z = n // (RING * RING), n // RING % RING, n % RING
        source = pieces[core].at[(place[2] + x) % RING, (place[1] + z) % RING]
        copies.append(pltpu.make_async_copy(source, buf.at[pl.ds(n * per, per)], sems.at[n]))
    return copies


def tile_wait(copies, i):
    for t in range(len(copies) // 2):

        @pl.when(i == t)
        def _(t=t):
            copies[2 * t].wait()
            copies[2 * t + 1].wait()


class Tiles:
    def __init__(self, half_panels, kept_here, zh):
        self.half_panels, self.kept_here, self.zh = half_panels, kept_here, zh
        self.pairs = kept_here // 2
        self.per_panel = kept_here + self.pairs

    def at(self, group, p, k):
        return (group * self.half_panels + p) * self.per_panel + k

    def kept(self, group, k):
        return (group // 2) * (2 * self.kept_here) + (self.zh ^ (group % 2)) * self.kept_here + k

    def row(self, idx_ref, p, j):
        return pl.multiple_of(idx_ref[self.zh * self.half_panels + p, j] * BLK, BLK)


def put_blocks(w_ref, places):
    mask = left_half((BLK, 2 * BLK))
    old = [w_ref[rows, lanes] for rows, lanes, _, _ in places]
    for before, (rows, lanes, tile, left) in zip(old, places):
        w_ref[rows, lanes] = jnp.where(mask, tile, before) if left else jnp.where(mask, before, tile)


def build_input_weights(where, gate_idx, up_idx, tiles, w_ref):
    w_ref[...] = jnp.zeros_like(w_ref)

    def put(step, carry):
        group, k = step // where.kept_here, step % where.kept_here
        j = where.kept(group, k)
        block = [tiles[where.at(group, p, k)] for p in range(where.half_panels)]
        for idx_ref, left in ((gate_idx, True), (up_idx, False)):
            put_blocks(w_ref, [
                (pl.ds(where.row(idx_ref, p, j), BLK), pl.ds(p * 2 * BLK, 2 * BLK), block[p], left)
                for p in range(where.half_panels)
            ])
        return carry

    lax.fori_loop(0, 2 * RING * where.kept_here, put, 0)


def build_down_weights(where, down_idx, tiles, w_ref):
    w_ref[...] = jnp.zeros_like(w_ref)

    def put(step, carry):
        group, m = step // where.pairs, step % where.pairs
        j = where.kept(group, 2 * m)
        for parity in range(2):
            places = []
            for p in range(parity, where.half_panels, 2):
                tile = tiles[where.at(group, p, where.kept_here + m)]
                for h in range(2):
                    rows = pl.ds(where.row(down_idx, p, j + h), BLK)
                    source = tile if h == parity else flip(tile)
                    places.append((rows, pl.ds((p // 2) * 128, 128), source, parity == 0))
            put_blocks(w_ref, places)
        return carry

    lax.fori_loop(0, 2 * RING * where.pairs, put, 0)


def back_rows(left, w_ref, out_ref, i):
    width = w_ref.shape[0]
    step = min(width, 1024)
    per = out_ref.shape[1]
    for start in range(0, width, step):
        part = lax.dot_general(
            left, w_ref[start : start + step, :], (((1,), (1,)), ((), ())),
            preferred_element_type=F32,
        ).astype(BF)
        for a in range(RING // 2):
            for b in range(RING):
                at = (a * RING + b) * per
                chunk = (i * (RING // 2) + a) * RING + b
                out_ref[chunk, :, start : start + step] = part[at : at + per]


def forward_tile(half_panels, x_tile, w_ref, m_ref, h_ref, h2_ref):
    rows = x_tile.shape[0]
    both = jnp.dot(x_tile, w_ref[...], preferred_element_type=F32)
    mask = left_half((rows, 2 * BLK))
    per = m_ref.shape[3]
    spans = [(a, b, (a * RING + b) * per) for a in range(RING // 2) for b in range(RING)]
    previous = None
    for p in range(half_panels):
        lanes = slice(p * 2 * BLK, (p + 1) * 2 * BLK)
        here = both[:, lanes]
        turned = flip(here)
        gate = jnp.where(mask, here, turned)
        up = jnp.where(mask, turned, here)
        sigma = jax.nn.sigmoid(gate)
        silu = gate * sigma
        mult = jnp.where(mask, up * sigma * (1.0 + gate * (1.0 - sigma)), silu)
        for a, b, at in spans:
            m_ref[0, a, b, :, lanes] = mult[at : at + per]
        hidden = silu * up
        if p % 2 == 0:
            previous = hidden
        if p % 2 == 1 or p == half_panels - 1:
            merged = jnp.where(mask, previous, hidden if p % 2 == 1 else 0.0).astype(BF)
            out = slice((p // 2) * 128, (p // 2 + 1) * 128)
            h_ref[:, out] = merged
            for a, b, at in spans:
                h2_ref[0, b, a, :, out] = merged[at : at + per]


def forward_kernel(half_panels, kept_here, first, place, *refs):
    if first:
        gate_idx, up_idx, down_idx, tiles = refs[:4]
        pieces, refs = refs[4:8], refs[8:]
        m_ref, h2_ref, y_ref, w_other, wd_other = refs[:5]
    else:
        w_other, wd_other = refs[:2]
        pieces, refs = refs[2:6], refs[8:]
        m_ref, h2_ref, y_ref = refs[:3]
    w_ref, wd_ref, h_ref, buf, sems, w_sems = refs[-6:]
    i = pl.program_id(0)
    rows = buf.shape[0] // 2
    copies = row_copies(pieces, buf, sems)
    pairs = ((w_ref, w_other), (wd_ref, wd_other))
    if not first:
        pairs = [(b, a) for a, b in pairs]
    w_copies = [pltpu.make_async_copy(a, b, w_sems.at[n]) for n, (a, b) in enumerate(pairs)]

    @pl.when(i == 0)
    def _():
        if not first:
            w_copies[0].start()
        for copy in copies:
            copy.start()
        if not first:
            w_copies[1].start()
        if first:
            where = Tiles(half_panels, kept_here, place[0])
            build_input_weights(where, gate_idx, up_idx, tiles, w_ref)
            w_copies[0].start()
            build_down_weights(where, down_idx, tiles, wd_ref)
            w_copies[1].start()
        else:
            w_copies[0].wait()

    tile_wait(copies, i)
    x_tile = buf[pl.ds(pl.multiple_of(i * rows, rows), rows), :]
    forward_tile(half_panels, x_tile, w_ref, m_ref, h_ref, h2_ref)
    if not first:

        @pl.when(i == 0)
        def _():
            w_copies[1].wait()

    back_rows(h_ref[...], wd_ref, y_ref, i)
    if first:

        @pl.when(i == pl.num_programs(0) - 1)
        def _():
            for copy in w_copies:
                copy.wait()


def gradient_kernel(half_panels, kept_here, place, gate_idx, up_idx, down_idx, *refs):
    dy_pieces, x_pieces, refs = refs[:2], refs[2:10], refs[10:]
    wd_ref, m_ref, h_ref, w_gu, back_kept, dx_away, out_ref = refs[:7]
    dy_buf, x_buf, g_ref, acc, w_ref, dy_sems, x_sems, g_sems = refs[7:]
    i = pl.program_id(0)
    where = Tiles(half_panels, kept_here, place[0])
    rows = dy_buf.shape[0] // 4
    dy_copies = ring_copies(dy_pieces, dy_buf, dy_sems, place)
    x_copies = chunk_copies(x_pieces, x_buf, x_sems, place)
    w_copy = pltpu.make_async_copy(w_gu, w_ref, g_sems.at[2])
    half_rows = back_kept.shape[0]
    g_copy = pltpu.make_async_copy(g_ref.at[pl.ds(0, half_rows)], back_kept, g_sems.at[0])
    dx_copy = pltpu.make_async_copy(dy_buf.at[pl.ds(0, half_rows)], dx_away, g_sems.at[1])
    hid = h_ref.shape[1]
    cols = dy_buf.shape[1] // 4
    mask = left_half((rows, 2 * BLK))
    small = left_half((BLK, 2 * BLK))

    @pl.when(i == 0)
    def _():
        for copy in dy_copies:
            copy.start()

    for t in range(4):

        @pl.when(i == t)
        def _(t=t):
            for copy in dy_copies[8 * t : 8 * t + 8]:
                copy.wait()

    @pl.when(i < 4)
    def _():
        dy_tile = dy_buf[pl.ds(pl.multiple_of(i * rows, rows), rows), :]
        d_hidden = jnp.dot(dy_tile, wd_ref[...], preferred_element_type=F32)
        per = m_ref.shape[3]
        for p in range(half_panels):
            if p % 2 == 0:
                here = d_hidden[:, (p // 2) * 128 : (p // 2 + 1) * 128]
                turned = flip(here)
                spread = jnp.where(mask, here, turned)
            else:
                spread = jnp.where(mask, turned, here)
            lanes = slice(p * 2 * BLK, (p + 1) * 2 * BLK)
            for a in range(RING // 2):
                for b in range(RING):
                    at = (a * RING + b) * per
                    chunk = owner_row(i // 2, b, place[2] + (i % 2) * (RING // 2) + a)
                    rows_at = pl.ds(pl.multiple_of(chunk * per, per), per)
                    g_ref[rows_at, lanes] = (
                        spread[at : at + per] * m_ref[0, b, a, :, lanes]
                    ).astype(BF)

    @pl.when((i >= 4) & (i < 8))
    def _():
        at = pl.multiple_of((i - 4) * cols, cols)
        part = lax.dot_general(
            dy_buf[:, pl.ds(at, cols)], h_ref[...], (((0,), (0,)), ((), ())),
            preferred_element_type=F32,
        )
        acc[pl.ds(at, cols), :hid] = part.astype(BF)

    @pl.when(i == 3)
    def _():
        w_copy.start()
        for copy in x_copies:
            copy.start()

    @pl.when(i == 4)
    def _():
        g_copy.start()

    @pl.when(i == 7)
    def _():
        def take(step, carry):
            group, m = step // where.pairs, step % where.pairs
            j = where.kept(group, 2 * m)
            for p in range(half_panels):
                lanes = pl.ds((p // 2) * 128, 128)
                first = acc[pl.ds(where.row(down_idx, p, j), BLK), lanes]
                second = acc[pl.ds(where.row(down_idx, p, j + 1), BLK), lanes]
                if p % 2 == 0:
                    second = flip(second)
                else:
                    first = flip(first)
                out_ref[where.at(group, p, kept_here + m)] = jnp.where(small, first, second)
            return carry

        lax.fori_loop(0, 2 * RING * where.pairs, take, 0)

    @pl.when(i == 8)
    def _():
        w_copy.wait()

    @pl.when((i >= 8) & (i < 12))
    def _():
        at = pl.multiple_of((i - 8) * cols, cols)
        part = lax.dot_general(
            g_ref[half_rows:, :], w_ref[pl.ds(at, cols), :], (((1,), (1,)), ((), ())),
            preferred_element_type=F32,
        )
        dy_buf[:half_rows, pl.ds(at, cols)] = part.astype(BF)

    @pl.when(i == 12)
    def _():
        dx_copy.start()
        for copy in x_copies:
            copy.wait()

    @pl.when(i >= 12)
    def _():
        at = pl.multiple_of((i - 12) * cols, cols)
        part = lax.dot_general(
            x_buf[:, pl.ds(at, cols)], g_ref[...], (((0,), (0,)), ((), ())),
            preferred_element_type=F32,
        )
        acc[pl.ds(at, cols), :] = part.astype(BF)

    @pl.when(i == pl.num_programs(0) - 1)
    def _():
        def take(step, carry):
            group, k = step // kept_here, step % kept_here
            j = where.kept(group, k)
            for p in range(half_panels):
                lanes = pl.ds(p * 2 * BLK, 2 * BLK)
                first = acc[pl.ds(where.row(gate_idx, p, j), BLK), lanes]
                second = acc[pl.ds(where.row(up_idx, p, j), BLK), lanes]
                out_ref[where.at(group, p, k)] = jnp.where(small, first, second)
            return carry

        lax.fori_loop(0, 2 * RING * kept_here, take, 0)
        g_copy.wait()
        dx_copy.wait()


def cost(flops, nbytes):
    return pl.CostEstimate(flops=flops // 8, bytes_accessed=nbytes // 8, transcendentals=0)


def per_device(x_seq, dy_seq, gate_vals, gate_idx, up_vals, up_idx, down_vals, down_idx):
    panels, kept_here, square = gate_vals.shape
    per, width = x_seq.shape
    edge = BLK
    half = panels // 2
    pairs = kept_here // 2
    per_panel = kept_here + pairs
    zh, z_place = lax.axis_index("zh"), lax.axis_index(Z)
    place = jnp.stack([zh, z_place, lax.axis_index("x")]).astype(jnp.int32)
    shape = jax.ShapeDtypeStruct

    gate_blk = gate_vals.reshape(panels, kept_here, edge, edge)
    up_blk = up_vals.reshape(panels, kept_here, edge, edge)
    pair_gu = jnp.concatenate([gate_blk, up_blk], axis=3)
    down_blk = down_vals.reshape(panels, pairs, 2, edge, edge)
    pair_d = jnp.transpose(down_blk, (0, 1, 4, 2, 3)).reshape(panels, pairs, edge, 2 * edge)
    all_pairs = jnp.concatenate([pair_gu, pair_d], axis=1)
    own = lax.dynamic_slice_in_dim(all_pairs, zh * half, half, 0)
    other = swap(lax.dynamic_slice_in_dim(all_pairs, (1 - zh) * half, half, 0), "zh")

    def gather_all(value, axis):
        wide = jnp.broadcast_to(value[None], (RING, *value.shape))
        return lax.all_to_all(wide, axis, 0, 0, tiled=True)

    dy_row = gather_all(dy_seq, Z)
    x_row = jnp.concatenate(gather_direct(x_seq, "x"), axis=0)
    other, x_row, dy_row = lax.optimization_barrier((other, x_row, dy_row))
    both = jnp.stack([own, other]).reshape(-1, edge, 2 * edge)
    tiles = lax.all_gather(both, "y", axis=0, tiled=True)
    dy_own = gather_all(dy_row, "x")
    x_own = gather_direct(x_row, Z)
    x_core = [swap(v, "c") for v in x_own]
    x_core, dy_own = lax.optimization_barrier((x_core, dy_own))
    dy_core = swap(dy_own, "c")

    tokens = 2 * RING * RING * per
    rows = tokens // 4
    hid = -(-half * edge // 128) * 128
    two = half * 2 * edge
    pair = RING // 2
    once = pl.Buffered(1)
    full = lambda *dims: pl.BlockSpec(dims, lambda i: (0,) * len(dims), pipeline_mode=once)
    out_full = lambda *dims: pl.BlockSpec(dims, lambda i: (0,) * len(dims))
    smem = pl.BlockSpec(memory_space=pltpu.SMEM)
    hbm = pl.BlockSpec(memory_space=pl.ANY)
    ordered = lambda last: (2, RING, RING, per, last)
    gu_flops = 2 * tokens * width * two
    d_flops = 2 * tokens * width * hid
    chunks = (RING * RING, per, width)

    def part(fn, *extra):
        def body(*refs):
            fn(*extra, *refs)

        return body

    def forward(core, first, inputs, name):
        specs = [smem] * 4 + [full(*tiles.shape)] + [hbm] * 4 if first else [smem] + [hbm] * 8
        extra_out = [shape((width, two), BF), shape((width, hid), BF)] if first else []
        return pl.pallas_call(
            part(forward_kernel, half, kept_here, first),
            grid=(2,),
            in_specs=specs,
            out_specs=[
                pl.BlockSpec((1, pair, RING, per, two), lambda i: (core, i, 0, 0, 0)),
                pl.BlockSpec((1, RING, pair, per, hid), lambda i: (core, 0, i, 0, 0)),
                out_full(*chunks),
            ] + [hbm] * len(extra_out),
            out_shape=[shape(ordered(two), F32), shape(ordered(hid), BF), shape(chunks, BF)] + extra_out,
            scratch_shapes=[
                pltpu.VMEM((width, two), BF),
                pltpu.VMEM((width, hid), BF),
                pltpu.VMEM((rows, hid), BF),
                pltpu.VMEM((tokens // 2, width), BF),
                pltpu.SemaphoreType.DMA((4,)),
                pltpu.SemaphoreType.DMA((2,)),
            ],
            input_output_aliases={} if first else {7: 0, 8: 1},
            compiler_params=kernel_params(56),
            cost_estimate=cost((gu_flops + d_flops) // 2, 24 * MIB),
            name=name,
        )(place, *inputs)

    mult, hidden, y_away, w_gu, w_d = forward(
        1, True, (gate_idx, up_idx, down_idx, tiles, *x_core), "forward_away"
    )
    y_recv = swap(y_away, "c")
    mult, hidden, y_kept = forward(0, False, (w_gu, w_d, *x_own, mult, hidden), "forward_kept")
    y_kept, dy_core = lax.optimization_barrier((y_kept, dy_core))
    dy_pieces = [v.reshape(RING, RING, per, width) for v in (dy_own, dy_core)]
    y_sum = [add(y_kept[n * RING : n * RING + RING], y_recv[n * RING : n * RING + RING]) for n in range(RING)]
    mult, y_sum = lax.optimization_barrier((mult, y_sum))
    y_z = scatter_direct(y_sum, Z)

    steps = 16
    x_tile = lambda i: jnp.minimum(i, 3)
    back_kept, dx_away, terms = pl.pallas_call(
        part(gradient_kernel, half, kept_here),
        grid=(steps,),
        in_specs=[smem] * 4
        + [hbm] * 10
        + [
            full(width, hid),
            pl.BlockSpec(
                (1, RING, pair, per, two), lambda i: (x_tile(i) // 2, 0, x_tile(i) % 2, 0, 0)
            ),
            full(tokens, hid),
            hbm,
        ],
        out_specs=[hbm, hbm, out_full(*tiles.shape)],
        out_shape=[
            shape((tokens // 2, two), BF),
            shape((tokens // 2, width), BF),
            shape(tiles.shape, BF),
        ],
        scratch_shapes=[
            pltpu.VMEM((tokens, width), BF),
            pltpu.VMEM((tokens, width), BF),
            pltpu.VMEM((tokens, two), BF),
            pltpu.VMEM((width, two), BF),
            pltpu.VMEM((width, two), BF),
            pltpu.SemaphoreType.DMA((32,)),
            pltpu.SemaphoreType.DMA((32,)),
            pltpu.SemaphoreType.DMA((3,)),
        ],
        compiler_params=kernel_params(60),
        cost_estimate=cost(gu_flops + 2 * d_flops, 40 * MIB),
        name="gradients",
    )(
        place, gate_idx, up_idx, down_idx, *dy_pieces, *x_own, *x_core,
        w_d, mult, hidden.reshape(tokens, hid), w_gu,
    )

    def project(left):
        return lax.dot_general(left, w_gu, (((1,), (1,)), ((), ())), preferred_element_type=F32)

    back_kept, dx_away, terms, y_z = lax.optimization_barrier((back_kept, dx_away, terms, y_z))
    dx_recv = swap(dx_away, "c")
    dx_kept, dx_recv = lax.optimization_barrier((project(back_kept).astype(BF), dx_recv))

    def chip_rows(first, count):
        split = lambda v: v[:, first : first + count].reshape(RING, RING, per, count)
        return add(split(dx_kept), split(dx_recv))

    def over_x(value):
        return jnp.sum(lax.all_to_all(value, "x", 0, 0, tiled=True).astype(F32), axis=0).astype(BF)

    x_first = jnp.transpose(chip_rows(0, width // 2), (1, 0, 2, 3))
    z_first = chip_rows(width // 2, width // 2)
    y_z, x_first, z_first = lax.optimization_barrier((y_z, x_first, z_first))
    x_first = over_x(x_first)
    z_first = scatter_direct([z_first[n] for n in range(RING)], Z)
    y_seq = scatter_direct([y_z[n] for n in range(RING)], "x")
    x_first, z_first, y_seq = lax.optimization_barrier((x_first, z_first, y_seq))
    x_first = scatter_direct([x_first[n] for n in range(RING)], Z)
    z_first = over_x(z_first)
    dx_seq = jnp.concatenate([x_first, z_first], axis=1)

    summed = lax.psum_scatter(terms, "y", scatter_dimension=0, tiled=True)
    summed = summed.reshape(2, half, per_panel, edge, 2 * edge)
    other = swap(summed[1], "zh")
    low = jnp.where(zh == 0, summed[0], other)
    high = jnp.where(zh == 0, other, summed[0])
    grads = jnp.concatenate([low, high], axis=0)
    gu_grads = grads[:, :kept_here]
    d_gate_vals = gu_grads[..., :edge].reshape(panels, kept_here, square)
    d_up_vals = gu_grads[..., edge:].reshape(panels, kept_here, square)
    d_grads = grads[:, kept_here:].reshape(panels, pairs, edge, 2, edge)
    d_down_vals = jnp.transpose(d_grads, (0, 1, 3, 4, 2)).reshape(panels, kept_here, square)
    return (y_seq, dx_seq, d_gate_vals, d_up_vals, d_down_vals)


def solution(mesh):
    grid = Mesh(mesh.devices.reshape(4, 2, 4, 2, 2), AXES)
    row, col = ("y", "zh"), ("x", "zl", "c")
    tokens = P(row + col, None)
    vals = P(col, row, None)
    idx = P(col, None)
    return jax.shard_map(
        per_device,
        mesh=grid,
        in_specs=(tokens, tokens, vals, idx, vals, idx, vals, idx),
        out_specs=(tokens, tokens, vals, vals, vals),
        check_vma=False,
    )
```

```python
import jax
import jax.numpy as jnp
from jax import lax
from jax.experimental import pallas as pl
from jax.experimental.pallas import tpu as pltpu
from jax.sharding import Mesh, PartitionSpec as P

BLK = 64
AXES = ("y", "zh", "x", "zl", "c")
Z = ("zh", "zl")
ZX = ("zh", "zl", "x")
RING = 4
BF = jnp.bfloat16
F32 = jnp.float32
MIB = 1024 * 1024


def shift(value, axis, step):
    return lax.ppermute(value, axis, [(i, (i + step) % RING) for i in range(RING)])


def swap(value, axis):
    return lax.ppermute(value, axis, [(0, 1), (1, 0)])


def gather_direct(own, axis):
    below = shift(own, axis, 1)
    above = shift(own, axis, -1)
    across = shift(own, axis, 2)
    return [own, above, across, below]


def scatter_direct(chunks, axis):
    from_below = shift(chunks[1], axis, 1)
    from_above = shift(chunks[3], axis, -1)
    from_across = shift(chunks[2], axis, 2)
    total = chunks[0].astype(F32) + from_below.astype(F32)
    total = total + from_above.astype(F32) + from_across.astype(F32)
    return total.astype(BF)


def add(first, second):
    return (first.astype(F32) + second.astype(F32)).astype(BF)


def left_half(shape):
    return lax.broadcasted_iota(jnp.int32, shape, len(shape) - 1) % (2 * BLK) < BLK


def flip(value):
    return pltpu.roll(value, BLK, 1)


def kernel_params(limit):
    return pltpu.CompilerParams(
        dimension_semantics=("arbitrary",), vmem_limit_bytes=limit * MIB
    )


def row_copies(pieces, buf, sems):
    rows = pieces[0].shape[0]
    return [
        pltpu.make_async_copy(piece, buf.at[pl.ds(n * rows, rows)], sems.at[n])
        for n, piece in enumerate(pieces)
    ]


def owner_row(core, z, x):
    return core * RING * RING + z * RING + x % RING


def chunk_copies(pieces, buf, sems, place):
    per = pieces[0].shape[0] // RING
    copies = []
    for n, piece in enumerate(pieces):
        for x in range(RING):
            at = owner_row(n // RING, n % RING, place[2] + x) * per
            copies.append(
                pltpu.make_async_copy(
                    piece.at[pl.ds(x * per, per)],
                    buf.at[pl.ds(pl.multiple_of(at, per), per)],
                    sems.at[n * RING + x],
                )
            )
    return copies


def ring_copies(pieces, buf, sems, place):
    per = pieces[0].shape[2]
    copies = []
    for n in range(2 * RING * RING):
        core, x, z = n // (RING * RING), n // RING % RING, n % RING
        source = pieces[core].at[(place[2] + x) % RING, (place[1] + z) % RING]
        copies.append(pltpu.make_async_copy(source, buf.at[pl.ds(n * per, per)], sems.at[n]))
    return copies


def tile_wait(copies, i):
    for t in range(len(copies) // 2):

        @pl.when(i == t)
        def _(t=t):
            copies[2 * t].wait()
            copies[2 * t + 1].wait()


class Tiles:
    def __init__(self, half_panels, kept_here, zh):
        self.half_panels, self.kept_here, self.zh = half_panels, kept_here, zh
        self.pairs = kept_here // 2
        self.per_panel = kept_here + self.pairs

    def at(self, group, p, k):
        return (group * self.half_panels + p) * self.per_panel + k

    def kept(self, group, k):
        return (group // 2) * (2 * self.kept_here) + (self.zh ^ (group % 2)) * self.kept_here + k

    def row(self, idx_ref, p, j):
        return pl.multiple_of(idx_ref[self.zh * self.half_panels + p, j] * BLK, BLK)


def put_blocks(w_ref, places):
    mask = left_half((BLK, 2 * BLK))
    old = [w_ref[rows, lanes] for rows, lanes, _, _ in places]
    for before, (rows, lanes, tile, left) in zip(old, places):
        w_ref[rows, lanes] = jnp.where(mask, tile, before) if left else jnp.where(mask, before, tile)


def build_input_weights(where, gate_idx, up_idx, tiles, w_ref):
    w_ref[...] = jnp.zeros_like(w_ref)

    def put(step, carry):
        group, k = step // where.kept_here, step % where.kept_here
        j = where.kept(group, k)
        block = [tiles[where.at(group, p, k)] for p in range(where.half_panels)]
        for idx_ref, left in ((gate_idx, True), (up_idx, False)):
            put_blocks(w_ref, [
                (pl.ds(where.row(idx_ref, p, j), BLK), pl.ds(p * 2 * BLK, 2 * BLK), block[p], left)
                for p in range(where.half_panels)
            ])
        return carry

    lax.fori_loop(0, 2 * RING * where.kept_here, put, 0)


def build_down_weights(where, down_idx, tiles, w_ref):
    w_ref[...] = jnp.zeros_like(w_ref)

    def put(step, carry):
        group, m = step // where.pairs, step % where.pairs
        j = where.kept(group, 2 * m)
        for parity in range(2):
            places = []
            for p in range(parity, where.half_panels, 2):
                tile = tiles[where.at(group, p, where.kept_here + m)]
                for h in range(2):
                    rows = pl.ds(where.row(down_idx, p, j + h), BLK)
                    source = tile if h == parity else flip(tile)
                    places.append((rows, pl.ds((p // 2) * 128, 128), source, parity == 0))
            put_blocks(w_ref, places)
        return carry

    lax.fori_loop(0, 2 * RING * where.pairs, put, 0)


def back_rows(left, w_ref, out_ref, place):
    width = w_ref.shape[0]
    step = min(width, 1024)
    per = out_ref.shape[1]
    for start in range(0, width, step):
        part = lax.dot_general(
            left, w_ref[start : start + step, :], (((1,), (1,)), ((), ())),
            preferred_element_type=F32,
        ).astype(BF)
        for a in range(RING // 2):
            for b in range(RING):
                at = (a * RING + b) * per
                chunk = a * RING + (place[2] + b) % RING
                out_ref[chunk, :, start : start + step] = part[at : at + per]


def forward_tile(half_panels, x_tile, w_ref, m_ref, h_ref, h2_ref):
    rows = x_tile.shape[0]
    both = jnp.dot(x_tile, w_ref[...], preferred_element_type=F32)
    mask = left_half((rows, 2 * BLK))
    per = m_ref.shape[3]
    spans = [(a, b, (a * RING + b) * per) for a in range(RING // 2) for b in range(RING)]
    for first in range(0, half_panels, 2):
        group = [slice(p * 2 * BLK, (p + 1) * 2 * BLK) for p in range(first, min(first + 2, half_panels))]
        low, high = both[:, group[0]], both[:, group[-1]]
        gate = jnp.where(mask, low, flip(high))
        up = jnp.where(mask, flip(low), high)
        sigma = jax.nn.sigmoid(gate)
        silu = gate * sigma
        slope = up * sigma * (1.0 + gate * (1.0 - sigma))
        mults = [jnp.where(mask, slope, flip(silu)), jnp.where(mask, flip(slope), silu)]
        for lanes, mult in zip(group, mults):
            for a, b, at in spans:
                m_ref[0, a, b, :, lanes] = mult[at : at + per]
        hidden = silu * up
        if len(group) == 1:
            hidden = jnp.where(mask, hidden, 0.0)
        hidden = hidden.astype(BF)
        out = slice(first * BLK, (first + 2) * BLK)
        h_ref[:, out] = hidden
        for a, b, at in spans:
            h2_ref[0, b, a, :, out] = hidden[at : at + per]


def forward_kernel(half_panels, kept_here, first, place, *refs):
    if first:
        gate_idx, up_idx, down_idx, tiles = refs[:4]
        pieces, refs = refs[4:8], refs[8:]
        m_ref, h2_ref, y_ref, w_other, wd_other = refs[:5]
    else:
        w_other, wd_other = refs[:2]
        pieces, refs = refs[2:6], refs[8:]
        m_ref, h2_ref, y_ref = refs[:3]
    w_ref, wd_ref, h_ref, buf, sems, w_sems = refs[-6:]
    i = pl.program_id(0)
    rows = buf.shape[0] // 2
    copies = row_copies(pieces, buf, sems)
    pairs = ((w_ref, w_other), (wd_ref, wd_other))
    if not first:
        pairs = [(b, a) for a, b in pairs]
    w_copies = [pltpu.make_async_copy(a, b, w_sems.at[n]) for n, (a, b) in enumerate(pairs)]

    @pl.when(i == 0)
    def _():
        if not first:
            w_copies[0].start()
        for copy in copies:
            copy.start()
        if not first:
            w_copies[1].start()
        if first:
            where = Tiles(half_panels, kept_here, place[0])
            build_input_weights(where, gate_idx, up_idx, tiles, w_ref)
            w_copies[0].start()
            build_down_weights(where, down_idx, tiles, wd_ref)
            w_copies[1].start()
        else:
            w_copies[0].wait()

    tile_wait(copies, i)
    x_tile = buf[pl.ds(pl.multiple_of(i * rows, rows), rows), :]
    forward_tile(half_panels, x_tile, w_ref, m_ref, h_ref, h2_ref)
    if not first:

        @pl.when(i == 0)
        def _():
            w_copies[1].wait()

    back_rows(h_ref[...], wd_ref, y_ref, place)
    if first:

        @pl.when(i == pl.num_programs(0) - 1)
        def _():
            for copy in w_copies:
                copy.wait()


def gradient_kernel(half_panels, kept_here, place, gate_idx, up_idx, down_idx, *refs):
    dy_pieces, x_pieces, refs = refs[:2], refs[2:10], refs[10:]
    wd_ref, m_ref, h_ref, back_kept, back_away, out_ref = refs[:6]
    dy_buf, x_buf, g_ref, acc, dy_sems, x_sems, g_sems = refs[6:]
    i = pl.program_id(0)
    where = Tiles(half_panels, kept_here, place[0])
    rows = dy_buf.shape[0] // 4
    dy_copies = ring_copies(dy_pieces, dy_buf, dy_sems, place)
    x_copies = chunk_copies(x_pieces, x_buf, x_sems, place)
    half_rows = back_kept.shape[0]
    g_copies = [
        pltpu.make_async_copy(g_ref.at[pl.ds(n * half_rows, half_rows)], out, g_sems.at[n])
        for n, out in enumerate((back_kept, back_away))
    ]
    hid = h_ref.shape[1]
    cols = dy_buf.shape[1] // 4
    mask = left_half((rows, 2 * BLK))
    small = left_half((BLK, 2 * BLK))

    @pl.when(i == 0)
    def _():
        for copy in dy_copies:
            copy.start()

    for t in range(4):

        @pl.when(i == t)
        def _(t=t):
            for copy in dy_copies[8 * t : 8 * t + 8]:
                copy.wait()

    @pl.when(i < 4)
    def _():
        dy_tile = dy_buf[pl.ds(pl.multiple_of(i * rows, rows), rows), :]
        d_hidden = jnp.dot(dy_tile, wd_ref[...], preferred_element_type=F32)
        per = m_ref.shape[3]
        for p in range(half_panels):
            if p % 2 == 0:
                here = d_hidden[:, (p // 2) * 128 : (p // 2 + 1) * 128]
                turned = flip(here)
                spread = jnp.where(mask, here, turned)
            else:
                spread = jnp.where(mask, turned, here)
            lanes = slice(p * 2 * BLK, (p + 1) * 2 * BLK)
            for a in range(RING // 2):
                for b in range(RING):
                    at = (a * RING + b) * per
                    chunk = owner_row(i // 2, b, place[2] + (i % 2) * (RING // 2) + a)
                    rows_at = pl.ds(pl.multiple_of(chunk * per, per), per)
                    g_ref[rows_at, lanes] = (
                        spread[at : at + per] * m_ref[0, b, a, :, lanes]
                    ).astype(BF)

    @pl.when((i >= 4) & (i < 8))
    def _():
        at = pl.multiple_of((i - 4) * cols, cols)
        part = lax.dot_general(
            dy_buf[:, pl.ds(at, cols)], h_ref[...], (((0,), (0,)), ((), ())),
            preferred_element_type=F32,
        )
        acc[pl.ds(at, cols), :hid] = part.astype(BF)

    @pl.when(i == 3)
    def _():
        for copy in x_copies:
            copy.start()

    @pl.when(i == 4)
    def _():
        for copy in g_copies:
            copy.start()

    @pl.when(i == 7)
    def _():
        def take(step, carry):
            group, m = step // where.pairs, step % where.pairs
            j = where.kept(group, 2 * m)
            for p in range(half_panels):
                lanes = pl.ds((p // 2) * 128, 128)
                first = acc[pl.ds(where.row(down_idx, p, j), BLK), lanes]
                second = acc[pl.ds(where.row(down_idx, p, j + 1), BLK), lanes]
                if p % 2 == 0:
                    second = flip(second)
                else:
                    first = flip(first)
                out_ref[where.at(group, p, kept_here + m)] = jnp.where(small, first, second)
            return carry

        lax.fori_loop(0, 2 * RING * where.pairs, take, 0)

    @pl.when(i == 8)
    def _():
        for copy in x_copies:
            copy.wait()

    @pl.when(i >= 8)
    def _():
        at = pl.multiple_of((i - 8) * cols, cols)
        part = lax.dot_general(
            x_buf[:, pl.ds(at, cols)], g_ref[...], (((0,), (0,)), ((), ())),
            preferred_element_type=F32,
        )
        acc[pl.ds(at, cols), :] = part.astype(BF)

    @pl.when(i == pl.num_programs(0) - 1)
    def _():
        def take(step, carry):
            group, k = step // kept_here, step % kept_here
            j = where.kept(group, k)
            for p in range(half_panels):
                lanes = pl.ds(p * 2 * BLK, 2 * BLK)
                first = acc[pl.ds(where.row(gate_idx, p, j), BLK), lanes]
                second = acc[pl.ds(where.row(up_idx, p, j), BLK), lanes]
                out_ref[where.at(group, p, k)] = jnp.where(small, first, second)
            return carry

        lax.fori_loop(0, 2 * RING * kept_here, take, 0)
        for copy in g_copies:
            copy.wait()


def cost(flops, nbytes):
    return pl.CostEstimate(flops=flops // 8, bytes_accessed=nbytes // 8, transcendentals=0)


def per_device(x_seq, dy_seq, gate_vals, gate_idx, up_vals, up_idx, down_vals, down_idx):
    panels, kept_here, square = gate_vals.shape
    per, width = x_seq.shape
    edge = BLK
    half = panels // 2
    pairs = kept_here // 2
    per_panel = kept_here + pairs
    zh, z_place = lax.axis_index("zh"), lax.axis_index(Z)
    place = jnp.stack([zh, z_place, lax.axis_index("x")]).astype(jnp.int32)
    shape = jax.ShapeDtypeStruct

    gate_blk = gate_vals.reshape(panels, kept_here, edge, edge)
    up_blk = up_vals.reshape(panels, kept_here, edge, edge)
    pair_gu = jnp.concatenate([gate_blk, up_blk], axis=3)
    down_blk = down_vals.reshape(panels, pairs, 2, edge, edge)
    pair_d = jnp.transpose(down_blk, (0, 1, 4, 2, 3)).reshape(panels, pairs, edge, 2 * edge)
    all_pairs = jnp.concatenate([pair_gu, pair_d], axis=1)
    own = lax.dynamic_slice_in_dim(all_pairs, zh * half, half, 0)
    other = swap(lax.dynamic_slice_in_dim(all_pairs, (1 - zh) * half, half, 0), "zh")

    def gather_all(value, axis):
        wide = jnp.broadcast_to(value[None], (RING, *value.shape))
        return lax.all_to_all(wide, axis, 0, 0, tiled=True)

    dy_row = gather_all(dy_seq, Z)
    x_row = jnp.concatenate(gather_direct(x_seq, "x"), axis=0)
    other, x_row, dy_row = lax.optimization_barrier((other, x_row, dy_row))
    both = jnp.stack([own, other]).reshape(-1, edge, 2 * edge)
    tiles = lax.all_gather(both, "y", axis=0, tiled=True)
    dy_own = gather_all(dy_row, "x")
    x_own = gather_direct(x_row, Z)
    x_core = [swap(v, "c") for v in x_own]
    x_core, dy_own = lax.optimization_barrier((x_core, dy_own))
    dy_core = swap(dy_own, "c")

    tokens = 2 * RING * RING * per
    rows = tokens // 4
    hid = -(-half * edge // 128) * 128
    two = half * 2 * edge
    pair = RING // 2
    once = pl.Buffered(1)
    full = lambda *dims: pl.BlockSpec(dims, lambda i: (0,) * len(dims), pipeline_mode=once)
    out_full = lambda *dims: pl.BlockSpec(dims, lambda i: (0,) * len(dims))
    smem = pl.BlockSpec(memory_space=pltpu.SMEM)
    hbm = pl.BlockSpec(memory_space=pl.ANY)
    ordered = lambda last: (2, RING, RING, per, last)
    gu_flops = 2 * tokens * width * two
    d_flops = 2 * tokens * width * hid
    chunks = (RING * RING, per, width)

    def part(fn, *extra):
        def body(*refs):
            fn(*extra, *refs)

        return body

    def forward(core, first, inputs, name):
        specs = [smem] * 4 + [full(*tiles.shape)] + [hbm] * 4 if first else [smem] + [hbm] * 8
        extra_out = [shape((width, two), BF), shape((width, hid), BF)] if first else []
        return pl.pallas_call(
            part(forward_kernel, half, kept_here, first),
            grid=(2,),
            in_specs=specs,
            out_specs=[
                pl.BlockSpec((1, pair, RING, per, two), lambda i: (core, i, 0, 0, 0)),
                pl.BlockSpec((1, RING, pair, per, hid), lambda i: (core, 0, i, 0, 0)),
                pl.BlockSpec((pair * RING, per, width), lambda i: (i, 0, 0)),
            ] + [hbm] * len(extra_out),
            out_shape=[shape(ordered(two), F32), shape(ordered(hid), BF), shape(chunks, BF)] + extra_out,
            scratch_shapes=[
                pltpu.VMEM((width, two), BF),
                pltpu.VMEM((width, hid), BF),
                pltpu.VMEM((rows, hid), BF),
                pltpu.VMEM((tokens // 2, width), BF),
                pltpu.SemaphoreType.DMA((4,)),
                pltpu.SemaphoreType.DMA((2,)),
            ],
            input_output_aliases={} if first else {7: 0, 8: 1},
            compiler_params=kernel_params(56),
            cost_estimate=cost((gu_flops + d_flops) // 2, 24 * MIB),
            name=name,
        )(place, *inputs)

    mult, hidden, y_away, w_gu, w_d = forward(
        1, True, (gate_idx, up_idx, down_idx, tiles, *x_core), "forward_away"
    )
    y_recv = swap(y_away, "c")
    mult, hidden, y_kept = forward(0, False, (w_gu, w_d, *x_own, mult, hidden), "forward_kept")
    y_kept, dy_core = lax.optimization_barrier((y_kept, dy_core))
    dy_pieces = [v.reshape(RING, RING, per, width) for v in (dy_own, dy_core)]

    def chip_rows(kept, received):
        halves = []
        for first in range(0, width, width // 2):
            split = lambda v: v.reshape(RING, RING, per, width)[..., first : first + width // 2]
            halves.append(add(split(kept), split(received)))
        return jnp.transpose(halves[0], (1, 0, 2, 3)), halves[1]

    def over_x(value):
        return jnp.sum(lax.all_to_all(value, "x", 0, 0, tiled=True).astype(F32), axis=0).astype(BF)

    def over_z(value):
        return scatter_direct([value[n] for n in range(RING)], Z)

    y_half = chip_rows(y_kept, y_recv)
    mult, y_half = lax.optimization_barrier((mult, y_half))
    y_half = over_x(y_half[0]), over_z(y_half[1])

    steps = 12
    x_tile = lambda i: jnp.minimum(i, 3)
    back_kept, back_away, terms = pl.pallas_call(
        part(gradient_kernel, half, kept_here),
        grid=(steps,),
        in_specs=[smem] * 4
        + [hbm] * 10
        + [
            full(width, hid),
            pl.BlockSpec(
                (1, RING, pair, per, two), lambda i: (x_tile(i) // 2, 0, x_tile(i) % 2, 0, 0)
            ),
            full(tokens, hid),
        ],
        out_specs=[hbm, hbm, out_full(*tiles.shape)],
        out_shape=[shape((tokens // 2, two), BF)] * 2 + [shape(tiles.shape, BF)],
        scratch_shapes=[
            pltpu.VMEM((tokens, width), BF),
            pltpu.VMEM((tokens, width), BF),
            pltpu.VMEM((tokens, two), BF),
            pltpu.VMEM((width, two), BF),
            pltpu.SemaphoreType.DMA((32,)),
            pltpu.SemaphoreType.DMA((32,)),
            pltpu.SemaphoreType.DMA((2,)),
        ],
        compiler_params=kernel_params(60),
        cost_estimate=cost(gu_flops + 2 * d_flops, 40 * MIB),
        name="gradients",
    )(
        place, gate_idx, up_idx, down_idx, *dy_pieces, *x_own, *x_core,
        w_d, mult, hidden.reshape(tokens, hid),
    )

    def project(left):
        return lax.dot_general(left, w_gu, (((1,), (1,)), ((), ())), preferred_element_type=F32)

    back_away, y_half = lax.optimization_barrier((back_away, y_half))
    dx_away = project(back_away).astype(BF)
    dx_recv = swap(dx_away, "c")
    back_kept, dx_away = lax.optimization_barrier((back_kept, dx_away))
    dx_kept, dx_recv = lax.optimization_barrier((project(back_kept).astype(BF), dx_recv))
    dx_half = lax.optimization_barrier(chip_rows(dx_kept, dx_recv))
    dx_half = over_x(dx_half[0]), over_z(dx_half[1])
    x_first, z_first = (jnp.stack(parts, axis=1) for parts in zip(y_half, dx_half))
    summed = lax.psum_scatter(terms, "y", scatter_dimension=0, tiled=True)
    x_first, z_first, summed = lax.optimization_barrier((x_first, z_first, summed))
    x_first, z_first = over_z(x_first), over_x(z_first)
    y_seq, dx_seq = (jnp.concatenate([x_first[n], z_first[n]], axis=1) for n in range(2))

    summed = summed.reshape(2, half, per_panel, edge, 2 * edge)
    other = swap(summed[1], "zh")
    low = jnp.where(zh == 0, summed[0], other)
    high = jnp.where(zh == 0, other, summed[0])
    grads = jnp.concatenate([low, high], axis=0)
    gu_grads = grads[:, :kept_here]
    d_gate_vals = gu_grads[..., :edge].reshape(panels, kept_here, square)
    d_up_vals = gu_grads[..., edge:].reshape(panels, kept_here, square)
    d_grads = grads[:, kept_here:].reshape(panels, pairs, edge, 2, edge)
    d_down_vals = jnp.transpose(d_grads, (0, 1, 3, 4, 2)).reshape(panels, kept_here, square)
    return (y_seq, dx_seq, d_gate_vals, d_up_vals, d_down_vals)


def solution(mesh):
    grid = Mesh(mesh.devices.reshape(4, 2, 4, 2, 2), AXES)
    row, col = ("y", "zh"), ("x", "zl", "c")
    tokens = P(row + col, None)
    vals = P(col, row, None)
    idx = P(col, None)
    return jax.shard_map(
        per_device,
        mesh=grid,
        in_specs=(tokens, tokens, vals, idx, vals, idx, vals, idx),
        out_specs=(tokens, tokens, vals, vals, vals),
        check_vma=False,
    )
```

```python
import jax
import jax.numpy as jnp
from jax import lax
from jax.experimental import pallas as pl
from jax.experimental.pallas import tpu as pltpu
from jax.sharding import Mesh, PartitionSpec as P

BLK = 64
AXES = ("y", "zh", "x", "zl", "c")
Z = ("zh", "zl")
ZX = ("zh", "zl", "x")
RING = 4
BF = jnp.bfloat16
F32 = jnp.float32
MIB = 1024 * 1024


def shift(value, axis, step):
    return lax.ppermute(value, axis, [(i, (i + step) % RING) for i in range(RING)])


def swap(value, axis):
    return lax.ppermute(value, axis, [(0, 1), (1, 0)])


def gather_direct(own, axis):
    below = shift(own, axis, 1)
    above = shift(own, axis, -1)
    across = shift(own, axis, 2)
    return [own, above, across, below]


def scatter_direct(chunks, axis):
    return chunks[0], shift(chunks[1], axis, 1), shift(chunks[2], axis, 2), shift(chunks[3], axis, -1)


def total(parts):
    return sum(part.astype(F32) for part in parts).astype(BF)


def add(first, second):
    return (first.astype(F32) + second.astype(F32)).astype(BF)


def left_half(shape):
    return lax.broadcasted_iota(jnp.int32, shape, len(shape) - 1) % (2 * BLK) < BLK


def flip(value):
    return pltpu.roll(value, BLK, 1)


def kernel_params(limit):
    return pltpu.CompilerParams(
        dimension_semantics=("arbitrary",), vmem_limit_bytes=limit * MIB
    )


def row_copies(pieces, buf, sems):
    rows = pieces[0].shape[0]
    return [
        pltpu.make_async_copy(piece, buf.at[pl.ds(n * rows, rows)], sems.at[n])
        for n, piece in enumerate(pieces)
    ]


def owner_row(core, z, x):
    return core * RING * RING + z * RING + x % RING


def chunk_copies(pieces, buf, sems, place):
    per = pieces[0].shape[0] // RING
    copies = []
    for n, piece in enumerate(pieces):
        for x in range(RING):
            at = owner_row(n // RING, n % RING, place[2] + x) * per
            copies.append(
                pltpu.make_async_copy(
                    piece.at[pl.ds(x * per, per)],
                    buf.at[pl.ds(pl.multiple_of(at, per), per)],
                    sems.at[n * RING + x],
                )
            )
    return copies


def ring_copies(pieces, buf, sems, place):
    per = pieces[0].shape[2]
    copies = []
    for n in range(2 * RING * RING):
        core, x, z = n // (RING * RING), n // RING % RING, n % RING
        source = pieces[core].at[(place[2] + x) % RING, (place[1] + z) % RING]
        copies.append(pltpu.make_async_copy(source, buf.at[pl.ds(n * per, per)], sems.at[n]))
    return copies


def tile_wait(copies, i):
    for t in range(len(copies) // 2):

        @pl.when(i == t)
        def _(t=t):
            copies[2 * t].wait()
            copies[2 * t + 1].wait()


class Tiles:
    def __init__(self, half_panels, kept_here, zh):
        self.half_panels, self.kept_here, self.zh = half_panels, kept_here, zh
        self.pairs = kept_here // 2
        self.per_panel = kept_here + self.pairs

    def at(self, group, p, k):
        return (group * self.half_panels + p) * self.per_panel + k

    def kept(self, group, k):
        return (group // 2) * (2 * self.kept_here) + (self.zh ^ (group % 2)) * self.kept_here + k

    def row(self, idx_ref, p, j):
        return pl.multiple_of(idx_ref[self.zh * self.half_panels + p, j] * BLK, BLK)


def put_blocks(w_ref, places):
    mask = left_half((BLK, 2 * BLK))
    old = [w_ref[rows, lanes] for rows, lanes, _, _ in places]
    for before, (rows, lanes, tile, left) in zip(old, places):
        w_ref[rows, lanes] = jnp.where(mask, tile, before) if left else jnp.where(mask, before, tile)


def build_input_weights(where, gate_idx, up_idx, tiles, w_ref):
    w_ref[...] = jnp.zeros_like(w_ref)

    def put(step, carry):
        group, k = step // where.kept_here, step % where.kept_here
        j = where.kept(group, k)
        block = [tiles[where.at(group, p, k)] for p in range(where.half_panels)]
        for idx_ref, left in ((gate_idx, True), (up_idx, False)):
            put_blocks(w_ref, [
                (pl.ds(where.row(idx_ref, p, j), BLK), pl.ds(p * 2 * BLK, 2 * BLK), block[p], left)
                for p in range(where.half_panels)
            ])
        return carry

    lax.fori_loop(0, 2 * RING * where.kept_here, put, 0)


def build_down_weights(where, down_idx, tiles, w_ref):
    w_ref[...] = jnp.zeros_like(w_ref)

    def put(step, carry):
        group, m = step // where.pairs, step % where.pairs
        j = where.kept(group, 2 * m)
        for parity in range(2):
            places = []
            for p in range(parity, where.half_panels, 2):
                tile = tiles[where.at(group, p, where.kept_here + m)]
                for h in range(2):
                    rows = pl.ds(where.row(down_idx, p, j + h), BLK)
                    source = tile if h == parity else flip(tile)
                    places.append((rows, pl.ds((p // 2) * 128, 128), source, parity == 0))
            put_blocks(w_ref, places)
        return carry

    lax.fori_loop(0, 2 * RING * where.pairs, put, 0)


def back_rows(left, w_ref, out_ref, place):
    width = w_ref.shape[0]
    step = min(width, 1024)
    per = out_ref.shape[1]
    for start in range(0, width, step):
        part = lax.dot_general(
            left, w_ref[start : start + step, :], (((1,), (1,)), ((), ())),
            preferred_element_type=F32,
        ).astype(BF)
        for a in range(RING // 2):
            for b in range(RING):
                at = (a * RING + b) * per
                chunk = a * RING + (place[2] + b) % RING
                out_ref[chunk, :, start : start + step] = part[at : at + per]


def forward_tile(half_panels, x_tile, w_ref, m_ref, h_ref, h2_ref):
    rows = x_tile.shape[0]
    both = jnp.dot(x_tile, w_ref[...], preferred_element_type=F32)
    mask = left_half((rows, 2 * BLK))
    per = m_ref.shape[3]
    spans = [(a, b, (a * RING + b) * per) for a in range(RING // 2) for b in range(RING)]
    for first in range(0, half_panels, 2):
        group = [slice(p * 2 * BLK, (p + 1) * 2 * BLK) for p in range(first, min(first + 2, half_panels))]
        low, high = both[:, group[0]], both[:, group[-1]]
        gate = jnp.where(mask, low, flip(high))
        up = jnp.where(mask, flip(low), high)
        sigma = jax.nn.sigmoid(gate)
        silu = gate * sigma
        slope = up * sigma * (1.0 + gate * (1.0 - sigma))
        mults = [jnp.where(mask, slope, flip(silu)), jnp.where(mask, flip(slope), silu)]
        for lanes, mult in zip(group, mults):
            for a, b, at in spans:
                m_ref[0, a, b, :, lanes] = mult[at : at + per]
        hidden = silu * up
        if len(group) == 1:
            hidden = jnp.where(mask, hidden, 0.0)
        hidden = hidden.astype(BF)
        out = slice(first * BLK, (first + 2) * BLK)
        h_ref[:, out] = hidden
        for a, b, at in spans:
            h2_ref[0, b, a, :, out] = hidden[at : at + per]


def forward_kernel(half_panels, kept_here, first, place, *refs):
    if first:
        gate_idx, up_idx, down_idx, tiles = refs[:4]
        pieces, refs = refs[4:8], refs[8:]
        m_ref, h2_ref, y_ref, w_other, wd_other = refs[:5]
    else:
        w_other, wd_other = refs[:2]
        pieces, refs = refs[2:6], refs[8:]
        m_ref, h2_ref, y_ref = refs[:3]
    w_ref, wd_ref, h_ref, buf, sems, w_sems = refs[-6:]
    i = pl.program_id(0)
    rows = buf.shape[0] // 2
    copies = row_copies(pieces, buf, sems)
    pairs = ((w_ref, w_other), (wd_ref, wd_other))
    if not first:
        pairs = [(b, a) for a, b in pairs]
    w_copies = [pltpu.make_async_copy(a, b, w_sems.at[n]) for n, (a, b) in enumerate(pairs)]

    @pl.when(i == 0)
    def _():
        if not first:
            w_copies[0].start()
        for copy in copies:
            copy.start()
        if not first:
            w_copies[1].start()
        if first:
            where = Tiles(half_panels, kept_here, place[0])
            build_input_weights(where, gate_idx, up_idx, tiles, w_ref)
            w_copies[0].start()
            build_down_weights(where, down_idx, tiles, wd_ref)
            w_copies[1].start()
        else:
            w_copies[0].wait()

    tile_wait(copies, i)
    x_tile = buf[pl.ds(pl.multiple_of(i * rows, rows), rows), :]
    forward_tile(half_panels, x_tile, w_ref, m_ref, h_ref, h2_ref)
    if not first:

        @pl.when(i == 0)
        def _():
            w_copies[1].wait()

    back_rows(h_ref[...], wd_ref, y_ref, place)
    if first:

        @pl.when(i == pl.num_programs(0) - 1)
        def _():
            for copy in w_copies:
                copy.wait()


def gradient_kernel(half_panels, kept_here, place, gate_idx, up_idx, down_idx, *refs):
    dy_pieces, x_pieces, refs = refs[:2], refs[2:10], refs[10:]
    wd_ref, m_ref, h_ref, back_kept, back_away, out_ref = refs[:6]
    dy_buf, x_buf, g_ref, acc, dy_sems, x_sems, g_sems = refs[6:]
    i = pl.program_id(0)
    where = Tiles(half_panels, kept_here, place[0])
    rows = dy_buf.shape[0] // 4
    dy_copies = ring_copies(dy_pieces, dy_buf, dy_sems, place)
    x_copies = chunk_copies(x_pieces, x_buf, x_sems, place)
    half_rows = back_kept.shape[0]
    g_copies = [
        pltpu.make_async_copy(g_ref.at[pl.ds(n * half_rows, half_rows)], out, g_sems.at[n])
        for n, out in enumerate((back_kept, back_away))
    ]
    hid = h_ref.shape[1]
    cols = dy_buf.shape[1] // 4
    mask = left_half((rows, 2 * BLK))
    small = left_half((BLK, 2 * BLK))

    @pl.when(i == 0)
    def _():
        for copy in dy_copies:
            copy.start()

    for t in range(4):

        @pl.when(i == t)
        def _(t=t):
            for copy in dy_copies[8 * t : 8 * t + 8]:
                copy.wait()

    @pl.when(i < 4)
    def _():
        dy_tile = dy_buf[pl.ds(pl.multiple_of(i * rows, rows), rows), :]
        d_hidden = jnp.dot(dy_tile, wd_ref[...], preferred_element_type=F32)
        per = m_ref.shape[3]
        for p in range(half_panels):
            if p % 2 == 0:
                here = d_hidden[:, (p // 2) * 128 : (p // 2 + 1) * 128]
                turned = flip(here)
                spread = jnp.where(mask, here, turned)
            else:
                spread = jnp.where(mask, turned, here)
            lanes = slice(p * 2 * BLK, (p + 1) * 2 * BLK)
            for a in range(RING // 2):
                for b in range(RING):
                    at = (a * RING + b) * per
                    chunk = owner_row(i // 2, b, place[2] + (i % 2) * (RING // 2) + a)
                    rows_at = pl.ds(pl.multiple_of(chunk * per, per), per)
                    g_ref[rows_at, lanes] = (
                        spread[at : at + per] * m_ref[0, b, a, :, lanes]
                    ).astype(BF)

    @pl.when((i >= 4) & (i < 8))
    def _():
        at = pl.multiple_of((i - 4) * cols, cols)
        part = lax.dot_general(
            dy_buf[:, pl.ds(at, cols)], h_ref[...], (((0,), (0,)), ((), ())),
            preferred_element_type=F32,
        )
        acc[pl.ds(at, cols), :hid] = part.astype(BF)

    @pl.when(i == 3)
    def _():
        for copy in x_copies:
            copy.start()

    @pl.when(i == 4)
    def _():
        for copy in g_copies:
            copy.start()

    @pl.when(i == 7)
    def _():
        def take(step, carry):
            group, m = step // where.pairs, step % where.pairs
            j = where.kept(group, 2 * m)
            for p in range(half_panels):
                lanes = pl.ds((p // 2) * 128, 128)
                first = acc[pl.ds(where.row(down_idx, p, j), BLK), lanes]
                second = acc[pl.ds(where.row(down_idx, p, j + 1), BLK), lanes]
                if p % 2 == 0:
                    second = flip(second)
                else:
                    first = flip(first)
                out_ref[where.at(group, p, kept_here + m)] = jnp.where(small, first, second)
            return carry

        lax.fori_loop(0, 2 * RING * where.pairs, take, 0)

    @pl.when(i == 8)
    def _():
        for copy in x_copies:
            copy.wait()

    @pl.when(i >= 8)
    def _():
        at = pl.multiple_of((i - 8) * cols, cols)
        part = lax.dot_general(
            x_buf[:, pl.ds(at, cols)], g_ref[...], (((0,), (0,)), ((), ())),
            preferred_element_type=F32,
        )
        acc[pl.ds(at, cols), :] = part.astype(BF)

    @pl.when(i == pl.num_programs(0) - 1)
    def _():
        def take(step, carry):
            group, k = step // kept_here, step % kept_here
            j = where.kept(group, k)
            for p in range(half_panels):
                lanes = pl.ds(p * 2 * BLK, 2 * BLK)
                first = acc[pl.ds(where.row(gate_idx, p, j), BLK), lanes]
                second = acc[pl.ds(where.row(up_idx, p, j), BLK), lanes]
                out_ref[where.at(group, p, k)] = jnp.where(small, first, second)
            return carry

        lax.fori_loop(0, 2 * RING * kept_here, take, 0)
        for copy in g_copies:
            copy.wait()


def cost(flops, nbytes):
    return pl.CostEstimate(flops=flops // 8, bytes_accessed=nbytes // 8, transcendentals=0)


def per_device(x_seq, dy_seq, gate_vals, gate_idx, up_vals, up_idx, down_vals, down_idx):
    panels, kept_here, square = gate_vals.shape
    per, width = x_seq.shape
    edge = BLK
    half = panels // 2
    pairs = kept_here // 2
    per_panel = kept_here + pairs
    zh, z_place = lax.axis_index("zh"), lax.axis_index(Z)
    place = jnp.stack([zh, z_place, lax.axis_index("x")]).astype(jnp.int32)
    shape = jax.ShapeDtypeStruct

    gate_blk = gate_vals.reshape(panels, kept_here, edge, edge)
    up_blk = up_vals.reshape(panels, kept_here, edge, edge)
    pair_gu = jnp.concatenate([gate_blk, up_blk], axis=3)
    down_blk = down_vals.reshape(panels, pairs, 2, edge, edge)
    pair_d = jnp.transpose(down_blk, (0, 1, 4, 2, 3)).reshape(panels, pairs, edge, 2 * edge)
    all_pairs = jnp.concatenate([pair_gu, pair_d], axis=1)
    own = lax.dynamic_slice_in_dim(all_pairs, zh * half, half, 0)
    other = swap(lax.dynamic_slice_in_dim(all_pairs, (1 - zh) * half, half, 0), "zh")

    def gather_all(value, axis):
        wide = jnp.broadcast_to(value[None], (RING, *value.shape))
        return lax.all_to_all(wide, axis, 0, 0, tiled=True)

    dy_row = gather_all(dy_seq, Z)
    x_row = jnp.concatenate(gather_direct(x_seq, "x"), axis=0)
    other, x_row, dy_row = lax.optimization_barrier((other, x_row, dy_row))
    both = jnp.stack([own, other]).reshape(-1, edge, 2 * edge)
    tiles = lax.all_gather(both, "y", axis=0, tiled=True)
    dy_own = gather_all(dy_row, "x")
    x_own = gather_direct(x_row, Z)
    x_core = [swap(v, "c") for v in x_own]
    x_core, dy_own = lax.optimization_barrier((x_core, dy_own))
    dy_core = swap(dy_own, "c")

    tokens = 2 * RING * RING * per
    rows = tokens // 4
    hid = -(-half * edge // 128) * 128
    two = half * 2 * edge
    pair = RING // 2
    once = pl.Buffered(1)
    full = lambda *dims: pl.BlockSpec(dims, lambda i: (0,) * len(dims), pipeline_mode=once)
    out_full = lambda *dims: pl.BlockSpec(dims, lambda i: (0,) * len(dims))
    smem = pl.BlockSpec(memory_space=pltpu.SMEM)
    hbm = pl.BlockSpec(memory_space=pl.ANY)
    ordered = lambda last: (2, RING, RING, per, last)
    gu_flops = 2 * tokens * width * two
    d_flops = 2 * tokens * width * hid
    chunks = (RING * RING, per, width)

    def part(fn, *extra):
        def body(*refs):
            fn(*extra, *refs)

        return body

    def forward(core, first, inputs, name):
        specs = [smem] * 4 + [full(*tiles.shape)] + [hbm] * 4 if first else [smem] + [hbm] * 8
        extra_out = [shape((width, two), BF), shape((width, hid), BF)] if first else []
        return pl.pallas_call(
            part(forward_kernel, half, kept_here, first),
            grid=(2,),
            in_specs=specs,
            out_specs=[
                pl.BlockSpec((1, pair, RING, per, two), lambda i: (core, i, 0, 0, 0)),
                pl.BlockSpec((1, RING, pair, per, hid), lambda i: (core, 0, i, 0, 0)),
                pl.BlockSpec((pair * RING, per, width), lambda i: (i, 0, 0)),
            ] + [hbm] * len(extra_out),
            out_shape=[shape(ordered(two), F32), shape(ordered(hid), BF), shape(chunks, BF)] + extra_out,
            scratch_shapes=[
                pltpu.VMEM((width, two), BF),
                pltpu.VMEM((width, hid), BF),
                pltpu.VMEM((rows, hid), BF),
                pltpu.VMEM((tokens // 2, width), BF),
                pltpu.SemaphoreType.DMA((4,)),
                pltpu.SemaphoreType.DMA((2,)),
            ],
            input_output_aliases={} if first else {7: 0, 8: 1},
            compiler_params=kernel_params(56),
            cost_estimate=cost((gu_flops + d_flops) // 2, 24 * MIB),
            name=name,
        )(place, *inputs)

    mult, hidden, y_away, w_gu, w_d = forward(
        1, True, (gate_idx, up_idx, down_idx, tiles, *x_core), "forward_away"
    )
    y_recv = swap(y_away, "c")
    mult, hidden, y_kept = forward(0, False, (w_gu, w_d, *x_own, mult, hidden), "forward_kept")
    y_kept, dy_core = lax.optimization_barrier((y_kept, dy_core))
    dy_pieces = [v.reshape(RING, RING, per, width) for v in (dy_own, dy_core)]

    def chip_rows(kept, received):
        halves = []
        for first in range(0, width, width // 2):
            split = lambda v: v.reshape(RING, RING, per, width)[..., first : first + width // 2]
            halves.append(add(split(kept), split(received)))
        return jnp.transpose(halves[0], (1, 0, 2, 3)), halves[1]

    def over_x(value):
        return lax.all_to_all(value, "x", 0, 0, tiled=True)

    def over_z(value):
        return scatter_direct([value[n] for n in range(RING)], Z)

    y_half = chip_rows(y_kept, y_recv)
    mult, y_half = lax.optimization_barrier((mult, y_half))
    y_half = over_x(y_half[0]), over_z(y_half[1])

    steps = 12
    x_tile = lambda i: jnp.minimum(i, 3)
    back_kept, back_away, terms = pl.pallas_call(
        part(gradient_kernel, half, kept_here),
        grid=(steps,),
        in_specs=[smem] * 4
        + [hbm] * 10
        + [
            full(width, hid),
            pl.BlockSpec(
                (1, RING, pair, per, two), lambda i: (x_tile(i) // 2, 0, x_tile(i) % 2, 0, 0)
            ),
            full(tokens, hid),
        ],
        out_specs=[hbm, hbm, out_full(*tiles.shape)],
        out_shape=[shape((tokens // 2, two), BF)] * 2 + [shape(tiles.shape, BF)],
        scratch_shapes=[
            pltpu.VMEM((tokens, width), BF),
            pltpu.VMEM((tokens, width), BF),
            pltpu.VMEM((tokens, two), BF),
            pltpu.VMEM((width, two), BF),
            pltpu.SemaphoreType.DMA((32,)),
            pltpu.SemaphoreType.DMA((32,)),
            pltpu.SemaphoreType.DMA((2,)),
        ],
        compiler_params=kernel_params(60),
        cost_estimate=cost(gu_flops + 2 * d_flops, 40 * MIB),
        name="gradients",
    )(
        place, gate_idx, up_idx, down_idx, *dy_pieces, *x_own, *x_core,
        w_d, mult, hidden.reshape(tokens, hid),
    )

    def project(left):
        return lax.dot_general(left, w_gu, (((1,), (1,)), ((), ())), preferred_element_type=F32)

    back_away, terms, y_half = lax.optimization_barrier((back_away, terms, y_half))
    y_half = total(y_half[0]), total(y_half[1])
    dx_away = project(back_away).astype(BF)
    dx_recv = swap(dx_away, "c")
    back_kept, dx_away = lax.optimization_barrier((back_kept, dx_away))
    dx_kept, dx_recv = lax.optimization_barrier((project(back_kept).astype(BF), dx_recv))
    dx_half = lax.optimization_barrier(chip_rows(dx_kept, dx_recv))
    dx_half = total(over_x(dx_half[0])), total(over_z(dx_half[1]))
    x_first, z_first = (jnp.stack(parts, axis=1) for parts in zip(y_half, dx_half))
    summed = lax.psum_scatter(terms, "y", scatter_dimension=0, tiled=True)
    x_first, z_first, summed = lax.optimization_barrier((x_first, z_first, summed))
    x_first, z_first = total(over_z(x_first)), total(over_x(z_first))
    y_seq, dx_seq = (jnp.concatenate([x_first[n], z_first[n]], axis=1) for n in range(2))

    summed = summed.reshape(2, half, per_panel, edge, 2 * edge)
    other = swap(summed[1], "zh")
    low = jnp.where(zh == 0, summed[0], other)
    high = jnp.where(zh == 0, other, summed[0])
    grads = jnp.concatenate([low, high], axis=0)
    gu_grads = grads[:, :kept_here]
    d_gate_vals = gu_grads[..., :edge].reshape(panels, kept_here, square)
    d_up_vals = gu_grads[..., edge:].reshape(panels, kept_here, square)
    d_grads = grads[:, kept_here:].reshape(panels, pairs, edge, 2, edge)
    d_down_vals = jnp.transpose(d_grads, (0, 1, 3, 4, 2)).reshape(panels, kept_here, square)
    return (y_seq, dx_seq, d_gate_vals, d_up_vals, d_down_vals)


def solution(mesh):
    grid = Mesh(mesh.devices.reshape(4, 2, 4, 2, 2), AXES)
    row, col = ("y", "zh"), ("x", "zl", "c")
    tokens = P(row + col, None)
    vals = P(col, row, None)
    idx = P(col, None)
    return jax.shard_map(
        per_device,
        mesh=grid,
        in_specs=(tokens, tokens, vals, idx, vals, idx, vals, idx),
        out_specs=(tokens, tokens, vals, vals, vals),
        check_vma=False,
    )
```

```python
import jax
import jax.numpy as jnp
from jax import lax
from jax.experimental import pallas as pl
from jax.experimental.pallas import tpu as pltpu
from jax.sharding import Mesh, PartitionSpec as P

BLK = 64
AXES = ("y", "zh", "x", "zl", "c")
Z = ("zh", "zl")
ZX = ("zh", "zl", "x")
RING = 4
BF = jnp.bfloat16
F32 = jnp.float32
MIB = 1024 * 1024


def shift(value, axis, step):
    return lax.ppermute(value, axis, [(i, (i + step) % RING) for i in range(RING)])


def swap(value, axis):
    return lax.ppermute(value, axis, [(0, 1), (1, 0)])


def gather_direct(own, axis):
    below = shift(own, axis, 1)
    above = shift(own, axis, -1)
    across = shift(own, axis, 2)
    return [own, above, across, below]


def scatter_direct(chunks, axis):
    return chunks[0], shift(chunks[1], axis, 1), shift(chunks[2], axis, 2), shift(chunks[3], axis, -1)


def total(parts):
    return sum(part.astype(F32) for part in parts).astype(BF)


def add(first, second):
    return (first.astype(F32) + second.astype(F32)).astype(BF)


def left_half(shape):
    return lax.broadcasted_iota(jnp.int32, shape, len(shape) - 1) % (2 * BLK) < BLK


def flip(value):
    return pltpu.roll(value, BLK, 1)


def kernel_params(limit):
    return pltpu.CompilerParams(
        dimension_semantics=("arbitrary",), vmem_limit_bytes=limit * MIB
    )


def row_copies(pieces, buf, sems):
    rows = pieces[0].shape[0]
    return [
        pltpu.make_async_copy(piece, buf.at[pl.ds(n * rows, rows)], sems.at[n])
        for n, piece in enumerate(pieces)
    ]


def owner_row(core, z, x):
    return core * RING * RING + z * RING + x % RING


def chunk_copies(pieces, buf, sems, place):
    per = pieces[0].shape[0] // RING
    copies = []
    for n, piece in enumerate(pieces):
        for x in range(RING):
            at = owner_row(n // RING, n % RING, place[2] + x) * per
            copies.append(
                pltpu.make_async_copy(
                    piece.at[pl.ds(x * per, per)],
                    buf.at[pl.ds(pl.multiple_of(at, per), per)],
                    sems.at[n * RING + x],
                )
            )
    return copies


def ring_copies(pieces, buf, sems, place):
    per = pieces[0].shape[2]
    copies = []
    for n in range(2 * RING * RING):
        core, x, z = n // (RING * RING), n // RING % RING, n % RING
        source = pieces[core].at[(place[2] + x) % RING, (place[1] + z) % RING]
        copies.append(pltpu.make_async_copy(source, buf.at[pl.ds(n * per, per)], sems.at[n]))
    return copies


def tile_wait(copies, i):
    for t in range(len(copies) // 2):

        @pl.when(i == t)
        def _(t=t):
            copies[2 * t].wait()
            copies[2 * t + 1].wait()


class Tiles:
    def __init__(self, half_panels, kept_here, zh):
        self.half_panels, self.kept_here, self.zh = half_panels, kept_here, zh
        self.pairs = kept_here // 2
        self.per_panel = kept_here + self.pairs

    def at(self, group, p, k):
        return (group * self.half_panels + p) * self.per_panel + k

    def kept(self, group, k):
        return (group // 2) * (2 * self.kept_here) + (self.zh ^ (group % 2)) * self.kept_here + k

    def row(self, idx_ref, p, j):
        return pl.multiple_of(idx_ref[self.zh * self.half_panels + p, j] * BLK, BLK)


def put_blocks(w_ref, places):
    mask = left_half((BLK, 2 * BLK))
    old = [w_ref[rows, lanes] for rows, lanes, _, _ in places]
    for before, (rows, lanes, tile, left) in zip(old, places):
        w_ref[rows, lanes] = jnp.where(mask, tile, before) if left else jnp.where(mask, before, tile)


def build_input_weights(where, gate_idx, up_idx, tiles, w_ref):
    w_ref[...] = jnp.zeros_like(w_ref)

    def put(step, carry):
        group, k = step // where.kept_here, step % where.kept_here
        j = where.kept(group, k)
        block = [tiles[where.at(group, p, k)] for p in range(where.half_panels)]
        for idx_ref, left in ((gate_idx, True), (up_idx, False)):
            put_blocks(w_ref, [
                (pl.ds(where.row(idx_ref, p, j), BLK), pl.ds(p * 2 * BLK, 2 * BLK), block[p], left)
                for p in range(where.half_panels)
            ])
        return carry

    lax.fori_loop(0, 2 * RING * where.kept_here, put, 0)


def build_down_weights(where, down_idx, tiles, w_ref):
    w_ref[...] = jnp.zeros_like(w_ref)

    def put(step, carry):
        group, m = step // where.pairs, step % where.pairs
        j = where.kept(group, 2 * m)
        for parity in range(2):
            places = []
            for p in range(parity, where.half_panels, 2):
                tile = tiles[where.at(group, p, where.kept_here + m)]
                for h in range(2):
                    rows = pl.ds(where.row(down_idx, p, j + h), BLK)
                    source = tile if h == parity else flip(tile)
                    places.append((rows, pl.ds((p // 2) * 128, 128), source, parity == 0))
            put_blocks(w_ref, places)
        return carry

    lax.fori_loop(0, 2 * RING * where.pairs, put, 0)


def back_rows(left, w_ref, out_ref, place):
    width = w_ref.shape[0]
    step = min(width, 1024)
    per = out_ref.shape[1]
    for start in range(0, width, step):
        part = lax.dot_general(
            left, w_ref[start : start + step, :], (((1,), (1,)), ((), ())),
            preferred_element_type=F32,
        ).astype(BF)
        for a in range(RING // 2):
            for b in range(RING):
                at = (a * RING + b) * per
                chunk = a * RING + (place[2] + b) % RING
                out_ref[chunk, :, start : start + step] = part[at : at + per]


def forward_tile(half_panels, x_tile, w_ref, m_ref, h_ref, h2_ref):
    rows = x_tile.shape[0]
    both = jnp.dot(x_tile, w_ref[...], preferred_element_type=F32)
    mask = left_half((rows, 2 * BLK))
    per = m_ref.shape[3]
    spans = [(a, b, (a * RING + b) * per) for a in range(RING // 2) for b in range(RING)]
    for first in range(0, half_panels, 2):
        group = [slice(p * 2 * BLK, (p + 1) * 2 * BLK) for p in range(first, min(first + 2, half_panels))]
        low, high = both[:, group[0]], both[:, group[-1]]
        gate = jnp.where(mask, low, flip(high))
        up = jnp.where(mask, flip(low), high)
        sigma = jax.nn.sigmoid(gate)
        silu = gate * sigma
        slope = up * sigma * (1.0 + gate * (1.0 - sigma))
        mults = [jnp.where(mask, slope, flip(silu)), jnp.where(mask, flip(slope), silu)]
        for lanes, mult in zip(group, mults):
            for a, b, at in spans:
                m_ref[0, a, b, :, lanes] = mult[at : at + per]
        hidden = silu * up
        if len(group) == 1:
            hidden = jnp.where(mask, hidden, 0.0)
        hidden = hidden.astype(BF)
        out = slice(first * BLK, (first + 2) * BLK)
        h_ref[:, out] = hidden
        for a, b, at in spans:
            h2_ref[0, b, a, :, out] = hidden[at : at + per]


def forward_kernel(half_panels, kept_here, first, place, *refs):
    if first:
        gate_idx, up_idx, down_idx, tiles = refs[:4]
        pieces, refs = refs[4:8], refs[8:]
        m_ref, h2_ref, y_ref, w_other, wd_other = refs[:5]
    else:
        w_other, wd_other = refs[:2]
        pieces, refs = refs[2:6], refs[8:]
        m_ref, h2_ref, y_ref = refs[:3]
    w_ref, wd_ref, h_ref, buf, sems, w_sems = refs[-6:]
    i = pl.program_id(0)
    rows = buf.shape[0] // 2
    copies = row_copies(pieces, buf, sems)
    pairs = ((w_ref, w_other), (wd_ref, wd_other))
    if not first:
        pairs = [(b, a) for a, b in pairs]
    w_copies = [pltpu.make_async_copy(a, b, w_sems.at[n]) for n, (a, b) in enumerate(pairs)]

    @pl.when(i == 0)
    def _():
        if not first:
            w_copies[0].start()
        for copy in copies:
            copy.start()
        if not first:
            w_copies[1].start()
        if first:
            where = Tiles(half_panels, kept_here, place[0])
            build_input_weights(where, gate_idx, up_idx, tiles, w_ref)
            w_copies[0].start()
            build_down_weights(where, down_idx, tiles, wd_ref)
            w_copies[1].start()
        else:
            w_copies[0].wait()

    tile_wait(copies, i)
    x_tile = buf[pl.ds(pl.multiple_of(i * rows, rows), rows), :]
    forward_tile(half_panels, x_tile, w_ref, m_ref, h_ref, h2_ref)
    if not first:

        @pl.when(i == 0)
        def _():
            w_copies[1].wait()

    back_rows(h_ref[...], wd_ref, y_ref, place)
    if first:

        @pl.when(i == pl.num_programs(0) - 1)
        def _():
            for copy in w_copies:
                copy.wait()


def gradient_kernel(half_panels, kept_here, place, gate_idx, up_idx, down_idx, *refs):
    dy_pieces, x_pieces, refs = refs[:2], refs[2:10], refs[10:]
    wd_ref, m_ref, h_ref, back_kept, back_away, out_ref = refs[:6]
    dy_buf, x_buf, g_ref, acc, dy_sems, x_sems, g_sems = refs[6:]
    i = pl.program_id(0)
    where = Tiles(half_panels, kept_here, place[0])
    rows = dy_buf.shape[0] // 4
    dy_copies = ring_copies(dy_pieces, dy_buf, dy_sems, place)
    x_copies = chunk_copies(x_pieces, x_buf, x_sems, place)
    half_rows = back_kept.shape[0]
    g_copies = [
        pltpu.make_async_copy(g_ref.at[pl.ds(n * half_rows, half_rows)], out, g_sems.at[n])
        for n, out in enumerate((back_kept, back_away))
    ]
    hid = h_ref.shape[1]
    cols = dy_buf.shape[1] // 4
    mask = left_half((rows, 2 * BLK))
    small = left_half((BLK, 2 * BLK))

    @pl.when(i == 0)
    def _():
        for copy in dy_copies:
            copy.start()

    for t in range(4):

        @pl.when(i == t)
        def _(t=t):
            for copy in dy_copies[8 * t : 8 * t + 8]:
                copy.wait()

    @pl.when(i < 4)
    def _():
        dy_tile = dy_buf[pl.ds(pl.multiple_of(i * rows, rows), rows), :]
        d_hidden = jnp.dot(dy_tile, wd_ref[...], preferred_element_type=F32)
        per = m_ref.shape[3]
        for p in range(half_panels):
            if p % 2 == 0:
                here = d_hidden[:, (p // 2) * 128 : (p // 2 + 1) * 128]
                turned = flip(here)
                spread = jnp.where(mask, here, turned)
            else:
                spread = jnp.where(mask, turned, here)
            lanes = slice(p * 2 * BLK, (p + 1) * 2 * BLK)
            for a in range(RING // 2):
                for b in range(RING):
                    at = (a * RING + b) * per
                    chunk = owner_row(i // 2, b, place[2] + (i % 2) * (RING // 2) + a)
                    rows_at = pl.ds(pl.multiple_of(chunk * per, per), per)
                    g_ref[rows_at, lanes] = (
                        spread[at : at + per] * m_ref[0, b, a, :, lanes]
                    ).astype(BF)

    @pl.when((i >= 4) & (i < 8))
    def _():
        at = pl.multiple_of((i - 4) * cols, cols)
        part = lax.dot_general(
            dy_buf[:, pl.ds(at, cols)], h_ref[...], (((0,), (0,)), ((), ())),
            preferred_element_type=F32,
        )
        acc[pl.ds(at, cols), :hid] = part.astype(BF)

    @pl.when(i == 3)
    def _():
        for copy in x_copies:
            copy.start()

    @pl.when(i == 4)
    def _():
        for copy in g_copies:
            copy.start()

    @pl.when(i == 7)
    def _():
        def take(step, carry):
            group, m = step // where.pairs, step % where.pairs
            j = where.kept(group, 2 * m)
            for p in range(half_panels):
                lanes = pl.ds((p // 2) * 128, 128)
                first = acc[pl.ds(where.row(down_idx, p, j), BLK), lanes]
                second = acc[pl.ds(where.row(down_idx, p, j + 1), BLK), lanes]
                if p % 2 == 0:
                    second = flip(second)
                else:
                    first = flip(first)
                out_ref[where.at(group, p, kept_here + m)] = jnp.where(small, first, second)
            return carry

        lax.fori_loop(0, 2 * RING * where.pairs, take, 0)

    @pl.when(i == 8)
    def _():
        for copy in x_copies:
            copy.wait()

    @pl.when(i >= 8)
    def _():
        at = pl.multiple_of((i - 8) * cols, cols)
        part = lax.dot_general(
            x_buf[:, pl.ds(at, cols)], g_ref[...], (((0,), (0,)), ((), ())),
            preferred_element_type=F32,
        )
        acc[pl.ds(at, cols), :] = part.astype(BF)

    @pl.when(i == pl.num_programs(0) - 1)
    def _():
        def take(step, carry):
            group, k = step // kept_here, step % kept_here
            j = where.kept(group, k)
            for p in range(half_panels):
                lanes = pl.ds(p * 2 * BLK, 2 * BLK)
                first = acc[pl.ds(where.row(gate_idx, p, j), BLK), lanes]
                second = acc[pl.ds(where.row(up_idx, p, j), BLK), lanes]
                out_ref[where.at(group, p, k)] = jnp.where(small, first, second)
            return carry

        lax.fori_loop(0, 2 * RING * kept_here, take, 0)
        for copy in g_copies:
            copy.wait()


def cost(flops, nbytes):
    return pl.CostEstimate(flops=flops // 8, bytes_accessed=nbytes // 8, transcendentals=0)


def per_device(x_seq, dy_seq, gate_vals, gate_idx, up_vals, up_idx, down_vals, down_idx):
    panels, kept_here, square = gate_vals.shape
    per, width = x_seq.shape
    edge = BLK
    half = panels // 2
    pairs = kept_here // 2
    per_panel = kept_here + pairs
    zh, z_place = lax.axis_index("zh"), lax.axis_index(Z)
    place = jnp.stack([zh, z_place, lax.axis_index("x")]).astype(jnp.int32)
    shape = jax.ShapeDtypeStruct

    gate_blk = gate_vals.reshape(panels, kept_here, edge, edge)
    up_blk = up_vals.reshape(panels, kept_here, edge, edge)
    pair_gu = jnp.concatenate([gate_blk, up_blk], axis=3)
    down_blk = down_vals.reshape(panels, pairs, 2, edge, edge)
    pair_d = jnp.transpose(down_blk, (0, 1, 4, 2, 3)).reshape(panels, pairs, edge, 2 * edge)
    all_pairs = jnp.concatenate([pair_gu, pair_d], axis=1)
    own = lax.dynamic_slice_in_dim(all_pairs, zh * half, half, 0)
    other = swap(lax.dynamic_slice_in_dim(all_pairs, (1 - zh) * half, half, 0), "zh")

    def gather_all(value, axis):
        wide = jnp.broadcast_to(value[None], (RING, *value.shape))
        return lax.all_to_all(wide, axis, 0, 0, tiled=True)

    dy_row = gather_all(dy_seq, Z)
    x_row = jnp.concatenate(gather_direct(x_seq, "x"), axis=0)
    other, x_row, dy_row = lax.optimization_barrier((other, x_row, dy_row))
    both = jnp.stack([own, other]).reshape(-1, edge, 2 * edge)
    tiles = lax.all_gather(both, "y", axis=0, tiled=True)
    dy_own = gather_all(dy_row, "x")
    x_own = gather_direct(x_row, Z)
    x_core = [swap(v, "c") for v in x_own]
    x_core, dy_own = lax.optimization_barrier((x_core, dy_own))
    dy_core = swap(dy_own, "c")

    tokens = 2 * RING * RING * per
    rows = tokens // 4
    hid = -(-half * edge // 128) * 128
    two = half * 2 * edge
    pair = RING // 2
    once = pl.Buffered(1)
    full = lambda *dims: pl.BlockSpec(dims, lambda i: (0,) * len(dims), pipeline_mode=once)
    out_full = lambda *dims: pl.BlockSpec(dims, lambda i: (0,) * len(dims))
    smem = pl.BlockSpec(memory_space=pltpu.SMEM)
    hbm = pl.BlockSpec(memory_space=pl.ANY)
    ordered = lambda last: (2, RING, RING, per, last)
    gu_flops = 2 * tokens * width * two
    d_flops = 2 * tokens * width * hid
    chunks = (RING * RING, per, width)

    def part(fn, *extra):
        def body(*refs):
            fn(*extra, *refs)

        return body

    def forward(core, first, inputs, name):
        specs = [smem] * 4 + [full(*tiles.shape)] + [hbm] * 4 if first else [smem] + [hbm] * 8
        extra_out = [shape((width, two), BF), shape((width, hid), BF)] if first else []
        return pl.pallas_call(
            part(forward_kernel, half, kept_here, first),
            grid=(2,),
            in_specs=specs,
            out_specs=[
                pl.BlockSpec((1, pair, RING, per, two), lambda i: (core, i, 0, 0, 0)),
                pl.BlockSpec((1, RING, pair, per, hid), lambda i: (core, 0, i, 0, 0)),
                pl.BlockSpec((pair * RING, per, width), lambda i: (i, 0, 0)),
            ] + [hbm] * len(extra_out),
            out_shape=[shape(ordered(two), F32), shape(ordered(hid), BF), shape(chunks, BF)] + extra_out,
            scratch_shapes=[
                pltpu.VMEM((width, two), BF),
                pltpu.VMEM((width, hid), BF),
                pltpu.VMEM((rows, hid), BF),
                pltpu.VMEM((tokens // 2, width), BF),
                pltpu.SemaphoreType.DMA((4,)),
                pltpu.SemaphoreType.DMA((2,)),
            ],
            input_output_aliases={} if first else {7: 0, 8: 1},
            compiler_params=kernel_params(56),
            cost_estimate=cost((gu_flops + d_flops) // 2, 24 * MIB),
            name=name,
        )(place, *inputs)

    mult, hidden, y_away, w_gu, w_d = forward(
        1, True, (gate_idx, up_idx, down_idx, tiles, *x_core), "forward_away"
    )
    y_recv = swap(y_away, "c")
    mult, hidden, y_kept = forward(0, False, (w_gu, w_d, *x_own, mult, hidden), "forward_kept")
    y_kept, dy_core = lax.optimization_barrier((y_kept, dy_core))
    dy_pieces = [v.reshape(RING, RING, per, width) for v in (dy_own, dy_core)]

    def chip_rows(kept, received):
        halves = []
        for first in range(0, width, width // 2):
            split = lambda v: v.reshape(RING, RING, per, width)[..., first : first + width // 2]
            halves.append(add(split(kept), split(received)))
        return jnp.transpose(halves[0], (1, 0, 2, 3)), halves[1]

    def over_x(value):
        return lax.all_to_all(value, "x", 0, 0, tiled=True)

    def over_z(value):
        return scatter_direct([value[n] for n in range(RING)], Z)

    y_half = chip_rows(y_kept, y_recv)
    mult, y_half = lax.optimization_barrier((mult, y_half))
    y_half = over_x(y_half[0]), over_z(y_half[1])

    steps = 12
    x_tile = lambda i: jnp.minimum(i, 3)
    back_kept, back_away, terms = pl.pallas_call(
        part(gradient_kernel, half, kept_here),
        grid=(steps,),
        in_specs=[smem] * 4
        + [hbm] * 10
        + [
            full(width, hid),
            pl.BlockSpec(
                (1, RING, pair, per, two), lambda i: (x_tile(i) // 2, 0, x_tile(i) % 2, 0, 0)
            ),
            full(tokens, hid),
        ],
        out_specs=[hbm, hbm, out_full(*tiles.shape)],
        out_shape=[shape((tokens // 2, two), BF)] * 2 + [shape(tiles.shape, BF)],
        scratch_shapes=[
            pltpu.VMEM((tokens, width), BF),
            pltpu.VMEM((tokens, width), BF),
            pltpu.VMEM((tokens, two), BF),
            pltpu.VMEM((width, two), BF),
            pltpu.SemaphoreType.DMA((32,)),
            pltpu.SemaphoreType.DMA((32,)),
            pltpu.SemaphoreType.DMA((2,)),
        ],
        compiler_params=kernel_params(60),
        cost_estimate=cost(gu_flops + 2 * d_flops, 40 * MIB),
        name="gradients",
    )(
        place, gate_idx, up_idx, down_idx, *dy_pieces, *x_own, *x_core,
        w_d, mult, hidden.reshape(tokens, hid),
    )

    def project(left):
        return lax.dot_general(left, w_gu, (((1,), (1,)), ((), ())), preferred_element_type=F32)

    back_away, terms, y_half = lax.optimization_barrier((back_away, terms, y_half))
    y_half = total(y_half[0]), total(y_half[1])
    dx_away = project(back_away).astype(BF)
    dx_recv = swap(dx_away, "c")
    back_kept, dx_away = lax.optimization_barrier((back_kept, dx_away))
    dx_kept, dx_recv = lax.optimization_barrier((project(back_kept).astype(BF), dx_recv))
    dx_half = lax.optimization_barrier(chip_rows(dx_kept, dx_recv))
    dx_half = total(over_x(dx_half[0])), total(over_z(dx_half[1]))
    x_first, z_first = (jnp.stack(parts, axis=1) for parts in zip(y_half, dx_half))
    summed = lax.psum_scatter(terms, "y", scatter_dimension=0, tiled=True)
    x_first, z_first, summed = lax.optimization_barrier((x_first, z_first, summed))
    x_first, z_first = over_z(x_first), over_x(z_first)

    summed = summed.reshape(2, half, per_panel, edge, 2 * edge)
    other = swap(summed[1], "zh")
    low = jnp.where(zh == 0, summed[0], other)
    high = jnp.where(zh == 0, other, summed[0])
    grads = jnp.concatenate([low, high], axis=0)
    gu_grads = grads[:, :kept_here]
    d_gate_vals = gu_grads[..., :edge].reshape(panels, kept_here, square)
    d_up_vals = gu_grads[..., edge:].reshape(panels, kept_here, square)
    d_grads = grads[:, kept_here:].reshape(panels, pairs, edge, 2, edge)
    d_down_vals = jnp.transpose(d_grads, (0, 1, 3, 4, 2)).reshape(panels, kept_here, square)
    x_first, z_first, d_gate_vals, d_up_vals, d_down_vals = lax.optimization_barrier(
        (x_first, z_first, d_gate_vals, d_up_vals, d_down_vals)
    )
    x_first, z_first = total(x_first), total(z_first)
    y_seq, dx_seq = (jnp.concatenate([x_first[n], z_first[n]], axis=1) for n in range(2))
    return (y_seq, dx_seq, d_gate_vals, d_up_vals, d_down_vals)


def solution(mesh):
    grid = Mesh(mesh.devices.reshape(4, 2, 4, 2, 2), AXES)
    row, col = ("y", "zh"), ("x", "zl", "c")
    tokens = P(row + col, None)
    vals = P(col, row, None)
    idx = P(col, None)
    return jax.shard_map(
        per_device,
        mesh=grid,
        in_specs=(tokens, tokens, vals, idx, vals, idx, vals, idx),
        out_specs=(tokens, tokens, vals, vals, vals),
        check_vma=False,
    )
```

```python
import jax
import jax.numpy as jnp
from jax import lax
from jax.experimental import pallas as pl
from jax.experimental.pallas import tpu as pltpu
from jax.sharding import Mesh, PartitionSpec as P

BLK = 64
AXES = ("y", "zh", "x", "zl", "c")
Z = ("zh", "zl")
ZX = ("zh", "zl", "x")
RING = 4
BF = jnp.bfloat16
F32 = jnp.float32
MIB = 1024 * 1024


def shift(value, axis, step):
    return lax.ppermute(value, axis, [(i, (i + step) % RING) for i in range(RING)])


def swap(value, axis):
    return lax.ppermute(value, axis, [(0, 1), (1, 0)])


def gather_direct(own, axis):
    below = shift(own, axis, 1)
    above = shift(own, axis, -1)
    across = shift(own, axis, 2)
    return [own, above, across, below]


def scatter_direct(chunks, axis):
    return chunks[0], shift(chunks[1], axis, 1), shift(chunks[2], axis, 2), shift(chunks[3], axis, -1)


def total(parts):
    return sum(part.astype(F32) for part in parts).astype(BF)


def add(first, second):
    return (first.astype(F32) + second.astype(F32)).astype(BF)


def left_half(shape):
    return lax.broadcasted_iota(jnp.int32, shape, len(shape) - 1) % (2 * BLK) < BLK


def flip(value):
    return pltpu.roll(value, BLK, 1)


def kernel_params(limit):
    return pltpu.CompilerParams(
        dimension_semantics=("arbitrary",), vmem_limit_bytes=limit * MIB
    )


def row_copies(pieces, buf, sems):
    rows = pieces[0].shape[0]
    return [
        pltpu.make_async_copy(piece, buf.at[pl.ds(n * rows, rows)], sems.at[n])
        for n, piece in enumerate(pieces)
    ]


def owner_row(core, z, x):
    return core * RING * RING + z * RING + x % RING


def chunk_copies(pieces, buf, sems, place):
    per = pieces[0].shape[0] // RING
    copies = []
    for n, piece in enumerate(pieces):
        for x in range(RING):
            at = owner_row(n // RING, n % RING, place[2] + x) * per
            copies.append(
                pltpu.make_async_copy(
                    piece.at[pl.ds(x * per, per)],
                    buf.at[pl.ds(pl.multiple_of(at, per), per)],
                    sems.at[n * RING + x],
                )
            )
    return copies


def ring_copies(pieces, buf, sems, place):
    per = pieces[0].shape[2]
    copies = []
    for n in range(2 * RING * RING):
        core, x, z = n // (RING * RING), n // RING % RING, n % RING
        source = pieces[core].at[(place[2] + x) % RING, (place[1] + z) % RING]
        copies.append(pltpu.make_async_copy(source, buf.at[pl.ds(n * per, per)], sems.at[n]))
    return copies


def tile_wait(copies, i):
    for t in range(len(copies) // 2):

        @pl.when(i == t)
        def _(t=t):
            copies[2 * t].wait()
            copies[2 * t + 1].wait()


class Tiles:
    def __init__(self, half_panels, kept_here, zh):
        self.half_panels, self.kept_here, self.zh = half_panels, kept_here, zh
        self.pairs = kept_here // 2
        self.per_panel = kept_here + self.pairs

    def at(self, group, p, k):
        return (group * self.half_panels + p) * self.per_panel + k

    def kept(self, group, k):
        return (group // 2) * (2 * self.kept_here) + (self.zh ^ (group % 2)) * self.kept_here + k

    def row(self, idx_ref, p, j):
        return pl.multiple_of(idx_ref[self.zh * self.half_panels + p, j] * BLK, BLK)


def put_blocks(w_ref, places):
    mask = left_half((BLK, 2 * BLK))
    old = [w_ref[rows, lanes] for rows, lanes, _, _ in places]
    for before, (rows, lanes, tile, left) in zip(old, places):
        w_ref[rows, lanes] = jnp.where(mask, tile, before) if left else jnp.where(mask, before, tile)


def build_input_weights(where, gate_idx, up_idx, tiles, w_ref):
    w_ref[...] = jnp.zeros_like(w_ref)

    def put(step, carry):
        group, k = step // where.kept_here, step % where.kept_here
        j = where.kept(group, k)
        block = [tiles[where.at(group, p, k)] for p in range(where.half_panels)]
        for idx_ref, left in ((gate_idx, True), (up_idx, False)):
            put_blocks(w_ref, [
                (pl.ds(where.row(idx_ref, p, j), BLK), pl.ds(p * 2 * BLK, 2 * BLK), block[p], left)
                for p in range(where.half_panels)
            ])
        return carry

    lax.fori_loop(0, 2 * RING * where.kept_here, put, 0)


def build_down_weights(where, down_idx, tiles, w_ref):
    w_ref[...] = jnp.zeros_like(w_ref)

    def put(step, carry):
        group, m = step // where.pairs, step % where.pairs
        j = where.kept(group, 2 * m)
        for parity in range(2):
            places = []
            for p in range(parity, where.half_panels, 2):
                tile = tiles[where.at(group, p, where.kept_here + m)]
                for h in range(2):
                    rows = pl.ds(where.row(down_idx, p, j + h), BLK)
                    source = tile if h == parity else flip(tile)
                    places.append((rows, pl.ds((p // 2) * 128, 128), source, parity == 0))
            put_blocks(w_ref, places)
        return carry

    lax.fori_loop(0, 2 * RING * where.pairs, put, 0)


def back_rows(left, w_ref, out_ref, place):
    width = w_ref.shape[0]
    step = min(width, 1024)
    per = out_ref.shape[1]
    for start in range(0, width, step):
        part = lax.dot_general(
            left, w_ref[start : start + step, :], (((1,), (1,)), ((), ())),
            preferred_element_type=F32,
        ).astype(BF)
        for a in range(RING // 2):
            for b in range(RING):
                at = (a * RING + b) * per
                chunk = a * RING + (place[2] + b) % RING
                out_ref[chunk, :, start : start + step] = part[at : at + per]


def forward_tile(half_panels, x_tile, w_ref, m_ref, h_ref, h2_ref):
    rows = x_tile.shape[0]
    both = jnp.dot(x_tile, w_ref[...], preferred_element_type=F32)
    mask = left_half((rows, 2 * BLK))
    per = m_ref.shape[3]
    spans = [(a, b, (a * RING + b) * per) for a in range(RING // 2) for b in range(RING)]
    for first in range(0, half_panels, 2):
        group = [slice(p * 2 * BLK, (p + 1) * 2 * BLK) for p in range(first, min(first + 2, half_panels))]
        low, high = both[:, group[0]], both[:, group[-1]]
        gate = jnp.where(mask, low, flip(high))
        up = jnp.where(mask, flip(low), high)
        sigma = jax.nn.sigmoid(gate)
        silu = gate * sigma
        slope = up * sigma * (1.0 + gate * (1.0 - sigma))
        mults = [jnp.where(mask, slope, flip(silu)), jnp.where(mask, flip(slope), silu)]
        for lanes, mult in zip(group, mults):
            for a, b, at in spans:
                m_ref[0, a, b, :, lanes] = mult[at : at + per]
        hidden = silu * up
        if len(group) == 1:
            hidden = jnp.where(mask, hidden, 0.0)
        hidden = hidden.astype(BF)
        out = slice(first * BLK, (first + 2) * BLK)
        h_ref[:, out] = hidden
        for a, b, at in spans:
            h2_ref[0, b, a, :, out] = hidden[at : at + per]


def forward_kernel(half_panels, kept_here, first, place, *refs):
    if first:
        gate_idx, up_idx, down_idx, tiles = refs[:4]
        pieces, refs = refs[4:8], refs[8:]
        m_ref, h2_ref, y_ref, w_other, wd_other = refs[:5]
    else:
        w_other, wd_other = refs[:2]
        pieces, refs = refs[2:6], refs[8:]
        m_ref, h2_ref, y_ref = refs[:3]
    w_ref, wd_ref, h_ref, buf, sems, w_sems = refs[-6:]
    i = pl.program_id(0)
    rows = buf.shape[0] // 2
    copies = row_copies(pieces, buf, sems)
    pairs = ((w_ref, w_other), (wd_ref, wd_other))
    if not first:
        pairs = [(b, a) for a, b in pairs]
    w_copies = [pltpu.make_async_copy(a, b, w_sems.at[n]) for n, (a, b) in enumerate(pairs)]

    @pl.when(i == 0)
    def _():
        if not first:
            w_copies[0].start()
        for copy in copies:
            copy.start()
        if not first:
            w_copies[1].start()
        if first:
            where = Tiles(half_panels, kept_here, place[0])
            build_input_weights(where, gate_idx, up_idx, tiles, w_ref)
            w_copies[0].start()
            build_down_weights(where, down_idx, tiles, wd_ref)
            w_copies[1].start()
        else:
            w_copies[0].wait()

    tile_wait(copies, i)
    x_tile = buf[pl.ds(pl.multiple_of(i * rows, rows), rows), :]
    forward_tile(half_panels, x_tile, w_ref, m_ref, h_ref, h2_ref)
    if not first:

        @pl.when(i == 0)
        def _():
            w_copies[1].wait()

    back_rows(h_ref[...], wd_ref, y_ref, place)
    if first:

        @pl.when(i == pl.num_programs(0) - 1)
        def _():
            for copy in w_copies:
                copy.wait()


def gradient_kernel(half_panels, kept_here, place, gate_idx, up_idx, down_idx, *refs):
    dy_pieces, x_pieces, refs = refs[:2], refs[2:10], refs[10:]
    wd_ref, m_ref, h_ref, back_kept, back_away, out_ref = refs[:6]
    dy_buf, x_buf, g_ref, acc, dy_sems, x_sems, g_sems = refs[6:]
    i = pl.program_id(0)
    where = Tiles(half_panels, kept_here, place[0])
    rows = dy_buf.shape[0] // 4
    dy_copies = ring_copies(dy_pieces, dy_buf, dy_sems, place)
    x_copies = chunk_copies(x_pieces, x_buf, x_sems, place)
    half_rows = back_kept.shape[0]
    g_copies = [
        pltpu.make_async_copy(g_ref.at[pl.ds(n * half_rows, half_rows)], out, g_sems.at[n])
        for n, out in enumerate((back_kept, back_away))
    ]
    hid = h_ref.shape[1]
    cols = dy_buf.shape[1] // 4
    mask = left_half((rows, 2 * BLK))
    small = left_half((BLK, 2 * BLK))

    @pl.when(i == 0)
    def _():
        for copy in dy_copies:
            copy.start()

    for t in range(4):

        @pl.when(i == t)
        def _(t=t):
            for copy in dy_copies[8 * t : 8 * t + 8]:
                copy.wait()

    @pl.when(i < 4)
    def _():
        dy_tile = dy_buf[pl.ds(pl.multiple_of(i * rows, rows), rows), :]
        d_hidden = jnp.dot(dy_tile, wd_ref[...], preferred_element_type=F32)
        per = m_ref.shape[3]
        for p in range(half_panels):
            if p % 2 == 0:
                here = d_hidden[:, (p // 2) * 128 : (p // 2 + 1) * 128]
                turned = flip(here)
                spread = jnp.where(mask, here, turned)
            else:
                spread = jnp.where(mask, turned, here)
            lanes = slice(p * 2 * BLK, (p + 1) * 2 * BLK)
            for a in range(RING // 2):
                for b in range(RING):
                    at = (a * RING + b) * per
                    chunk = owner_row(i // 2, b, place[2] + (i % 2) * (RING // 2) + a)
                    rows_at = pl.ds(pl.multiple_of(chunk * per, per), per)
                    g_ref[rows_at, lanes] = (
                        spread[at : at + per] * m_ref[0, b, a, :, lanes]
                    ).astype(BF)

    @pl.when((i >= 4) & (i < 8))
    def _():
        at = pl.multiple_of((i - 4) * cols, cols)
        part = lax.dot_general(
            dy_buf[:, pl.ds(at, cols)], h_ref[...], (((0,), (0,)), ((), ())),
            preferred_element_type=F32,
        )
        acc[pl.ds(at, cols), :hid] = part.astype(BF)

    @pl.when(i == 3)
    def _():
        for copy in x_copies:
            copy.start()

    @pl.when(i == 4)
    def _():
        for copy in g_copies:
            copy.start()

    @pl.when(i == 7)
    def _():
        def take(step, carry):
            group, m = step // where.pairs, step % where.pairs
            j = where.kept(group, 2 * m)
            for p in range(half_panels):
                lanes = pl.ds((p // 2) * 128, 128)
                first = acc[pl.ds(where.row(down_idx, p, j), BLK), lanes]
                second = acc[pl.ds(where.row(down_idx, p, j + 1), BLK), lanes]
                if p % 2 == 0:
                    second = flip(second)
                else:
                    first = flip(first)
                out_ref[where.at(group, p, kept_here + m)] = jnp.where(small, first, second)
            return carry

        lax.fori_loop(0, 2 * RING * where.pairs, take, 0)

    @pl.when(i == 8)
    def _():
        for copy in x_copies:
            copy.wait()

    @pl.when(i >= 8)
    def _():
        at = pl.multiple_of((i - 8) * cols, cols)
        part = lax.dot_general(
            x_buf[:, pl.ds(at, cols)], g_ref[...], (((0,), (0,)), ((), ())),
            preferred_element_type=F32,
        )
        acc[pl.ds(at, cols), :] = part.astype(BF)

    @pl.when(i == pl.num_programs(0) - 1)
    def _():
        def take(step, carry):
            group, k = step // kept_here, step % kept_here
            j = where.kept(group, k)
            for p in range(half_panels):
                lanes = pl.ds(p * 2 * BLK, 2 * BLK)
                first = acc[pl.ds(where.row(gate_idx, p, j), BLK), lanes]
                second = acc[pl.ds(where.row(up_idx, p, j), BLK), lanes]
                out_ref[where.at(group, p, k)] = jnp.where(small, first, second)
            return carry

        lax.fori_loop(0, 2 * RING * kept_here, take, 0)
        for copy in g_copies:
            copy.wait()


def cost(flops, nbytes):
    return pl.CostEstimate(flops=flops // 8, bytes_accessed=nbytes // 8, transcendentals=0)


def per_device(x_seq, dy_seq, gate_vals, gate_idx, up_vals, up_idx, down_vals, down_idx):
    panels, kept_here, square = gate_vals.shape
    per, width = x_seq.shape
    edge = BLK
    half = panels // 2
    pairs = kept_here // 2
    per_panel = kept_here + pairs
    zh, z_place = lax.axis_index("zh"), lax.axis_index(Z)
    place = jnp.stack([zh, z_place, lax.axis_index("x")]).astype(jnp.int32)
    shape = jax.ShapeDtypeStruct

    gate_blk = gate_vals.reshape(panels, kept_here, edge, edge)
    up_blk = up_vals.reshape(panels, kept_here, edge, edge)
    pair_gu = jnp.concatenate([gate_blk, up_blk], axis=3)
    down_blk = down_vals.reshape(panels, pairs, 2, edge, edge)
    pair_d = jnp.transpose(down_blk, (0, 1, 4, 2, 3)).reshape(panels, pairs, edge, 2 * edge)
    all_pairs = jnp.concatenate([pair_gu, pair_d], axis=1)
    own = lax.dynamic_slice_in_dim(all_pairs, zh * half, half, 0)
    other = swap(lax.dynamic_slice_in_dim(all_pairs, (1 - zh) * half, half, 0), "zh")

    def gather_all(value, axis):
        wide = jnp.broadcast_to(value[None], (RING, *value.shape))
        return lax.all_to_all(wide, axis, 0, 0, tiled=True)

    dy_row = gather_all(dy_seq, Z)
    x_row = jnp.concatenate(gather_direct(x_seq, "x"), axis=0)
    other, x_row, dy_row = lax.optimization_barrier((other, x_row, dy_row))
    both = jnp.stack([own, other]).reshape(-1, edge, 2 * edge)
    tiles = lax.all_gather(both, "y", axis=0, tiled=True)
    dy_own = gather_all(dy_row, "x")
    x_own = gather_direct(x_row, Z)
    x_core = [swap(v, "c") for v in x_own]
    x_core, dy_own = lax.optimization_barrier((x_core, dy_own))
    dy_core = swap(dy_own, "c")

    tokens = 2 * RING * RING * per
    rows = tokens // 4
    hid = -(-half * edge // 128) * 128
    two = half * 2 * edge
    pair = RING // 2
    once = pl.Buffered(1)
    full = lambda *dims: pl.BlockSpec(dims, lambda i: (0,) * len(dims), pipeline_mode=once)
    out_full = lambda *dims: pl.BlockSpec(dims, lambda i: (0,) * len(dims))
    smem = pl.BlockSpec(memory_space=pltpu.SMEM)
    hbm = pl.BlockSpec(memory_space=pl.ANY)
    ordered = lambda last: (2, RING, RING, per, last)
    gu_flops = 2 * tokens * width * two
    d_flops = 2 * tokens * width * hid
    chunks = (RING * RING, per, width)

    def part(fn, *extra):
        def body(*refs):
            fn(*extra, *refs)

        return body

    def forward(core, first, inputs, name):
        specs = [smem] * 4 + [full(*tiles.shape)] + [hbm] * 4 if first else [smem] + [hbm] * 8
        extra_out = [shape((width, two), BF), shape((width, hid), BF)] if first else []
        return pl.pallas_call(
            part(forward_kernel, half, kept_here, first),
            grid=(2,),
            in_specs=specs,
            out_specs=[
                pl.BlockSpec((1, pair, RING, per, two), lambda i: (core, i, 0, 0, 0)),
                pl.BlockSpec((1, RING, pair, per, hid), lambda i: (core, 0, i, 0, 0)),
                pl.BlockSpec((pair * RING, per, width), lambda i: (i, 0, 0)),
            ] + [hbm] * len(extra_out),
            out_shape=[shape(ordered(two), F32), shape(ordered(hid), BF), shape(chunks, BF)] + extra_out,
            scratch_shapes=[
                pltpu.VMEM((width, two), BF),
                pltpu.VMEM((width, hid), BF),
                pltpu.VMEM((rows, hid), BF),
                pltpu.VMEM((tokens // 2, width), BF),
                pltpu.SemaphoreType.DMA((4,)),
                pltpu.SemaphoreType.DMA((2,)),
            ],
            input_output_aliases={} if first else {7: 0, 8: 1},
            compiler_params=kernel_params(56),
            cost_estimate=cost((gu_flops + d_flops) // 2, 24 * MIB),
            name=name,
        )(place, *inputs)

    mult, hidden, y_away, w_gu, w_d = forward(
        1, True, (gate_idx, up_idx, down_idx, tiles, *x_core), "forward_away"
    )
    y_recv = swap(y_away, "c")
    mult, hidden, y_kept = forward(0, False, (w_gu, w_d, *x_own, mult, hidden), "forward_kept")
    y_kept, dy_core = lax.optimization_barrier((y_kept, dy_core))
    dy_pieces = [v.reshape(RING, RING, per, width) for v in (dy_own, dy_core)]

    def chip_rows(kept, received):
        halves = []
        for first in range(0, width, width // 2):
            split = lambda v: v.reshape(RING, RING, per, width)[..., first : first + width // 2]
            halves.append(add(split(kept), split(received)))
        return jnp.transpose(halves[0], (1, 0, 2, 3)), halves[1]

    def over_x(value):
        return lax.all_to_all(value, "x", 0, 0, tiled=True)

    def over_z(value):
        return scatter_direct([value[n] for n in range(RING)], Z)

    y_half = chip_rows(y_kept, y_recv)
    mult, y_half = lax.optimization_barrier((mult, y_half))
    y_half = over_x(y_half[0]), over_z(y_half[1])

    steps = 12
    x_tile = lambda i: jnp.minimum(i, 3)
    back_kept, back_away, terms = pl.pallas_call(
        part(gradient_kernel, half, kept_here),
        grid=(steps,),
        in_specs=[smem] * 4
        + [hbm] * 10
        + [
            full(width, hid),
            pl.BlockSpec(
                (1, RING, pair, per, two), lambda i: (x_tile(i) // 2, 0, x_tile(i) % 2, 0, 0)
            ),
            full(tokens, hid),
        ],
        out_specs=[hbm, hbm, out_full(*tiles.shape)],
        out_shape=[shape((tokens // 2, two), BF)] * 2 + [shape(tiles.shape, BF)],
        scratch_shapes=[
            pltpu.VMEM((tokens, width), BF),
            pltpu.VMEM((tokens, width), BF),
            pltpu.VMEM((tokens, two), BF),
            pltpu.VMEM((width, two), BF),
            pltpu.SemaphoreType.DMA((32,)),
            pltpu.SemaphoreType.DMA((32,)),
            pltpu.SemaphoreType.DMA((2,)),
        ],
        compiler_params=kernel_params(60),
        cost_estimate=cost(gu_flops + 2 * d_flops, 40 * MIB),
        name="gradients",
    )(
        place, gate_idx, up_idx, down_idx, *dy_pieces, *x_own, *x_core,
        w_d, mult, hidden.reshape(tokens, hid),
    )

    def project(left):
        return lax.dot_general(left, w_gu, (((1,), (1,)), ((), ())), preferred_element_type=F32)

    back_away, terms, y_half = lax.optimization_barrier((back_away, terms, y_half))
    y_half = total(y_half[0]), total(y_half[1])
    dx_away = project(back_away).astype(BF)
    dx_recv = swap(dx_away, "c")
    back_kept, dx_away = lax.optimization_barrier((back_kept, dx_away))
    dx_kept, dx_recv = lax.optimization_barrier((project(back_kept).astype(BF), dx_recv))
    dx_half = lax.optimization_barrier(chip_rows(dx_kept, dx_recv))
    dx_half = total(over_x(dx_half[0])), total(over_z(dx_half[1]))
    x_first, z_first = (jnp.stack(parts, axis=1) for parts in zip(y_half, dx_half))
    summed = lax.psum_scatter(terms, "y", scatter_dimension=0, tiled=True)
    x_first, z_first, summed = lax.optimization_barrier((x_first, z_first, summed))
    x_first, z_first = over_z(x_first), over_x(z_first)

    summed = summed.reshape(2, half, per_panel, edge, 2 * edge)

    def both_halves(mine, theirs):
        low = jnp.where(zh == 0, mine, theirs)
        high = jnp.where(zh == 0, theirs, mine)
        return jnp.concatenate([low, high], axis=0)

    theirs = swap(summed[1, :, :kept_here], "zh")
    theirs_down = swap(summed[1, :, kept_here:], "zh")
    gu_grads = both_halves(summed[0, :, :kept_here], theirs)
    d_gate_vals = gu_grads[..., :edge].reshape(panels, kept_here, square)
    d_up_vals = gu_grads[..., edge:].reshape(panels, kept_here, square)
    d_gate_vals, d_up_vals, theirs_down = lax.optimization_barrier(
        (d_gate_vals, d_up_vals, theirs_down)
    )
    d_grads = both_halves(summed[0, :, kept_here:], theirs_down)
    d_grads = d_grads.reshape(panels, pairs, edge, 2, edge)
    d_down_vals = jnp.transpose(d_grads, (0, 1, 3, 4, 2)).reshape(panels, kept_here, square)
    x_first, z_first, d_gate_vals, d_up_vals, d_down_vals = lax.optimization_barrier(
        (x_first, z_first, d_gate_vals, d_up_vals, d_down_vals)
    )
    x_first, z_first = total(x_first), total(z_first)
    y_seq, dx_seq = (jnp.concatenate([x_first[n], z_first[n]], axis=1) for n in range(2))
    return (y_seq, dx_seq, d_gate_vals, d_up_vals, d_down_vals)


def solution(mesh):
    grid = Mesh(mesh.devices.reshape(4, 2, 4, 2, 2), AXES)
    row, col = ("y", "zh"), ("x", "zl", "c")
    tokens = P(row + col, None)
    vals = P(col, row, None)
    idx = P(col, None)
    return jax.shard_map(
        per_device,
        mesh=grid,
        in_specs=(tokens, tokens, vals, idx, vals, idx, vals, idx),
        out_specs=(tokens, tokens, vals, vals, vals),
        check_vma=False,
    )
```

```python
import jax
import jax.numpy as jnp
from jax import lax
from jax.experimental import pallas as pl
from jax.experimental.pallas import tpu as pltpu
from jax.sharding import Mesh, PartitionSpec as P

BLK = 64
AXES = ("y", "zh", "x", "zl", "c")
Z = ("zh", "zl")
ZX = ("zh", "zl", "x")
RING = 4
BF = jnp.bfloat16
F32 = jnp.float32
MIB = 1024 * 1024


def shift(value, axis, step):
    return lax.ppermute(value, axis, [(i, (i + step) % RING) for i in range(RING)])


def swap(value, axis):
    return lax.ppermute(value, axis, [(0, 1), (1, 0)])


def gather_direct(own, axis):
    below = shift(own, axis, 1)
    above = shift(own, axis, -1)
    across = shift(own, axis, 2)
    return [own, above, across, below]


def scatter_parts(chunks, axis):
    return chunks[0], shift(chunks[1], axis, 1), shift(chunks[3], axis, -1), shift(chunks[2], axis, 2)


def total(parts):
    return sum(part.astype(F32) for part in parts).astype(BF)


def scatter_direct(chunks, axis):
    return total(scatter_parts(chunks, axis))


def add(first, second):
    return (first.astype(F32) + second.astype(F32)).astype(BF)


def left_half(shape):
    return lax.broadcasted_iota(jnp.int32, shape, len(shape) - 1) % (2 * BLK) < BLK


def flip(value):
    return pltpu.roll(value, BLK, 1)


def kernel_params(limit):
    return pltpu.CompilerParams(
        dimension_semantics=("arbitrary",), vmem_limit_bytes=limit * MIB
    )


def row_copies(pieces, buf, sems):
    rows = pieces[0].shape[0]
    return [
        pltpu.make_async_copy(piece, buf.at[pl.ds(n * rows, rows)], sems.at[n])
        for n, piece in enumerate(pieces)
    ]


def owner_row(core, z, x):
    return core * RING * RING + z * RING + x % RING


def chunk_copies(pieces, buf, sems, place):
    per = pieces[0].shape[0] // RING
    copies = []
    for n, piece in enumerate(pieces):
        for x in range(RING):
            at = owner_row(n // RING, n % RING, place[2] + x) * per
            copies.append(
                pltpu.make_async_copy(
                    piece.at[pl.ds(x * per, per)],
                    buf.at[pl.ds(pl.multiple_of(at, per), per)],
                    sems.at[n * RING + x],
                )
            )
    return copies


def ring_copies(pieces, buf, sems, place):
    per = pieces[0].shape[2]
    copies = []
    for n in range(2 * RING * RING):
        core, x, z = n // (RING * RING), n // RING % RING, n % RING
        source = pieces[core].at[(place[2] + x) % RING, (place[1] + z) % RING]
        copies.append(pltpu.make_async_copy(source, buf.at[pl.ds(n * per, per)], sems.at[n]))
    return copies


def tile_wait(copies, i):
    for t in range(len(copies) // 2):

        @pl.when(i == t)
        def _(t=t):
            copies[2 * t].wait()
            copies[2 * t + 1].wait()


class Tiles:
    def __init__(self, half_panels, kept_here, zh):
        self.half_panels, self.kept_here, self.zh = half_panels, kept_here, zh
        self.pairs = kept_here // 2
        self.per_panel = kept_here + self.pairs

    def at(self, group, p, k):
        return (group * self.half_panels + p) * self.per_panel + k

    def kept(self, group, k):
        return (group // 2) * (2 * self.kept_here) + (self.zh ^ (group % 2)) * self.kept_here + k

    def row(self, idx_ref, p, j):
        return pl.multiple_of(idx_ref[self.zh * self.half_panels + p, j] * BLK, BLK)


def put_blocks(w_ref, places):
    mask = left_half((BLK, 2 * BLK))
    old = [w_ref[rows, lanes] for rows, lanes, _, _ in places]
    for before, (rows, lanes, tile, left) in zip(old, places):
        w_ref[rows, lanes] = jnp.where(mask, tile, before) if left else jnp.where(mask, before, tile)


def build_input_weights(where, gate_idx, up_idx, tiles, w_ref):
    w_ref[...] = jnp.zeros_like(w_ref)

    def put(step, carry):
        group, k = step // where.kept_here, step % where.kept_here
        j = where.kept(group, k)
        block = [tiles[where.at(group, p, k)] for p in range(where.half_panels)]
        for idx_ref, left in ((gate_idx, True), (up_idx, False)):
            put_blocks(w_ref, [
                (pl.ds(where.row(idx_ref, p, j), BLK), pl.ds(p * 2 * BLK, 2 * BLK), block[p], left)
                for p in range(where.half_panels)
            ])
        return carry

    lax.fori_loop(0, 2 * RING * where.kept_here, put, 0)


def build_down_weights(where, down_idx, tiles, w_ref):
    w_ref[...] = jnp.zeros_like(w_ref)

    def put(step, carry):
        group, m = step // where.pairs, step % where.pairs
        j = where.kept(group, 2 * m)
        for parity in range(2):
            places = []
            for p in range(parity, where.half_panels, 2):
                tile = tiles[where.at(group, p, where.kept_here + m)]
                for h in range(2):
                    rows = pl.ds(where.row(down_idx, p, j + h), BLK)
                    source = tile if h == parity else flip(tile)
                    places.append((rows, pl.ds((p // 2) * 128, 128), source, parity == 0))
            put_blocks(w_ref, places)
        return carry

    lax.fori_loop(0, 2 * RING * where.pairs, put, 0)


def back_rows(left, w_ref, out_ref):
    width = w_ref.shape[0]
    step = min(width, 1024)
    per = out_ref.shape[1]
    for start in range(0, width, step):
        part = lax.dot_general(
            left, w_ref[start : start + step, :], (((1,), (1,)), ((), ())),
            preferred_element_type=F32,
        ).astype(BF)
        for a in range(RING // 2):
            for b in range(RING):
                at = (a * RING + b) * per
                chunk = a * RING + b
                out_ref[chunk, :, start : start + step] = part[at : at + per]


def forward_tile(half_panels, x_tile, w_ref, m_ref, h_ref, h2_ref):
    rows = x_tile.shape[0]
    both = jnp.dot(x_tile, w_ref[...], preferred_element_type=F32)
    mask = left_half((rows, 2 * BLK))
    per = m_ref.shape[3]
    spans = [(a, b, (a * RING + b) * per) for a in range(RING // 2) for b in range(RING)]
    for first in range(0, half_panels, 2):
        group = [slice(p * 2 * BLK, (p + 1) * 2 * BLK) for p in range(first, min(first + 2, half_panels))]
        low, high = both[:, group[0]], both[:, group[-1]]
        gate = jnp.where(mask, low, flip(high))
        up = jnp.where(mask, flip(low), high)
        sigma = jax.nn.sigmoid(gate)
        silu = gate * sigma
        slope = up * sigma * (1.0 + gate * (1.0 - sigma))
        mults = [jnp.where(mask, slope, flip(silu)), jnp.where(mask, flip(slope), silu)]
        for lanes, mult in zip(group, mults):
            for a, b, at in spans:
                m_ref[0, a, b, :, lanes] = mult[at : at + per]
        hidden = silu * up
        if len(group) == 1:
            hidden = jnp.where(mask, hidden, 0.0)
        hidden = hidden.astype(BF)
        out = slice(first * BLK, (first + 2) * BLK)
        h_ref[:, out] = hidden
        for a, b, at in spans:
            h2_ref[0, b, a, :, out] = hidden[at : at + per]


def forward_kernel(half_panels, kept_here, first, place, *refs):
    if first:
        gate_idx, up_idx, down_idx, tiles = refs[:4]
        pieces, refs = refs[4:8], refs[8:]
        m_ref, h2_ref, y_ref, w_other, wd_other = refs[:5]
    else:
        w_other, wd_other = refs[:2]
        pieces, refs = refs[2:6], refs[8:]
        m_ref, h2_ref, y_ref = refs[:3]
    w_ref, wd_ref, h_ref, buf, sems, w_sems = refs[-6:]
    i = pl.program_id(0)
    rows = buf.shape[0] // 2
    copies = row_copies(pieces, buf, sems)
    pairs = ((w_ref, w_other), (wd_ref, wd_other))
    if not first:
        pairs = [(b, a) for a, b in pairs]
    w_copies = [pltpu.make_async_copy(a, b, w_sems.at[n]) for n, (a, b) in enumerate(pairs)]

    @pl.when(i == 0)
    def _():
        if not first:
            w_copies[0].start()
        for copy in copies:
            copy.start()
        if not first:
            w_copies[1].start()
        if first:
            where = Tiles(half_panels, kept_here, place[0])
            build_input_weights(where, gate_idx, up_idx, tiles, w_ref)
            w_copies[0].start()
            build_down_weights(where, down_idx, tiles, wd_ref)
            w_copies[1].start()
        else:
            w_copies[0].wait()

    tile_wait(copies, i)
    x_tile = buf[pl.ds(pl.multiple_of(i * rows, rows), rows), :]
    forward_tile(half_panels, x_tile, w_ref, m_ref, h_ref, h2_ref)
    if not first:

        @pl.when(i == 0)
        def _():
            w_copies[1].wait()

    back_rows(h_ref[...], wd_ref, y_ref)
    if first:

        @pl.when(i == pl.num_programs(0) - 1)
        def _():
            for copy in w_copies:
                copy.wait()


def gradient_kernel(half_panels, kept_here, place, gate_idx, up_idx, down_idx, *refs):
    dy_pieces, x_pieces, refs = refs[:2], refs[2:10], refs[10:]
    wd_ref, m_ref, h_ref, w_gu, back_kept, dx_away, out_ref = refs[:7]
    dy_buf, x_buf, g_ref, acc, w_ref, dy_sems, x_sems, g_sems = refs[7:]
    i = pl.program_id(0)
    where = Tiles(half_panels, kept_here, place[0])
    rows = dy_buf.shape[0] // 4
    dy_copies = ring_copies(dy_pieces, dy_buf, dy_sems, place)
    x_copies = chunk_copies(x_pieces, x_buf, x_sems, place)
    w_copy = pltpu.make_async_copy(w_gu, w_ref, g_sems.at[2])
    half_rows = back_kept.shape[0]
    g_copy = pltpu.make_async_copy(g_ref.at[pl.ds(0, half_rows)], back_kept, g_sems.at[0])
    dx_copy = pltpu.make_async_copy(dy_buf.at[pl.ds(0, half_rows)], dx_away, g_sems.at[1])
    hid = h_ref.shape[1]
    cols = dy_buf.shape[1] // 4
    mask = left_half((rows, 2 * BLK))
    small = left_half((BLK, 2 * BLK))

    @pl.when(i == 0)
    def _():
        for copy in dy_copies:
            copy.start()

    for t in range(4):

        @pl.when(i == t)
        def _(t=t):
            for copy in dy_copies[8 * t : 8 * t + 8]:
                copy.wait()

    @pl.when(i < 4)
    def _():
        dy_tile = dy_buf[pl.ds(pl.multiple_of(i * rows, rows), rows), :]
        d_hidden = jnp.dot(dy_tile, wd_ref[...], preferred_element_type=F32)
        per = m_ref.shape[3]
        for p in range(half_panels):
            if p % 2 == 0:
                here = d_hidden[:, (p // 2) * 128 : (p // 2 + 1) * 128]
                turned = flip(here)
                spread = jnp.where(mask, here, turned)
            else:
                spread = jnp.where(mask, turned, here)
            lanes = slice(p * 2 * BLK, (p + 1) * 2 * BLK)
            for a in range(RING // 2):
                for b in range(RING):
                    at = (a * RING + b) * per
                    chunk = owner_row(i // 2, b, place[2] + (i % 2) * (RING // 2) + a)
                    rows_at = pl.ds(pl.multiple_of(chunk * per, per), per)
                    g_ref[rows_at, lanes] = (
                        spread[at : at + per] * m_ref[0, b, a, :, lanes]
                    ).astype(BF)

    @pl.when((i >= 4) & (i < 8))
    def _():
        at = pl.multiple_of((i - 4) * cols, cols)
        part = lax.dot_general(
            dy_buf[:, pl.ds(at, cols)], h_ref[...], (((0,), (0,)), ((), ())),
            preferred_element_type=F32,
        )
        acc[pl.ds(at, cols), :hid] = part.astype(BF)

    @pl.when(i == 3)
    def _():
        w_copy.start()
        for copy in x_copies:
            copy.start()

    @pl.when(i == 4)
    def _():
        g_copy.start()

    @pl.when(i == 7)
    def _():
        def take(step, carry):
            group, m = step // where.pairs, step % where.pairs
            j = where.kept(group, 2 * m)
            for p in range(half_panels):
                lanes = pl.ds((p // 2) * 128, 128)
                first = acc[pl.ds(where.row(down_idx, p, j), BLK), lanes]
                second = acc[pl.ds(where.row(down_idx, p, j + 1), BLK), lanes]
                if p % 2 == 0:
                    second = flip(second)
                else:
                    first = flip(first)
                out_ref[where.at(group, p, kept_here + m)] = jnp.where(small, first, second)
            return carry

        lax.fori_loop(0, 2 * RING * where.pairs, take, 0)

    @pl.when(i == 8)
    def _():
        w_copy.wait()

    @pl.when((i >= 8) & (i < 12))
    def _():
        at = pl.multiple_of((i - 8) * cols, cols)
        part = lax.dot_general(
            g_ref[half_rows:, :], w_ref[pl.ds(at, cols), :], (((1,), (1,)), ((), ())),
            preferred_element_type=F32,
        )
        dy_buf[:half_rows, pl.ds(at, cols)] = part.astype(BF)

    @pl.when(i == 12)
    def _():
        dx_copy.start()
        for copy in x_copies:
            copy.wait()

    @pl.when(i >= 12)
    def _():
        at = pl.multiple_of((i - 12) * cols, cols)
        part = lax.dot_general(
            x_buf[:, pl.ds(at, cols)], g_ref[...], (((0,), (0,)), ((), ())),
            preferred_element_type=F32,
        )
        acc[pl.ds(at, cols), :] = part.astype(BF)

    @pl.when(i == pl.num_programs(0) - 1)
    def _():
        def take(step, carry):
            group, k = step // kept_here, step % kept_here
            j = where.kept(group, k)
            for p in range(half_panels):
                lanes = pl.ds(p * 2 * BLK, 2 * BLK)
                first = acc[pl.ds(where.row(gate_idx, p, j), BLK), lanes]
                second = acc[pl.ds(where.row(up_idx, p, j), BLK), lanes]
                out_ref[where.at(group, p, k)] = jnp.where(small, first, second)
            return carry

        lax.fori_loop(0, 2 * RING * kept_here, take, 0)
        g_copy.wait()
        dx_copy.wait()


def cost(flops, nbytes):
    return pl.CostEstimate(flops=flops // 8, bytes_accessed=nbytes // 8, transcendentals=0)


def per_device(x_seq, dy_seq, gate_vals, gate_idx, up_vals, up_idx, down_vals, down_idx):
    panels, kept_here, square = gate_vals.shape
    per, width = x_seq.shape
    edge = BLK
    half = panels // 2
    pairs = kept_here // 2
    per_panel = kept_here + pairs
    zh, z_place = lax.axis_index("zh"), lax.axis_index(Z)
    place = jnp.stack([zh, z_place, lax.axis_index("x")]).astype(jnp.int32)
    shape = jax.ShapeDtypeStruct

    gate_blk = gate_vals.reshape(panels, kept_here, edge, edge)
    up_blk = up_vals.reshape(panels, kept_here, edge, edge)
    pair_gu = jnp.concatenate([gate_blk, up_blk], axis=3)
    down_blk = down_vals.reshape(panels, pairs, 2, edge, edge)
    pair_d = jnp.transpose(down_blk, (0, 1, 4, 2, 3)).reshape(panels, pairs, edge, 2 * edge)
    all_pairs = jnp.concatenate([pair_gu, pair_d], axis=1)
    own = lax.dynamic_slice_in_dim(all_pairs, zh * half, half, 0)
    other = swap(lax.dynamic_slice_in_dim(all_pairs, (1 - zh) * half, half, 0), "zh")

    def gather_all(value, axis):
        wide = jnp.broadcast_to(value[None], (RING, *value.shape))
        return lax.all_to_all(wide, axis, 0, 0, tiled=True)

    dy_row = gather_all(dy_seq, Z)
    x_row = jnp.concatenate(gather_direct(x_seq, "x"), axis=0)
    other, x_row, dy_row = lax.optimization_barrier((other, x_row, dy_row))
    both = jnp.stack([own, other]).reshape(-1, edge, 2 * edge)
    tiles = lax.all_gather(both, "y", axis=0, tiled=True)
    dy_own = gather_all(dy_row, "x")
    x_own = gather_direct(x_row, Z)
    x_core = [swap(v, "c") for v in x_own]
    x_core, dy_own = lax.optimization_barrier((x_core, dy_own))
    dy_core = swap(dy_own, "c")

    tokens = 2 * RING * RING * per
    rows = tokens // 4
    hid = -(-half * edge // 128) * 128
    two = half * 2 * edge
    pair = RING // 2
    once = pl.Buffered(1)
    full = lambda *dims: pl.BlockSpec(dims, lambda i: (0,) * len(dims), pipeline_mode=once)
    out_full = lambda *dims: pl.BlockSpec(dims, lambda i: (0,) * len(dims))
    smem = pl.BlockSpec(memory_space=pltpu.SMEM)
    hbm = pl.BlockSpec(memory_space=pl.ANY)
    ordered = lambda last: (2, RING, RING, per, last)
    gu_flops = 2 * tokens * width * two
    d_flops = 2 * tokens * width * hid
    chunks = (RING * RING, per, width)

    def part(fn, *extra):
        def body(*refs):
            fn(*extra, *refs)

        return body

    def forward(core, first, inputs, name):
        specs = [smem] * 4 + [full(*tiles.shape)] + [hbm] * 4 if first else [smem] + [hbm] * 8
        extra_out = [shape((width, two), BF), shape((width, hid), BF)] if first else []
        return pl.pallas_call(
            part(forward_kernel, half, kept_here, first),
            grid=(2,),
            in_specs=specs,
            out_specs=[
                pl.BlockSpec((1, pair, RING, per, two), lambda i: (core, i, 0, 0, 0)),
                pl.BlockSpec((1, RING, pair, per, hid), lambda i: (core, 0, i, 0, 0)),
                pl.BlockSpec((pair * RING, per, width), lambda i: (i, 0, 0)),
            ] + [hbm] * len(extra_out),
            out_shape=[shape(ordered(two), F32), shape(ordered(hid), BF), shape(chunks, BF)] + extra_out,
            scratch_shapes=[
                pltpu.VMEM((width, two), BF),
                pltpu.VMEM((width, hid), BF),
                pltpu.VMEM((rows, hid), BF),
                pltpu.VMEM((tokens // 2, width), BF),
                pltpu.SemaphoreType.DMA((4,)),
                pltpu.SemaphoreType.DMA((2,)),
            ],
            input_output_aliases={} if first else {7: 0, 8: 1},
            compiler_params=kernel_params(56),
            cost_estimate=cost((gu_flops + d_flops) // 2, 24 * MIB),
            name=name,
        )(place, *inputs)

    mult, hidden, y_away, w_gu, w_d = forward(
        1, True, (gate_idx, up_idx, down_idx, tiles, *x_core), "forward_away"
    )
    y_recv = swap(y_away, "c")
    mult, hidden, y_kept = forward(0, False, (w_gu, w_d, *x_own, mult, hidden), "forward_kept")
    y_kept, dy_core = lax.optimization_barrier((y_kept, dy_core))
    dy_pieces = [v.reshape(RING, RING, per, width) for v in (dy_own, dy_core)]
    y_sum = [add(y_kept[n * RING : n * RING + RING], y_recv[n * RING : n * RING + RING]) for n in range(RING)]
    mult, y_sum = lax.optimization_barrier((mult, y_sum))
    y_z = scatter_direct(y_sum, Z)

    steps = 16
    x_tile = lambda i: jnp.minimum(i, 3)
    back_kept, dx_away, terms = pl.pallas_call(
        part(gradient_kernel, half, kept_here),
        grid=(steps,),
        in_specs=[smem] * 4
        + [hbm] * 10
        + [
            full(width, hid),
            pl.BlockSpec(
                (1, RING, pair, per, two), lambda i: (x_tile(i) // 2, 0, x_tile(i) % 2, 0, 0)
            ),
            full(tokens, hid),
            hbm,
        ],
        out_specs=[hbm, hbm, out_full(*tiles.shape)],
        out_shape=[
            shape((tokens // 2, two), BF),
            shape((tokens // 2, width), BF),
            shape(tiles.shape, BF),
        ],
        scratch_shapes=[
            pltpu.VMEM((tokens, width), BF),
            pltpu.VMEM((tokens, width), BF),
            pltpu.VMEM((tokens, two), BF),
            pltpu.VMEM((width, two), BF),
            pltpu.VMEM((width, two), BF),
            pltpu.SemaphoreType.DMA((32,)),
            pltpu.SemaphoreType.DMA((32,)),
            pltpu.SemaphoreType.DMA((3,)),
        ],
        compiler_params=kernel_params(60),
        cost_estimate=cost(gu_flops + 2 * d_flops, 40 * MIB),
        name="gradients",
    )(
        place, gate_idx, up_idx, down_idx, *dy_pieces, *x_own, *x_core,
        w_d, mult, hidden.reshape(tokens, hid), w_gu,
    )

    def project(left):
        return lax.dot_general(left, w_gu, (((1,), (1,)), ((), ())), preferred_element_type=F32)

    back_kept, dx_away, terms, y_z = lax.optimization_barrier((back_kept, dx_away, terms, y_z))
    dx_recv = swap(dx_away, "c")
    dx_kept, dx_recv = lax.optimization_barrier((project(back_kept).astype(BF), dx_recv))

    def chip_rows(first, count):
        split = lambda v: v[:, first : first + count].reshape(RING, RING, per, count)
        return add(split(dx_kept), split(dx_recv))

    def over_x(value):
        return jnp.sum(lax.all_to_all(value, "x", 0, 0, tiled=True).astype(F32), axis=0).astype(BF)

    x_first = jnp.transpose(chip_rows(0, width // 2), (1, 0, 2, 3))
    z_first = chip_rows(width // 2, width // 2)
    y_z, x_first, z_first = lax.optimization_barrier((y_z, x_first, z_first))
    x_first = over_x(x_first)
    z_first = scatter_direct([z_first[n] for n in range(RING)], Z)
    y_seq = scatter_direct([y_z[n] for n in range(RING)], "x")
    x_first, z_first, y_seq = lax.optimization_barrier((x_first, z_first, y_seq))
    x_first = scatter_direct([x_first[n] for n in range(RING)], Z)
    z_first = over_x(z_first)
    dx_seq = jnp.concatenate([x_first, z_first], axis=1)

    summed = lax.psum_scatter(terms, "y", scatter_dimension=0, tiled=True)
    summed = summed.reshape(2, half, per_panel, edge, 2 * edge)
    other = swap(summed[1], "zh")
    low = jnp.where(zh == 0, summed[0], other)
    high = jnp.where(zh == 0, other, summed[0])
    grads = jnp.concatenate([low, high], axis=0)
    gu_grads = grads[:, :kept_here]
    d_gate_vals = gu_grads[..., :edge].reshape(panels, kept_here, square)
    d_up_vals = gu_grads[..., edge:].reshape(panels, kept_here, square)
    d_grads = grads[:, kept_here:].reshape(panels, pairs, edge, 2, edge)
    d_down_vals = jnp.transpose(d_grads, (0, 1, 3, 4, 2)).reshape(panels, kept_here, square)
    return (y_seq, dx_seq, d_gate_vals, d_up_vals, d_down_vals)


def solution(mesh):
    grid = Mesh(mesh.devices.reshape(4, 2, 4, 2, 2), AXES)
    row, col = ("y", "zh"), ("x", "zl", "c")
    tokens = P(row + col, None)
    vals = P(col, row, None)
    idx = P(col, None)
    return jax.shard_map(
        per_device,
        mesh=grid,
        in_specs=(tokens, tokens, vals, idx, vals, idx, vals, idx),
        out_specs=(tokens, tokens, vals, vals, vals),
        check_vma=False,
    )
```

```python
import jax
import jax.numpy as jnp
from jax import lax
from jax.experimental import pallas as pl
from jax.experimental.pallas import tpu as pltpu
from jax.sharding import Mesh, PartitionSpec as P

BLK = 64
AXES = ("y", "zh", "x", "zl", "c")
Z = ("zh", "zl")
ZX = ("zh", "zl", "x")
RING = 4
BF = jnp.bfloat16
F32 = jnp.float32
MIB = 1024 * 1024


def shift(value, axis, step):
    return lax.ppermute(value, axis, [(i, (i + step) % RING) for i in range(RING)])


def swap(value, axis):
    return lax.ppermute(value, axis, [(0, 1), (1, 0)])


def gather_direct(own, axis):
    below = shift(own, axis, 1)
    above = shift(own, axis, -1)
    across = shift(own, axis, 2)
    return [own, above, across, below]


def scatter_parts(chunks, axis):
    return chunks[0], shift(chunks[1], axis, 1), shift(chunks[3], axis, -1), shift(chunks[2], axis, 2)


def total(parts):
    return sum(part.astype(F32) for part in parts).astype(BF)


def scatter_direct(chunks, axis):
    return total(scatter_parts(chunks, axis))


def add(first, second):
    return (first.astype(F32) + second.astype(F32)).astype(BF)


def left_half(shape):
    return lax.broadcasted_iota(jnp.int32, shape, len(shape) - 1) % (2 * BLK) < BLK


def flip(value):
    return pltpu.roll(value, BLK, 1)


def kernel_params(limit):
    return pltpu.CompilerParams(
        dimension_semantics=("arbitrary",), vmem_limit_bytes=limit * MIB
    )


def row_copies(pieces, buf, sems):
    rows = pieces[0].shape[0]
    return [
        pltpu.make_async_copy(piece, buf.at[pl.ds(n * rows, rows)], sems.at[n])
        for n, piece in enumerate(pieces)
    ]


def owner_row(core, z, x):
    return core * RING * RING + z * RING + x % RING


def chunk_copies(pieces, buf, sems, place):
    per = pieces[0].shape[0] // RING
    copies = []
    for n, piece in enumerate(pieces):
        for x in range(RING):
            at = owner_row(n // RING, n % RING, place[2] + x) * per
            copies.append(
                pltpu.make_async_copy(
                    piece.at[pl.ds(x * per, per)],
                    buf.at[pl.ds(pl.multiple_of(at, per), per)],
                    sems.at[n * RING + x],
                )
            )
    return copies


def ring_copies(pieces, buf, sems, place):
    per = pieces[0].shape[2]
    copies = []
    for n in range(2 * RING * RING):
        core, x, z = n // (RING * RING), n // RING % RING, n % RING
        source = pieces[core].at[(place[2] + x) % RING, (place[1] + z) % RING]
        copies.append(pltpu.make_async_copy(source, buf.at[pl.ds(n * per, per)], sems.at[n]))
    return copies


def tile_wait(copies, i):
    for t in range(len(copies) // 2):

        @pl.when(i == t)
        def _(t=t):
            copies[2 * t].wait()
            copies[2 * t + 1].wait()


class Tiles:
    def __init__(self, half_panels, kept_here, zh):
        self.half_panels, self.kept_here, self.zh = half_panels, kept_here, zh
        self.pairs = kept_here // 2
        self.per_panel = kept_here + self.pairs

    def at(self, group, p, k):
        return (group * self.half_panels + p) * self.per_panel + k

    def kept(self, group, k):
        return (group // 2) * (2 * self.kept_here) + (self.zh ^ (group % 2)) * self.kept_here + k

    def row(self, idx_ref, p, j):
        return pl.multiple_of(idx_ref[self.zh * self.half_panels + p, j] * BLK, BLK)


def put_blocks(w_ref, places):
    mask = left_half((BLK, 2 * BLK))
    old = [w_ref[rows, lanes] for rows, lanes, _, _ in places]
    for before, (rows, lanes, tile, left) in zip(old, places):
        w_ref[rows, lanes] = jnp.where(mask, tile, before) if left else jnp.where(mask, before, tile)


def build_input_weights(where, gate_idx, up_idx, tiles, w_ref):
    w_ref[...] = jnp.zeros_like(w_ref)

    def put(step, carry):
        group, k = step // where.kept_here, step % where.kept_here
        j = where.kept(group, k)
        block = [tiles[where.at(group, p, k)] for p in range(where.half_panels)]
        for idx_ref, left in ((gate_idx, True), (up_idx, False)):
            put_blocks(w_ref, [
                (pl.ds(where.row(idx_ref, p, j), BLK), pl.ds(p * 2 * BLK, 2 * BLK), block[p], left)
                for p in range(where.half_panels)
            ])
        return carry

    lax.fori_loop(0, 2 * RING * where.kept_here, put, 0)


def build_down_weights(where, down_idx, tiles, w_ref):
    w_ref[...] = jnp.zeros_like(w_ref)

    def put(step, carry):
        group, m = step // where.pairs, step % where.pairs
        j = where.kept(group, 2 * m)
        for parity in range(2):
            places = []
            for p in range(parity, where.half_panels, 2):
                tile = tiles[where.at(group, p, where.kept_here + m)]
                for h in range(2):
                    rows = pl.ds(where.row(down_idx, p, j + h), BLK)
                    source = tile if h == parity else flip(tile)
                    places.append((rows, pl.ds((p // 2) * 128, 128), source, parity == 0))
            put_blocks(w_ref, places)
        return carry

    lax.fori_loop(0, 2 * RING * where.pairs, put, 0)


def back_rows(left, w_ref, out_ref):
    width = w_ref.shape[0]
    step = min(width, 1024)
    per = out_ref.shape[1]
    for start in range(0, width, step):
        part = lax.dot_general(
            left, w_ref[start : start + step, :], (((1,), (1,)), ((), ())),
            preferred_element_type=F32,
        ).astype(BF)
        for a in range(RING // 2):
            for b in range(RING):
                at = (a * RING + b) * per
                chunk = a * RING + b
                out_ref[chunk, :, start : start + step] = part[at : at + per]


def forward_tile(half_panels, x_tile, w_ref, m_ref, h_ref, h2_ref):
    rows = x_tile.shape[0]
    both = jnp.dot(x_tile, w_ref[...], preferred_element_type=F32)
    mask = left_half((rows, 2 * BLK))
    per = m_ref.shape[3]
    spans = [(a, b, (a * RING + b) * per) for a in range(RING // 2) for b in range(RING)]
    for first in range(0, half_panels, 2):
        group = [slice(p * 2 * BLK, (p + 1) * 2 * BLK) for p in range(first, min(first + 2, half_panels))]
        low, high = both[:, group[0]], both[:, group[-1]]
        gate = jnp.where(mask, low, flip(high))
        up = jnp.where(mask, flip(low), high)
        sigma = jax.nn.sigmoid(gate)
        silu = gate * sigma
        slope = up * sigma * (1.0 + gate * (1.0 - sigma))
        mults = [jnp.where(mask, slope, flip(silu)), jnp.where(mask, flip(slope), silu)]
        for lanes, mult in zip(group, mults):
            for a, b, at in spans:
                m_ref[0, a, b, :, lanes] = mult[at : at + per]
        hidden = silu * up
        if len(group) == 1:
            hidden = jnp.where(mask, hidden, 0.0)
        hidden = hidden.astype(BF)
        out = slice(first * BLK, (first + 2) * BLK)
        h_ref[:, out] = hidden
        for a, b, at in spans:
            h2_ref[0, b, a, :, out] = hidden[at : at + per]


def forward_kernel(half_panels, kept_here, first, place, *refs):
    if first:
        gate_idx, up_idx, down_idx, tiles = refs[:4]
        pieces, refs = refs[4:8], refs[8:]
        m_ref, h2_ref, y_ref, w_other, wd_other = refs[:5]
    else:
        w_other, wd_other = refs[:2]
        pieces, refs = refs[2:6], refs[8:]
        m_ref, h2_ref, y_ref = refs[:3]
    w_ref, wd_ref, h_ref, buf, sems, w_sems = refs[-6:]
    i = pl.program_id(0)
    rows = buf.shape[0] // 2
    copies = row_copies(pieces, buf, sems)
    pairs = ((w_ref, w_other), (wd_ref, wd_other))
    if not first:
        pairs = [(b, a) for a, b in pairs]
    w_copies = [pltpu.make_async_copy(a, b, w_sems.at[n]) for n, (a, b) in enumerate(pairs)]

    @pl.when(i == 0)
    def _():
        if not first:
            w_copies[0].start()
        for copy in copies:
            copy.start()
        if not first:
            w_copies[1].start()
        if first:
            where = Tiles(half_panels, kept_here, place[0])
            build_input_weights(where, gate_idx, up_idx, tiles, w_ref)
            w_copies[0].start()
            build_down_weights(where, down_idx, tiles, wd_ref)
            w_copies[1].start()
        else:
            w_copies[0].wait()

    tile_wait(copies, i)
    x_tile = buf[pl.ds(pl.multiple_of(i * rows, rows), rows), :]
    forward_tile(half_panels, x_tile, w_ref, m_ref, h_ref, h2_ref)
    if not first:

        @pl.when(i == 0)
        def _():
            w_copies[1].wait()

    back_rows(h_ref[...], wd_ref, y_ref)
    if first:

        @pl.when(i == pl.num_programs(0) - 1)
        def _():
            for copy in w_copies:
                copy.wait()


def gradient_kernel(half_panels, kept_here, place, gate_idx, up_idx, down_idx, *refs):
    dy_pieces, x_pieces, refs = refs[:2], refs[2:10], refs[10:]
    wd_ref, m_ref, h_ref, w_gu, back_kept, dx_away, out_ref = refs[:7]
    dy_buf, x_buf, g_ref, acc, w_ref, dy_sems, x_sems, g_sems = refs[7:]
    i = pl.program_id(0)
    where = Tiles(half_panels, kept_here, place[0])
    rows = dy_buf.shape[0] // 4
    dy_copies = ring_copies(dy_pieces, dy_buf, dy_sems, place)
    x_copies = chunk_copies(x_pieces, x_buf, x_sems, place)
    w_copy = pltpu.make_async_copy(w_gu, w_ref, g_sems.at[2])
    half_rows = back_kept.shape[0]
    g_copy = pltpu.make_async_copy(g_ref.at[pl.ds(0, half_rows)], back_kept, g_sems.at[0])
    dx_copy = pltpu.make_async_copy(dy_buf.at[pl.ds(0, half_rows)], dx_away, g_sems.at[1])
    hid = h_ref.shape[1]
    cols = dy_buf.shape[1] // 4
    mask = left_half((rows, 2 * BLK))
    small = left_half((BLK, 2 * BLK))

    @pl.when(i == 0)
    def _():
        for copy in dy_copies:
            copy.start()

    for t in range(4):

        @pl.when(i == t)
        def _(t=t):
            for copy in dy_copies[8 * t : 8 * t + 8]:
                copy.wait()

    @pl.when(i < 4)
    def _():
        dy_tile = dy_buf[pl.ds(pl.multiple_of(i * rows, rows), rows), :]
        d_hidden = jnp.dot(dy_tile, wd_ref[...], preferred_element_type=F32)
        per = m_ref.shape[3]
        for p in range(half_panels):
            if p % 2 == 0:
                here = d_hidden[:, (p // 2) * 128 : (p // 2 + 1) * 128]
                turned = flip(here)
                spread = jnp.where(mask, here, turned)
            else:
                spread = jnp.where(mask, turned, here)
            lanes = slice(p * 2 * BLK, (p + 1) * 2 * BLK)
            for a in range(RING // 2):
                for b in range(RING):
                    at = (a * RING + b) * per
                    chunk = owner_row(i // 2, b, place[2] + (i % 2) * (RING // 2) + a)
                    rows_at = pl.ds(pl.multiple_of(chunk * per, per), per)
                    g_ref[rows_at, lanes] = (
                        spread[at : at + per] * m_ref[0, b, a, :, lanes]
                    ).astype(BF)

    @pl.when((i >= 4) & (i < 8))
    def _():
        at = pl.multiple_of((i - 4) * cols, cols)
        part = lax.dot_general(
            dy_buf[:, pl.ds(at, cols)], h_ref[...], (((0,), (0,)), ((), ())),
            preferred_element_type=F32,
        )
        acc[pl.ds(at, cols), :hid] = part.astype(BF)

    @pl.when(i == 3)
    def _():
        w_copy.start()
        for copy in x_copies:
            copy.start()

    @pl.when(i == 4)
    def _():
        g_copy.start()

    @pl.when(i == 7)
    def _():
        def take(step, carry):
            group, m = step // where.pairs, step % where.pairs
            j = where.kept(group, 2 * m)
            for p in range(half_panels):
                lanes = pl.ds((p // 2) * 128, 128)
                first = acc[pl.ds(where.row(down_idx, p, j), BLK), lanes]
                second = acc[pl.ds(where.row(down_idx, p, j + 1), BLK), lanes]
                if p % 2 == 0:
                    second = flip(second)
                else:
                    first = flip(first)
                out_ref[where.at(group, p, kept_here + m)] = jnp.where(small, first, second)
            return carry

        lax.fori_loop(0, 2 * RING * where.pairs, take, 0)

    @pl.when(i == 8)
    def _():
        w_copy.wait()

    @pl.when((i >= 8) & (i < 12))
    def _():
        at = pl.multiple_of((i - 8) * cols, cols)
        part = lax.dot_general(
            g_ref[half_rows:, :], w_ref[pl.ds(at, cols), :], (((1,), (1,)), ((), ())),
            preferred_element_type=F32,
        )
        dy_buf[:half_rows, pl.ds(at, cols)] = part.astype(BF)

    @pl.when(i == 12)
    def _():
        dx_copy.start()
        for copy in x_copies:
            copy.wait()

    @pl.when(i >= 12)
    def _():
        at = pl.multiple_of((i - 12) * cols, cols)
        part = lax.dot_general(
            x_buf[:, pl.ds(at, cols)], g_ref[...], (((0,), (0,)), ((), ())),
            preferred_element_type=F32,
        )
        acc[pl.ds(at, cols), :] = part.astype(BF)

    @pl.when(i == pl.num_programs(0) - 1)
    def _():
        def take(step, carry):
            group, k = step // kept_here, step % kept_here
            j = where.kept(group, k)
            for p in range(half_panels):
                lanes = pl.ds(p * 2 * BLK, 2 * BLK)
                first = acc[pl.ds(where.row(gate_idx, p, j), BLK), lanes]
                second = acc[pl.ds(where.row(up_idx, p, j), BLK), lanes]
                out_ref[where.at(group, p, k)] = jnp.where(small, first, second)
            return carry

        lax.fori_loop(0, 2 * RING * kept_here, take, 0)
        g_copy.wait()
        dx_copy.wait()


def cost(flops, nbytes):
    return pl.CostEstimate(flops=flops // 8, bytes_accessed=nbytes // 8, transcendentals=0)


def per_device(x_seq, dy_seq, gate_vals, gate_idx, up_vals, up_idx, down_vals, down_idx):
    panels, kept_here, square = gate_vals.shape
    per, width = x_seq.shape
    edge = BLK
    half = panels // 2
    pairs = kept_here // 2
    per_panel = kept_here + pairs
    zh, z_place = lax.axis_index("zh"), lax.axis_index(Z)
    place = jnp.stack([zh, z_place, lax.axis_index("x")]).astype(jnp.int32)
    shape = jax.ShapeDtypeStruct

    gate_blk = gate_vals.reshape(panels, kept_here, edge, edge)
    up_blk = up_vals.reshape(panels, kept_here, edge, edge)
    pair_gu = jnp.concatenate([gate_blk, up_blk], axis=3)
    down_blk = down_vals.reshape(panels, pairs, 2, edge, edge)
    pair_d = jnp.transpose(down_blk, (0, 1, 4, 2, 3)).reshape(panels, pairs, edge, 2 * edge)
    all_pairs = jnp.concatenate([pair_gu, pair_d], axis=1)
    own = lax.dynamic_slice_in_dim(all_pairs, zh * half, half, 0)
    other = swap(lax.dynamic_slice_in_dim(all_pairs, (1 - zh) * half, half, 0), "zh")

    def gather_all(value, axis):
        wide = jnp.broadcast_to(value[None], (RING, *value.shape))
        return lax.all_to_all(wide, axis, 0, 0, tiled=True)

    dy_row = gather_all(dy_seq, Z)
    x_row = jnp.concatenate(gather_direct(x_seq, "x"), axis=0)
    other, x_row, dy_row = lax.optimization_barrier((other, x_row, dy_row))
    both = jnp.stack([own, other]).reshape(-1, edge, 2 * edge)
    tiles = lax.all_gather(both, "y", axis=0, tiled=True)
    dy_own = gather_all(dy_row, "x")
    x_own = gather_direct(x_row, Z)
    x_core = [swap(v, "c") for v in x_own]
    x_core, dy_own = lax.optimization_barrier((x_core, dy_own))
    dy_core = swap(dy_own, "c")

    tokens = 2 * RING * RING * per
    rows = tokens // 4
    hid = -(-half * edge // 128) * 128
    two = half * 2 * edge
    pair = RING // 2
    once = pl.Buffered(1)
    full = lambda *dims: pl.BlockSpec(dims, lambda i: (0,) * len(dims), pipeline_mode=once)
    out_full = lambda *dims: pl.BlockSpec(dims, lambda i: (0,) * len(dims))
    smem = pl.BlockSpec(memory_space=pltpu.SMEM)
    hbm = pl.BlockSpec(memory_space=pl.ANY)
    ordered = lambda last: (2, RING, RING, per, last)
    gu_flops = 2 * tokens * width * two
    d_flops = 2 * tokens * width * hid
    chunks = (RING * RING, per, width)

    def part(fn, *extra):
        def body(*refs):
            fn(*extra, *refs)

        return body

    def forward(core, first, inputs, name):
        specs = [smem] * 4 + [full(*tiles.shape)] + [hbm] * 4 if first else [smem] + [hbm] * 8
        extra_out = [shape((width, two), BF), shape((width, hid), BF)] if first else []
        return pl.pallas_call(
            part(forward_kernel, half, kept_here, first),
            grid=(2,),
            in_specs=specs,
            out_specs=[
                pl.BlockSpec((1, pair, RING, per, two), lambda i: (core, i, 0, 0, 0)),
                pl.BlockSpec((1, RING, pair, per, hid), lambda i: (core, 0, i, 0, 0)),
                pl.BlockSpec((pair * RING, per, width), lambda i: (i, 0, 0)),
            ] + [hbm] * len(extra_out),
            out_shape=[shape(ordered(two), F32), shape(ordered(hid), BF), shape(chunks, BF)] + extra_out,
            scratch_shapes=[
                pltpu.VMEM((width, two), BF),
                pltpu.VMEM((width, hid), BF),
                pltpu.VMEM((rows, hid), BF),
                pltpu.VMEM((tokens // 2, width), BF),
                pltpu.SemaphoreType.DMA((4,)),
                pltpu.SemaphoreType.DMA((2,)),
            ],
            input_output_aliases={} if first else {7: 0, 8: 1},
            compiler_params=kernel_params(56),
            cost_estimate=cost((gu_flops + d_flops) // 2, 24 * MIB),
            name=name,
        )(place, *inputs)

    mult, hidden, y_away, w_gu, w_d = forward(
        1, True, (gate_idx, up_idx, down_idx, tiles, *x_core), "forward_away"
    )
    y_recv = swap(y_away, "c")
    mult, hidden, y_kept = forward(0, False, (w_gu, w_d, *x_own, mult, hidden), "forward_kept")
    y_kept, dy_core = lax.optimization_barrier((y_kept, dy_core))
    dy_pieces = [v.reshape(RING, RING, per, width) for v in (dy_own, dy_core)]
    y_sum = [add(y_kept[n * RING : n * RING + RING], y_recv[n * RING : n * RING + RING]) for n in range(RING)]
    mult, y_sum = lax.optimization_barrier((mult, y_sum))
    y_z = scatter_direct(y_sum, Z)

    steps = 16
    x_tile = lambda i: jnp.minimum(i, 3)
    back_kept, dx_away, terms = pl.pallas_call(
        part(gradient_kernel, half, kept_here),
        grid=(steps,),
        in_specs=[smem] * 4
        + [hbm] * 10
        + [
            full(width, hid),
            pl.BlockSpec(
                (1, RING, pair, per, two), lambda i: (x_tile(i) // 2, 0, x_tile(i) % 2, 0, 0)
            ),
            full(tokens, hid),
            hbm,
        ],
        out_specs=[hbm, hbm, out_full(*tiles.shape)],
        out_shape=[
            shape((tokens // 2, two), BF),
            shape((tokens // 2, width), BF),
            shape(tiles.shape, BF),
        ],
        scratch_shapes=[
            pltpu.VMEM((tokens, width), BF),
            pltpu.VMEM((tokens, width), BF),
            pltpu.VMEM((tokens, two), BF),
            pltpu.VMEM((width, two), BF),
            pltpu.VMEM((width, two), BF),
            pltpu.SemaphoreType.DMA((32,)),
            pltpu.SemaphoreType.DMA((32,)),
            pltpu.SemaphoreType.DMA((3,)),
        ],
        compiler_params=kernel_params(60),
        cost_estimate=cost(gu_flops + 2 * d_flops, 40 * MIB),
        name="gradients",
    )(
        place, gate_idx, up_idx, down_idx, *dy_pieces, *x_own, *x_core,
        w_d, mult, hidden.reshape(tokens, hid), w_gu,
    )

    def project(left):
        return lax.dot_general(left, w_gu, (((1,), (1,)), ((), ())), preferred_element_type=F32)

    back_kept, dx_away, terms, y_z = lax.optimization_barrier((back_kept, dx_away, terms, y_z))
    dx_recv = swap(dx_away, "c")
    dx_kept, dx_recv = lax.optimization_barrier((project(back_kept).astype(BF), dx_recv))

    def chip_rows(first, count):
        split = lambda v: v[:, first : first + count].reshape(RING, RING, per, count)
        return add(split(dx_kept), split(dx_recv))

    def over_x(value):
        return jnp.sum(lax.all_to_all(value, "x", 0, 0, tiled=True).astype(F32), axis=0).astype(BF)

    x_first = jnp.transpose(chip_rows(0, width // 2), (1, 0, 2, 3))
    z_first = chip_rows(width // 2, width // 2)
    y_z, x_first, z_first = lax.optimization_barrier((y_z, x_first, z_first))
    x_first = over_x(x_first)
    z_first = scatter_direct([z_first[n] for n in range(RING)], Z)
    y_seq = scatter_direct([y_z[n] for n in range(RING)], "x")
    x_first, z_first, y_seq = lax.optimization_barrier((x_first, z_first, y_seq))
    x_first = scatter_direct([x_first[n] for n in range(RING)], Z)
    z_first = over_x(z_first)
    dx_seq = jnp.concatenate([x_first, z_first], axis=1)

    summed = lax.psum_scatter(terms, "y", scatter_dimension=0, tiled=True)
    summed = summed.reshape(2, half, per_panel, edge, 2 * edge)
    def both_halves(mine, theirs):
        low = jnp.where(zh == 0, mine, theirs)
        high = jnp.where(zh == 0, theirs, mine)
        return jnp.concatenate([low, high], axis=0)

    theirs = swap(summed[1, :, :kept_here], "zh")
    theirs_down = swap(summed[1, :, kept_here:], "zh")
    gu_grads = both_halves(summed[0, :, :kept_here], theirs)
    d_gate_vals = gu_grads[..., :edge].reshape(panels, kept_here, square)
    d_up_vals = gu_grads[..., edge:].reshape(panels, kept_here, square)
    d_gate_vals, d_up_vals, theirs_down = lax.optimization_barrier(
        (d_gate_vals, d_up_vals, theirs_down)
    )
    d_grads = both_halves(summed[0, :, kept_here:], theirs_down)
    d_grads = d_grads.reshape(panels, pairs, edge, 2, edge)
    d_down_vals = jnp.transpose(d_grads, (0, 1, 3, 4, 2)).reshape(panels, kept_here, square)
    return (y_seq, dx_seq, d_gate_vals, d_up_vals, d_down_vals)


def solution(mesh):
    grid = Mesh(mesh.devices.reshape(4, 2, 4, 2, 2), AXES)
    row, col = ("y", "zh"), ("x", "zl", "c")
    tokens = P(row + col, None)
    vals = P(col, row, None)
    idx = P(col, None)
    return jax.shard_map(
        per_device,
        mesh=grid,
        in_specs=(tokens, tokens, vals, idx, vals, idx, vals, idx),
        out_specs=(tokens, tokens, vals, vals, vals),
        check_vma=False,
    )
```
